32 devices in a mesh: dp: 8 (over z, y), tensor: 4 (over x, core).
Axes of the slice: x: 2, y: 2, z: 4, core: 2. Of those that a mesh axis runs over, the one named last changes fastest.
Arguments:
- tokens: bfloat16 [16384, 768], P(('dp', 'tensor')), may hold values from -6 to 6
- doc_lengths: int32 [8, 8], P('dp'), may hold values from 1 to 1537, 2048 in all within a row
- key_mask: int32 [16384], P(('dp', 'tensor')), may hold values 0 or 1
- qkv_weight: bfloat16 [768, 3, 768], P(None, None, 'tensor'), may hold values from -0.21875 to 0.21875
- out_weight: bfloat16 [768, 768], P('tensor'), may hold values from -1.5 to 1.5
- gate_up_weight: bfloat16 [768, 2, 3072], P(None, None, 'tensor'), may hold values from -0.21875 to 0.21875
- down_weight: bfloat16 [3072, 768], P('tensor'), may hold values from -0.109375 to 0.109375
- norm1_gain: float32 [768], replicated, may hold values from 0.25 to 1.75
- norm1_bias: float32 [768], replicated, may hold values from -2 to 2
- norm2_gain: float32 [768], replicated, may hold values from 0.25 to 1.75
- norm2_bias: float32 [768], replicated, may hold values from -2 to 2
- out_grad: bfloat16 [16384, 768], P(('dp', 'tensor')), may hold values from -6 to 6
Outputs:
- output: bfloat16 [16384, 768], P(('dp', 'tensor'))
- input_grad: float32 [16384, 768], P(('dp', 'tensor'))
- qkv_grad: float32 [768, 3, 768], P('dp', None, 'tensor')
- out_proj_grad: float32 [768, 768], P('tensor', 'dp')
- gate_up_grad: float32 [768, 2, 3072], P('dp', None, 'tensor')
- down_grad: float32 [3072, 768], P('tensor', 'dp')
- norm1_gain_grad: float32 [768], replicated
- norm1_bias_grad: float32 [768], replicated
- norm2_gain_grad: float32 [768], replicated
- norm2_bias_grad: float32 [768], replicated
The draws below stay inside these ranges and needn't reach their ends.
Inputs may be any that keep to these rules, and one draw needn't show every extreme that they name: `doc_lengths`: row g holds the lengths of the documents packed in order into group g; they sum to 2048, and the longest of every row has exactly 1537 tokens.
All inputs are finite; a program needn't handle non-finite values. No bound on the sum of `key_mask` on one device may be relied on, other than what follows from the above.
Results may differ from the reference program's by a relative error of at most 0.019.
Values may be sent and summed in bfloat16 or wider, within the bound.
No kernel may reach another device: no remote copies, remote signals or barrier semaphores. Data moves between devices by JAX's collectives and lax.ppermute only.
A program may use at most 128 MiB of HBM per device.

```python
import math
import jax
import jax.numpy as jnp
import numpy as np
from jax import lax

D = 768
HEADS = 12
HD = 64
FF = 3072
TOK_DEV = 512
DOCS = 8
GROUP = 2048
TOKENS = 16384
N_DP = 8


def with_ends(drawn, key, least, largest):
    dims = drawn.shape
    index_at = [jax.random.randint(jax.random.fold_in(key, axis), (), 0, dims[axis]) for axis in range(len(dims))]
    drawn = drawn.at[tuple(index_at)].set(least)
    longest = dims.index(max(dims))
    index_at[longest] = (index_at[longest] + 1) % dims[longest]
    return drawn.at[tuple(index_at)].set(largest)


def strengthened(values, rng, source, target, parts, factor):
    def block_of(axis_at):
        return (jnp.arange(values.shape[axis_at]) // (values.shape[axis_at] // parts)).reshape((-1,) + (1,) * (values.ndim - 1 - axis_at))

    first = jax.random.permutation(rng, parts)[block_of(target)]
    second = (block_of(target) + parts // 2) % parts
    return jnp.where((block_of(source) == first) | (block_of(source) == second), factor * values, values)


def steps_of(rng, dims, pieces, smallest, top_value):
    def one(dim, parts):
        draws = jax.random.uniform(jax.random.fold_in(jax.random.fold_in(rng, 6), dim), (parts,), jnp.float32, smallest / len(pieces), top_value / len(pieces))
        return jnp.repeat(jnp.exp(draws), dims[dim] // parts).reshape((-1,) + (1,) * (len(dims) - dim - 1))

    level = one(*pieces[0])
    for cut in pieces[1:]:
        level = level * one(*cut)
    return level


def length_profile(number_of, total, most, slope):
    portions = [(1 << 20) // math.isqrt(standing ** slope) + 1 for standing in range(2, number_of + 1)]
    surplus, given = total - most - (number_of - 1), [1] * (number_of - 1)
    while surplus > 0:
        candidates = [i for i in range(number_of - 1) if given[i] < most]
        mass, budget = sum([portions[i] for i in candidates]), surplus
        for i in candidates:
            addition = min(most - given[i], max(1, budget * portions[i] // mass), surplus)
            given[i] = given[i] + addition
            surplus = surplus - addition
    return np.array([most] + given)


def uneven(rng, amount, total, most, skew):
    if amount == 2:
        one = jax.random.randint(rng, (), max(1, total - most), min(most, total - 1) + 1)
        return jnp.stack([one, total - one])
    tallies = jnp.asarray(length_profile(amount, total, most, skew), jnp.int32)
    couples = (amount - 1) // 2
    giver, taker = tallies[1:1 + 2 * couples:2], tallies[2:2 + 2 * couples:2]
    room = jnp.minimum(giver - 1, most - taker)
    moved = jax.random.randint(jax.random.fold_in(rng, 1), (couples,), 0, 1 << 20) % (room + 1)
    tallies = tallies.at[1:1 + 2 * couples:2].set(giver - moved).at[2:2 + 2 * couples:2].set(taker + moved)
    return tallies[jax.random.permutation(jax.random.fold_in(rng, 2), amount)]


def normal_values(own_key, shape, deviation, bound, split=(), kind=jnp.bfloat16):
    drawn = deviation * jax.random.normal(own_key, shape, jnp.float32)
    if split:
        drawn = drawn * steps_of(own_key, shape, split, -0.22, 0.18)
    return jnp.clip(drawn, -bound, bound).astype(kind)


def bell_draw_with(own_key, shape, spread, reach, split, heavy, held_as=jnp.bfloat16):
    array = spread * jax.random.normal(own_key, shape, jnp.float32)
    if split:
        array = array * steps_of(own_key, shape, split, -0.22, 0.18)
    return jnp.clip(strengthened(array, jax.random.fold_in(own_key, 3), *heavy), -reach, reach).astype(held_as)


def setup_inputs(seed: int = 0) -> dict:
    seeds = jax.random.split(jax.random.key(seed), 13)
    return {
        "tokens": normal_values(seeds[0], (TOKENS, D), 1.0, 6.0, ((0, 32),)),
        "doc_lengths": jax.vmap(lambda own: uneven(own, DOCS, GROUP, 3 * TOK_DEV + 1, 2))(jax.random.split(seeds[1], N_DP)).reshape((N_DP, DOCS)).astype(jnp.int32),
        "key_mask": with_ends((jax.random.randint(seeds[2], (TOKENS,), 0, 8) < 7).astype(jnp.int32), jax.random.fold_in(seeds[2], 1), 0, 1),
        "qkv_weight": normal_values(seeds[3], (D, 3, HEADS * HD), D ** -0.5, 0.21875, ((2, 4),)),
        "out_weight": normal_values(seeds[4], (HEADS * HD, D), 16 ** -0.5, 1.5, ((0, 4),)),
        "gate_up_weight": normal_values(seeds[5], (D, 2, FF), D ** -0.5, 0.21875, ((2, 4),)),
        "down_weight": normal_values(seeds[6], (FF, D), FF ** -0.5, 0.109375, ((0, 4),)),
        "norm1_gain": jnp.clip(1.0 + 0.15 * jax.random.normal(seeds[7], (D,), jnp.float32), 0.25, 1.75),
        "norm1_bias": normal_values(seeds[8], (D,), 0.3, 2.0, (), jnp.float32),
        "norm2_gain": jnp.clip(1.0 + 0.15 * jax.random.normal(seeds[9], (D,), jnp.float32), 0.25, 1.75),
        "norm2_bias": normal_values(seeds[10], (D,), 0.3, 2.0, (), jnp.float32),
        "out_grad": bell_draw_with(seeds[11], (TOKENS, D), 1.0, 6.0, ((0, 32),), (0, 1, 32, 2.75)),
    }


@jax.custom_vjp
def low(v):
    return lax.optimization_barrier(v.astype(jnp.bfloat16)).astype(jnp.float32)

@jax.custom_vjp
def low_back(v):
    return v

def low_keep(v):
    return (low(v), None)

def low_pass(kept, grad):
    return (grad,)

def back_keep(v):
    return (v, None)

def back_low(kept, grad):
    return (low(grad),)
low.defvjp(low_keep, low_pass)
low_back.defvjp(back_keep, back_low)

def doc_layout(length_row, group_rows):
    places = jnp.arange(group_rows, dtype=jnp.int32)
    doc_ends = jnp.cumsum(length_row).astype(jnp.int32)
    earlier = places[:, None] >= doc_ends[None, :]
    segment = lax.optimization_barrier(jnp.sum(earlier.astype(jnp.int32), axis=1)).astype(jnp.int32)
    passed = lax.optimization_barrier(jnp.sum(jnp.where(earlier, length_row[None, :], 0), axis=1)).astype(jnp.int32)
    return (segment, places - passed)

def rope_tables(position):
    half_size = HD // 2
    freqs = 1000.0 ** (-(jnp.arange(half_size, dtype=jnp.float32) * 2.0 / HD))
    angles = position.astype(jnp.float32)[:, None] * freqs[None, :]
    cosine_table = jnp.concatenate([jnp.cos(angles), jnp.cos(angles)], axis=1)
    sine_table = jnp.concatenate([jnp.sin(angles), jnp.sin(angles)], axis=1)
    return (cosine_table, sine_table)

def rotate(values, cosine_table, sine_table):
    half_size = HD // 2
    turned = jnp.concatenate([-values[..., half_size:], values[..., :half_size]], axis=-1)
    return values * cosine_table[:, None, :] + turned * sine_table[:, None, :]

def layer_norm(hidden_in, gain, bias):
    centred = hidden_in - lax.optimization_barrier(jnp.mean(hidden_in, axis=-1, keepdims=True))
    inverse = lax.rsqrt(lax.optimization_barrier(jnp.mean(centred * centred, axis=-1, keepdims=True)) + 1e-05)
    return centred * inverse * gain + bias

def attend(queries, keys, values, segment, key_valid):
    group_rows = queries.shape[0]
    block_rows = min(512, group_rows)
    block_count = group_rows // block_rows
    places = jnp.arange(group_rows, dtype=jnp.int32)
    score_scale = HD ** (-0.5)

    def one_block(block_input):
        query_block, segment_block, place_block = block_input
        scores = jnp.einsum('qhd,khd->hqk', query_block, keys, precision=lax.Precision.HIGHEST) * score_scale
        scores = low_back(scores)
        allowed = (segment_block[:, None] == segment[None, :]) & (key_valid[None, :] | (place_block[:, None] == places[None, :]))
        scores = jnp.where(allowed[None], scores, -1e+30)
        probs = low(jax.nn.softmax(scores, axis=-1))
        return jnp.einsum('hqk,khd->qhd', probs, values, precision=lax.Precision.HIGHEST)
    blocked = (queries.reshape(block_count, block_rows, HEADS, HD), segment.reshape(block_count, block_rows), places.reshape(block_count, block_rows))
    result = lax.map(jax.checkpoint(one_block), blocked)
    return result.reshape(group_rows, HEADS, HD)

def apply_layer(tokens_in, params, segment, cosine_table, sine_table, key_valid):
    w_qkv, w_out, w_gate_up, w_down, gain_one, bias_one, gain_two, bias_two = params
    group_rows = tokens_in.shape[0]
    qkv = low_back(jnp.einsum('td,dce->tce', tokens_in, w_qkv, precision=lax.Precision.HIGHEST))
    queries = low_back(low(rotate(qkv[:, 0].reshape(group_rows, HEADS, HD), cosine_table, sine_table)))
    keys = low_back(low(rotate(qkv[:, 1].reshape(group_rows, HEADS, HD), cosine_table, sine_table)))
    values = low(qkv[:, 2].reshape(group_rows, HEADS, HD))
    attended = attend(queries, keys, values, segment, key_valid).reshape(group_rows, HEADS * HD)
    attended = low_back(low(attended))
    attn_out = low_back(jnp.dot(attended, w_out, precision=lax.Precision.HIGHEST))
    middle = layer_norm(tokens_in + attn_out, gain_one, bias_one)
    gate_up = low_back(jnp.einsum('td,dcf->tcf', low(middle), w_gate_up, precision=lax.Precision.HIGHEST))
    hidden = low(jax.nn.silu(gate_up[:, 0]) * gate_up[:, 1])
    mlp_out = low_back(jnp.dot(hidden, w_down, precision=lax.Precision.HIGHEST))
    return layer_norm(middle + mlp_out, gain_two, bias_two)

def reference(tokens, doc_lengths, key_mask, qkv_weight, out_weight, gate_up_weight, down_weight, norm1_gain, norm1_bias, norm2_gain, norm2_bias, out_grad):
    group_count = TOKENS // GROUP
    params = tuple((p.astype(jnp.float32) for p in (qkv_weight, out_weight, gate_up_weight, down_weight, norm1_gain, norm1_bias, norm2_gain, norm2_bias)))

    def per_group(totals, item):
        tokens_in, mask_row, length_row, grad_row = item
        segment, position = doc_layout(length_row, GROUP)
        cosine_table, sine_table = rope_tables(position)
        key_valid = mask_row > 0

        def forward(tokens_arg, *weights):
            return apply_layer(tokens_arg, weights, segment, cosine_table, sine_table, key_valid)
        result, pullback = jax.vjp(forward, tokens_in.astype(jnp.float32), *params)
        grads = pullback(grad_row.astype(jnp.float32))
        totals = tuple((a + b for a, b in zip(totals, grads[1:])))
        return (totals, (result.astype(jnp.bfloat16), grads[0]))
    start_totals = tuple((jnp.zeros_like(p) for p in params))
    inputs = (tokens.reshape(group_count, GROUP, D), key_mask.reshape(group_count, GROUP), doc_lengths, out_grad.reshape(group_count, GROUP, D))
    totals, (results, input_grads) = lax.scan(per_group, start_totals, inputs)
    return (results.reshape(TOKENS, D), input_grads.reshape(TOKENS, D), totals[0], totals[1], totals[2], totals[3], totals[4], totals[5], totals[6], totals[7])
```

```python
import functools

import jax
import jax.numpy as jnp
from jax import lax
from jax.experimental import pallas as pl
from jax.experimental.pallas import tpu as pltpu
from jax.sharding import PartitionSpec as P

HD = 64
F32 = jnp.float32
BF16 = jnp.bfloat16
BIG = -1e30
BLK = 256
VMEM_BYTES = 56 * 1024 * 1024

NN = (((1,), (0,)), ((), ()))
NT = (((1,), (1,)), ((), ()))
TN = (((0,), (0,)), ((), ()))


def mm(a, b, dims=NN):
    return lax.dot_general(a, b, dims, preferred_element_type=F32)


def lanes_of(rows):
    return lax.broadcasted_iota(jnp.int32, (rows, 128), 1)


def params(n_axes=1):
    return pltpu.CompilerParams(
        dimension_semantics=("arbitrary",) * n_axes, vmem_limit_bytes=VMEM_BYTES
    )


def cost(flops, moved, trans=0):
    return pl.CostEstimate(flops=flops, bytes_accessed=moved, transcendentals=trans)


def full(shape):
    return pl.BlockSpec(shape, lambda *_: (0,) * len(shape))


def split3(v):
    top = v.astype(BF16).astype(F32)
    rest = v - top
    middle = rest.astype(BF16).astype(F32)
    return top, middle, rest - middle


def sds(shape, dtype):
    return jax.ShapeDtypeStruct(shape, dtype)


def project_kernel(tok_ref, w_ref, cos_ref, sin_ref, qt_ref, kt_ref, *rest):
    q_ref, k_ref, v_ref = rest[-3:]
    lane = lanes_of(BLK)
    low = lane < 64
    v_tail = jnp.where((lane & 63) < 3, 1.0, 0.0)
    for start in range(0, tok_ref.shape[0], BLK):
        at = pl.ds(start, BLK)
        y = mm(tok_ref[at, :], w_ref[...], NT)
        cosine, sine = cos_ref[at, :], sin_ref[at, :]
        q01 = (y[:, 0:128] * cosine + y[:, 384:512] * sine) * 0.125
        q2k2 = y[:, 128:256] * cosine + y[:, 512:640] * sine
        k01 = y[:, 256:384] * cosine + y[:, 640:768] * sine
        v01, v2 = y[:, 768:896], y[:, 896:1024]
        q_tail, k_tail = qt_ref[at, :].astype(F32), kt_ref[at, :].astype(F32)
        q_ref[0, at, :] = jnp.where(low, q01, q_tail).astype(BF16)
        q_ref[1, at, :] = jnp.where(low, q_tail, q01).astype(BF16)
        q_ref[2, at, :] = jnp.where(low, q2k2 * 0.125, q_tail).astype(BF16)
        k_ref[0, at, :] = jnp.where(low, k01, k_tail).astype(BF16)
        k_ref[1, at, :] = jnp.where(low, k_tail, k01).astype(BF16)
        k_ref[2, at, :] = jnp.where(low, pltpu.roll(q2k2, 64, 1), k_tail).astype(BF16)
        v_ref[0, at, :] = jnp.where(low, v01, v_tail).astype(BF16)
        v_ref[1, at, :] = jnp.where(low, v_tail, v01).astype(BF16)
        v_ref[2, at, :] = jnp.where(low, v2, v_tail).astype(BF16)


def project(piece, tok, w, cosine, sine, q_tail, k_tail, before):
    rows, width = tok.shape
    total = rows * 4

    def side():
        return pl.BlockSpec((rows, 128), lambda i: (piece, 0))

    held = pl.BlockSpec((3, rows, 128), lambda i: (0, piece, 0))
    shape = sds((3, total, 128), BF16)
    extra = () if before is None else tuple(before)
    return pl.pallas_call(
        project_kernel,
        grid=(1,),
        in_specs=[full((rows, width)), full(w.shape), side(), side(), side(), side()]
        + [pl.BlockSpec(memory_space=pl.ANY)] * len(extra),
        out_specs=[held] * 3,
        out_shape=[shape] * 3,
        input_output_aliases={6 + i: i for i in range(len(extra))},
        compiler_params=params(),
        cost_estimate=cost(2 * rows * width * 1024, 4 * 2**20),
    )(tok, w, cosine, sine, q_tail, k_tail, *extra)


def attend_kernel(base, sp_ref, q_ref, k_ref, v_ref, a_ref, qb_ref, s_scr, m_scr, acc_scr):
    i = pl.program_id(0)
    here = base + i
    lo, hi, flip = sp_ref[here], sp_ref[8 + here], sp_ref[16]
    lane = lanes_of(BLK)
    low = lane < 64
    feats = (low, jnp.logical_not(low), low)
    own = pl.ds(pl.multiple_of(here * BLK, BLK), BLK)
    m_scr[...] = jnp.full(m_scr.shape, -3e38, F32)
    acc_scr[...] = jnp.zeros(acc_scr.shape, F32)

    def first(g, carry):
        at = pl.ds(pl.multiple_of((g ^ flip) * BLK, BLK), BLK)
        for h in range(3):
            s = mm(q_ref[h], k_ref[h, at, :], NT)
            s_scr[h, g] = s
            m_scr[h] = jnp.maximum(m_scr[h], jnp.maximum(s[:, :128], s[:, 128:]))
        return carry

    lax.fori_loop(lo, hi, first, 0)
    self_w = jnp.sum(jnp.where(lane == 72, k_ref[0, own, :].astype(F32), 0.0), axis=1, keepdims=True)
    tops, selfs = [], []
    for h in range(3):
        qk = q_ref[h].astype(F32) * k_ref[h, own, :].astype(F32)
        s_ii = jnp.sum(jnp.where(feats[h], qk, 0.0), axis=1, keepdims=True)
        s_ii = jnp.where(self_w > 0.5, s_ii, -3e38)
        tops.append(jnp.maximum(jnp.max(m_scr[h], axis=1, keepdims=True), s_ii))
        selfs.append(s_ii)

    def second(g, carry):
        at = pl.ds(pl.multiple_of((g ^ flip) * BLK, BLK), BLK)
        for h in range(3):
            p = jnp.exp(s_scr[h, g] - tops[h]).astype(BF16)
            acc_scr[h] += mm(p, v_ref[h, at, :])
        return carry

    lax.fori_loop(lo, hi, second, 0)
    outs = []
    for h in range(3):
        p_ii = jnp.exp(selfs[h] - tops[h])
        acc = acc_scr[h] + p_ii * v_ref[h, own, :].astype(F32)
        total = jnp.sum(jnp.where(lane == (0 if h == 1 else 64), acc, 0.0), axis=1, keepdims=True)
        outs.append(acc / total)
        top, middle, rest = split3(-(tops[h] + jnp.log(total)))
        spare = lane - (0 if h == 1 else 64)
        qb = q_ref[h].astype(F32)
        qb = jnp.where(spare == 9, top, jnp.where(spare == 10, middle, jnp.where(spare == 11, rest, qb)))
        qb_ref[h] = qb.astype(BF16)
    a_ref[0, pl.ds(pl.multiple_of((i % 2) * BLK, BLK), BLK), :] = jnp.where(low, outs[0], outs[1]).astype(BF16)

    @pl.when(i % 2 == 0)
    def _():
        a_ref[0, 2 * BLK :, :] = outs[2].astype(BF16)

    @pl.when(i % 2 == 1)
    def _():
        kept = a_ref[0, 2 * BLK :, :].astype(F32)
        a_ref[0, 2 * BLK :, :] = jnp.where(low, kept, pltpu.roll(outs[2], 64, 1)).astype(BF16)


def attend(half, sp, q, k, v):
    total = q.shape[1]
    base = half * 4
    return pl.pallas_call(
        functools.partial(attend_kernel, base),
        grid_spec=pltpu.PrefetchScalarGridSpec(
            num_scalar_prefetch=1,
            grid=(4,),
            in_specs=[
                pl.BlockSpec((3, BLK, 128), lambda i, sp: (0, base + i, 0)),
                full((3, total, 128)),
                full((3, total, 128)),
            ],
            out_specs=[
                pl.BlockSpec((1, 3 * BLK, 128), lambda i, sp: (i // 2, 0, 0)),
                pl.BlockSpec((3, BLK, 128), lambda i, sp: (0, i, 0)),
            ],
            scratch_shapes=[
                pltpu.VMEM((3, 8, BLK, BLK), F32),
                pltpu.VMEM((3, BLK, 128), F32),
                pltpu.VMEM((3, BLK, 128), F32),
            ],
        ),
        out_shape=[sds((2, 3 * BLK, 128), BF16), sds((3, 4 * BLK, 128), BF16)],
        compiler_params=params(),
        cost_estimate=cost(3 * 2 * 2 * 1024 * 2048 * 256, 8 * 2**20),
    )(sp, q, k, v)


def unpack(ref, half):
    pair = ref[pl.ds(half * BLK, BLK), :]
    third = ref[2 * BLK :, :]
    if half:
        third = pltpu.roll(third.astype(F32), 64, 1).astype(BF16)
    return pair, third


def pair_thirds(one, two, half):
    low = lanes_of(BLK) < 64
    a, b = one[2 * BLK :, :].astype(F32), two[2 * BLK :, :].astype(F32)
    if half:
        return jnp.where(low, pltpu.roll(a, 64, 1), b).astype(BF16)
    return jnp.where(low, a, pltpu.roll(b, 64, 1)).astype(BF16)


def norm_parts(h):
    centred = h - jnp.mean(h, axis=-1, keepdims=True)
    inverse = lax.rsqrt(jnp.mean(centred * centred, axis=-1, keepdims=True) + 1e-05)
    return centred * inverse, inverse


def norm_back(grad, normed, inverse, gain):
    scaled = grad * gain
    return inverse * (
        scaled
        - jnp.mean(scaled, axis=-1, keepdims=True)
        - normed * jnp.mean(scaled * normed, axis=-1, keepdims=True)
    )


def out_kernel(a0, a1, a2, a3, w0, w1, w2, w3, tok_ref, gain_ref, bias_ref, low_ref, xhat_ref, inv_ref):
    w01 = jnp.concatenate([w0[0:128, :], w1[0:128, :]], axis=0)
    w23 = jnp.concatenate([w2[0:128, :], w3[0:128, :]], axis=0)
    wt = jnp.concatenate([w0[128:192, :], w1[128:192, :], w2[128:192, :], w3[128:192, :]], axis=0)
    for half in range(2):
        at = pl.ds(half * BLK, BLK)
        h = mm(jnp.concatenate([a0[at, :], a1[at, :]], axis=1), w01)
        h += mm(jnp.concatenate([a2[at, :], a3[at, :]], axis=1), w23)
        h += mm(jnp.concatenate([pair_thirds(a0, a1, half), pair_thirds(a2, a3, half)], axis=1), wt)
        normed, inverse = norm_parts(tok_ref[at, :].astype(F32) + h)
        xhat_ref[at, :] = normed
        inv_ref[at, :] = jnp.broadcast_to(inverse, (BLK, 128))
        low_ref[at, :] = (normed * gain_ref[...] + bias_ref[...]).astype(BF16)


def out_project(a, w, tok, gain, bias):
    rows, width = tok.shape
    args = (*a, *w, tok, gain, bias)
    return pl.pallas_call(
        out_kernel,
        grid=(1,),
        in_specs=[full(v.shape) for v in args],
        out_specs=[full((rows, width)), full((rows, width)), full((rows, 128))],
        out_shape=[sds((rows, width), BF16), sds((rows, width), F32), sds((rows, 128), F32)],
        compiler_params=params(),
        cost_estimate=cost(2 * rows * width * width, 6 * 2**20),
    )(*args)


def mlp_kernel(ml0, ml1, wg_o, wu_o, wd_o, wg_p, wu_p, wd_p, own, sib, da_o, db_o, hid_o, da_p, db_p, acc_scr):
    j = pl.program_id(0)
    for block in range(4):
        src = (ml0, ml1)[block // 2]
        x = src[pl.ds((block % 2) * BLK, BLK), :]
        at = pl.ds(block * BLK, BLK)
        total = None
        for wg, wu, wd, da, db in ((wg_o, wu_o, wd_o, da_o, db_o), (wg_p, wu_p, wd_p, da_p, db_p)):
            gate, up = mm(x, wg[...]), mm(x, wu[...])
            s = 1.0 / (1.0 + jnp.exp(-gate))
            act = gate * s
            hidden = (act * up).astype(BF16)
            da[at, :] = (up * s * (1.0 + gate * (1.0 - s))).astype(BF16)
            db[at, :] = act.astype(BF16)
            if wg is wg_o:
                hid_o[at, :] = hidden
            part = mm(hidden, wd[...])
            total = part if total is None else total + part

        @pl.when(j == 0)
        def _():
            acc_scr[at, :] = total

        @pl.when(j > 0)
        def _():
            acc_scr[at, :] += total

    @pl.when(j == pl.num_programs(0) - 1)
    def _():
        own[...] = acc_scr[0 : 2 * BLK, :]
        sib[...] = acc_scr[2 * BLK :, :].astype(BF16)


def mlp_specs(width, hidden):
    chunks = hidden // BLK
    gate = pl.BlockSpec((width, BLK), lambda j: (0, j))
    up = pl.BlockSpec((width, BLK), lambda j: (0, chunks + j))
    down = pl.BlockSpec((BLK, width), lambda j: (j, 0))
    return chunks, gate, up, down


def mlp_forward(ml0, ml1, wgu_o, wd_o, wgu_p, wd_p):
    rows, width = ml0.shape
    hidden = wd_o.shape[0]
    chunks, gate, up, down = mlp_specs(width, hidden)
    saved = pl.BlockSpec((2 * rows, BLK), lambda j: (0, j))
    shape = sds((2 * rows, hidden), BF16)
    return pl.pallas_call(
        mlp_kernel,
        grid=(chunks,),
        in_specs=[full(ml0.shape), full(ml1.shape), gate, up, down, gate, up, down],
        out_specs=[full((rows, width)), full((rows, width))] + [saved] * 5,
        out_shape=[sds((rows, width), F32), sds((rows, width), BF16)] + [shape] * 5,
        scratch_shapes=[pltpu.VMEM((2 * rows, width), F32)],
        compiler_params=params(),
        cost_estimate=cost(2 * 2 * rows * width * hidden * 6, 18 * 2**20),
    )(ml0, ml1, wgu_o, wgu_o, wd_o, wgu_p, wgu_p, wd_p)


def mid_kernel(xhat_ref, own_ref, got_ref, go_ref, g1, b1, g2, b2, out_ref, dh_ref, dm_ref, sums_ref):
    i = pl.program_id(0)
    mid = xhat_ref[...] * g1[...] + b1[...]
    normed, inverse = norm_parts(mid + (own_ref[...] + got_ref[...].astype(F32)))
    out_ref[...] = (normed * g2[...] + b2[...]).astype(BF16)
    grad = go_ref[...].astype(F32)
    dh = norm_back(grad, normed, inverse, g2[...])
    dh_ref[...] = dh
    dm_ref[...] = dh.astype(BF16)

    @pl.when(i == 0)
    def _():
        sums_ref[...] = jnp.zeros(sums_ref.shape, F32)

    sums_ref[0:1, :] += jnp.sum(grad * normed, axis=0, keepdims=True)
    sums_ref[1:2, :] += jnp.sum(grad, axis=0, keepdims=True)


def mid_norm(xhat, own, got, out_grad, g1, b1, g2, b2):
    rows, width = xhat.shape
    block = pl.BlockSpec((128, width), lambda i: (i, 0))
    vec = full((1, width))
    return pl.pallas_call(
        mid_kernel,
        grid=(rows // 128,),
        in_specs=[block] * 4 + [vec] * 4,
        out_specs=[block, block, block, full((8, width))],
        out_shape=[sds((rows, width), BF16), sds((rows, width), F32), sds((rows, width), BF16), sds((8, width), F32)],
        compiler_params=params(),
        cost_estimate=cost(20 * rows * width, 8 * 2**20),
    )(xhat, own, got, out_grad, g1, b1, g2, b2)


def mlp_back_kernel(
    dm0, dm1, wg_o, wu_o, wd_o, wg_p, wu_p, wd_p, da_o, db_o, da_p, db_p, own, sib, dg_o, du_o, acc_scr
):
    j = pl.program_id(0)
    for block in range(4):
        src = (dm0, dm1)[block // 2]
        x = src[pl.ds((block % 2) * BLK, BLK), :]
        at = pl.ds(block * BLK, BLK)
        total = None
        for wg, wu, wd, da, db in ((wg_o, wu_o, wd_o, da_o, db_o), (wg_p, wu_p, wd_p, da_p, db_p)):
            dhid = mm(x, wd[...], NT)
            dgate = (dhid * da[at, :].astype(F32)).astype(BF16)
            dup = (dhid * db[at, :].astype(F32)).astype(BF16)
            if wg is wg_o:
                dg_o[at, :] = dgate
                du_o[at, :] = dup
            part = mm(dgate, wg[...], NT) + mm(dup, wu[...], NT)
            total = part if total is None else total + part

        @pl.when(j == 0)
        def _():
            acc_scr[at, :] = total

        @pl.when(j > 0)
        def _():
            acc_scr[at, :] += total

    @pl.when(j == pl.num_programs(0) - 1)
    def _():
        own[...] = acc_scr[0 : 2 * BLK, :]
        sib[...] = acc_scr[2 * BLK :, :].astype(BF16)


def mlp_backward(dm0, dm1, wgu_o, wd_o, wgu_p, wd_p, da_o, db_o, da_p, db_p):
    rows, width = dm0.shape
    hidden = wd_o.shape[0]
    chunks, gate, up, down = mlp_specs(width, hidden)
    saved = pl.BlockSpec((2 * rows, BLK), lambda j: (0, j))
    shape = sds((2 * rows, hidden), BF16)
    return pl.pallas_call(
        mlp_back_kernel,
        grid=(chunks,),
        in_specs=[full(dm0.shape), full(dm1.shape), gate, up, down, gate, up, down] + [saved] * 4,
        out_specs=[full((rows, width)), full((rows, width)), saved, saved],
        out_shape=[sds((rows, width), F32), sds((rows, width), BF16), shape, shape],
        scratch_shapes=[pltpu.VMEM((2 * rows, width), F32)],
        compiler_params=params(),
        cost_estimate=cost(2 * 2 * rows * width * hidden * 6, 18 * 2**20),
    )(dm0, dm1, wgu_o, wgu_o, wd_o, wgu_p, wgu_p, wd_p, da_o, db_o, da_p, db_p)


def first_norm_kernel(
    dh2, own, got, xhat, inv, g1, a0, a1, a2, a3, w0, w1, w2, w3, dh1, d0, d1, d2, d3, ea, eb, sums, dat_scr
):
    gain_sum, bias_sum = 0.0, 0.0
    w01 = jnp.concatenate([w0[0:128, :], w1[0:128, :], w2[0:128, :], w3[0:128, :]], axis=0)
    wt = jnp.concatenate([w0[128:192, :], w1[128:192, :], w2[128:192, :], w3[128:192, :]], axis=0)
    low = lanes_of(BLK) < 64
    for half in range(2):
        at = pl.ds(half * BLK, BLK)
        dmid = dh2[at, :] + (own[at, :] + got[at, :].astype(F32))
        normed = xhat[at, :]
        gain_sum += jnp.sum(dmid * normed, axis=0, keepdims=True)
        bias_sum += jnp.sum(dmid, axis=0, keepdims=True)
        grad = norm_back(dmid, normed, inv[at, 0:1], g1[...])
        dh1[at, :] = grad
        dat = grad.astype(BF16)
        dat_scr[at, :] = dat
        first = mm(dat, w01, NT)
        third = mm(dat, wt, NT)
        for p, d in enumerate((d0, d1, d2, d3)):
            d[at, :] = first[:, p * 128 : (p + 1) * 128].astype(BF16)
            part = third[:, (p // 2) * 128 : (p // 2 + 1) * 128]
            if (p % 2) != half:
                part = pltpu.roll(part, 64, 1)
            if half == 0:
                d[2 * BLK :, :] = part.astype(BF16)
            else:
                d[2 * BLK :, :] = jnp.where(low, d[2 * BLK :, :].astype(F32), part).astype(BF16)
    sums[...] = jnp.zeros(sums.shape, F32)
    sums[0:1, :] = gain_sum
    sums[1:2, :] = bias_sum
    for dst, (one, two) in ((ea, (a0, a2)), (eb, (a1, a3))):
        thirds = jnp.concatenate([pair_thirds(one, two, 0), pair_thirds(one, two, 1)], axis=0)
        cat = jnp.concatenate([one[0 : 2 * BLK, :], two[0 : 2 * BLK, :], thirds], axis=1)
        dst[...] = mm(dat_scr[...], cat, TN).astype(BF16)


def first_norm_back(dh2, own, got, xhat, inv, g1, a, w):
    rows, width = dh2.shape
    args = (dh2, own, got, xhat, inv, g1, *a, *w)
    return pl.pallas_call(
        first_norm_kernel,
        grid=(1,),
        in_specs=[full(v.shape) for v in args],
        out_specs=[full((rows, width))] + [full((3 * BLK, 128))] * 4 + [full((width, 384))] * 2 + [full((8, width))],
        out_shape=[sds((rows, width), F32)]
        + [sds((3 * BLK, 128), BF16)] * 4
        + [sds((width, 384), BF16)] * 2
        + [sds((8, width), F32)],
        scratch_shapes=[pltpu.VMEM((rows, width), BF16)],
        compiler_params=params(),
        cost_estimate=cost(4 * rows * width * width, 10 * 2**20),
    )(*args)


def weight_kernel(
    ml0, ml1, ml2, ml3, dm0, dm1, dm2, dm3, wg, wu, wd, dg_o, du_o, hid_o, out, mlt, dmt, dgs, dus, hids
):
    j = pl.program_id(0)
    rows = ml0.shape[0]

    @pl.when(j == 0)
    def _():
        for p, (a, b) in enumerate(((ml0, dm0), (ml1, dm1), (ml2, dm2), (ml3, dm3))):
            mlt[:, pl.ds(p * rows, rows)] = a[...].T
            dmt[:, pl.ds(p * rows, rows)] = b[...].T

    dgs[0 : 2 * rows, :] = dg_o[...]
    dus[0 : 2 * rows, :] = du_o[...]
    hids[0 : 2 * rows, :] = hid_o[...]
    for block in range(4):
        sub = pl.ds((block % 2) * BLK, BLK)
        at = pl.ds(2 * rows + block * BLK, BLK)
        x, dm = (ml2, ml3)[block // 2][sub, :], (dm2, dm3)[block // 2][sub, :]
        gate, up, dhid = mm(x, wg[...]), mm(x, wu[...]), mm(dm, wd[...], NT)
        s = 1.0 / (1.0 + jnp.exp(-gate))
        act = gate * s
        hids[at, :] = (act * up).astype(BF16)
        dgs[at, :] = (dhid * up * s * (1.0 + gate * (1.0 - s))).astype(BF16)
        dus[at, :] = (dhid * act).astype(BF16)
    out[0] = mm(mlt[...], dgs[...]).astype(BF16)
    out[1] = mm(mlt[...], dus[...]).astype(BF16)
    out[2] = mm(dmt[...], hids[...]).astype(BF16)


def weight_grads(ml, dm, wgu, wd, dg, du, hid):
    rows, width = ml[0].shape
    hidden = wd.shape[0]
    chunks, gate, up, down = mlp_specs(width, hidden)
    saved = pl.BlockSpec((2 * rows, BLK), lambda j: (0, j))
    return pl.pallas_call(
        weight_kernel,
        grid=(chunks,),
        in_specs=[full((rows, width))] * 8 + [gate, up, down] + [saved] * 3,
        out_specs=pl.BlockSpec((3, width, BLK), lambda j: (0, 0, j)),
        out_shape=sds((3, width, hidden), BF16),
        scratch_shapes=[pltpu.VMEM((width, 4 * rows), BF16)] * 2 + [pltpu.VMEM((4 * rows, BLK), BF16)] * 3,
        compiler_params=params(),
        cost_estimate=cost(2 * 2 * rows * width * hidden * 9, 18 * 2**20),
    )(*ml, *dm, wgu, wgu, wd, dg, du, hid)


def attend_back_kernel(
    sp_ref,
    qb_lo,
    qb_hi,
    k_ref,
    v_ref,
    a_lo,
    a_hi,
    d0,
    d1,
    d2,
    d3,
    cos_ref,
    sin_ref,
    turn_ref,
    out_ref,
    do_scr,
    dk_scr,
    dv_scr,
    dq_scr,
):
    flip = sp_ref[16]
    lane = lanes_of(BLK)
    low = lane < 64
    feats = (low, jnp.logical_not(low), low)
    starts = (64, 0, 64)
    dk_scr[...] = jnp.zeros(dk_scr.shape, F32)
    dv_scr[...] = jnp.zeros(dv_scr.shape, F32)
    for p, d in enumerate((d0, d1, d2, d3)):
        o = (a_lo, a_hi)[p // 2].at[p % 2]
        for half in range(2):
            at = pl.ds((2 * p + half) * BLK, BLK)
            d01, dt = unpack(d, half)
            o01, ot = unpack(o, half)
            d01, dt = d01.astype(F32), dt.astype(F32)
            e01, et = d01 * o01.astype(F32), dt * ot.astype(F32)
            deltas = (
                jnp.sum(jnp.where(low, e01, 0.0), axis=1, keepdims=True),
                jnp.sum(jnp.where(low, 0.0, e01), axis=1, keepdims=True),
                jnp.sum(jnp.where(low, et, 0.0), axis=1, keepdims=True),
            )
            for h in range(3):
                top, middle, rest = split3(-deltas[h])
                spare = lane - starts[h]
                tail = jnp.where(spare == 0, top, jnp.where(spare == 1, middle, jnp.where(spare == 2, rest, 0.0)))
                do_scr[h, at, :] = jnp.where(feats[h], (d01, d01, dt)[h], tail).astype(BF16)

    for half, qb_ref in enumerate((qb_lo, qb_hi)):

        def q_block(i, carry):
            here = half * 4 + i
            q_at = pl.ds(pl.multiple_of(i * BLK, BLK), BLK)
            own = pl.ds(pl.multiple_of(here * BLK, BLK), BLK)
            for h in range(3):
                dq_scr[h, own, :] = jnp.zeros((BLK, 128), F32)

            def inner(g, c):
                at = pl.ds(pl.multiple_of((g ^ flip) * BLK, BLK), BLK)
                for h in range(3):
                    q, do = qb_ref[h, q_at, :], do_scr[h, own, :]
                    k, v = k_ref[h, at, :], v_ref[h, at, :]
                    p = jnp.exp(mm(k, q, NT))
                    ds = (p * mm(v, do, NT)).astype(BF16)
                    dv_scr[h, at, :] += mm(p.astype(BF16), do)
                    dk_scr[h, at, :] += mm(ds, q)
                    dq_scr[h, own, :] += mm(ds, k, TN)
                return c

            lax.fori_loop(sp_ref[here], sp_ref[8 + here], inner, 0)
            self_w = jnp.sum(jnp.where(lane == 72, k_ref[0, own, :].astype(F32), 0.0), axis=1, keepdims=True)
            for h in range(3):
                spare = lane - starts[h]
                use = jnp.logical_or(feats[h], jnp.logical_and(spare >= 9, spare < 12))
                q, do = qb_ref[h, q_at, :].astype(F32), do_scr[h, own, :].astype(F32)
                k, v = k_ref[h, own, :].astype(F32), v_ref[h, own, :].astype(F32)
                s = jnp.sum(jnp.where(use, q * k, 0.0), axis=1, keepdims=True)
                p = jnp.exp(jnp.where(self_w > 0.5, s, -1e30))
                ds = p * jnp.sum(do * v, axis=1, keepdims=True)
                dv_scr[h, own, :] += p * do
                dk_scr[h, own, :] += ds * q
                dq_scr[h, own, :] += ds * k
            return carry

        lax.fori_loop(0, 4, q_block, 0)

    def finish(i, carry):
        at = pl.ds(pl.multiple_of(i * BLK, BLK), BLK)
        cosine, sine = cos_ref[at, :], sin_ref[at, :]

        def unrotate(g):
            g = g.astype(BF16)
            return (g.astype(F32) * cosine + mm(g, turn_ref[...]) * sine).astype(BF16)

        out_ref[at, 0:128] = unrotate(jnp.where(low, dq_scr[0, at, :], dq_scr[1, at, :]) * 0.125)
        out_ref[at, 128:256] = unrotate(
            jnp.where(low, dq_scr[2, at, :] * 0.125, pltpu.roll(dk_scr[2, at, :], 64, 1))
        )
        out_ref[at, 256:384] = unrotate(jnp.where(low, dk_scr[0, at, :], dk_scr[1, at, :]))
        out_ref[at, 384:512] = jnp.where(low, dv_scr[0, at, :], dv_scr[1, at, :]).astype(BF16)
        out_ref[at, 512:640] = jnp.where(low, dv_scr[2, at, :], 0.0).astype(BF16)
        return carry

    lax.fori_loop(0, 8, finish, 0)


def attend_back(sp, qb_lo, qb_hi, k, v, a_lo, a_hi, d, cosine, sine, turn):
    total = k.shape[1]
    args = (qb_lo, qb_hi, k, v, a_lo, a_hi, *d, cosine, sine, turn)
    held = pltpu.VMEM((3, total, 128), F32)
    return pl.pallas_call(
        attend_back_kernel,
        grid_spec=pltpu.PrefetchScalarGridSpec(
            num_scalar_prefetch=1,
            grid=(1,),
            in_specs=[full(a.shape) for a in args],
            out_specs=full((total, 640)),
            scratch_shapes=[pltpu.VMEM((3, total, 128), BF16), held, held, held],
        ),
        out_shape=sds((total, 640), BF16),
        compiler_params=params(),
        cost_estimate=cost(3 * 5 * 2 * 2048 * 2048 * 256, 12 * 2**20),
    )(sp, *args)


def swap(v, bit, axis="tensor"):
    n = lax.axis_size(axis)
    return lax.ppermute(v, axis, [(i, i ^ bit) for i in range(n)])


def scatter_dp(v, axis):
    n = lax.axis_size("dp")
    me = lax.axis_index("dp")
    shape = v.shape
    v = v.reshape(shape[:axis] + (n, shape[axis] // n) + shape[axis + 1 :])
    bit = 1
    while bit < n:
        mine = (me // bit) % 2
        v = v.reshape(v.shape[:axis] + (v.shape[axis] // 2, 2) + v.shape[axis + 1 :])
        kept = lax.dynamic_index_in_dim(v, mine, axis + 1, keepdims=False)
        sent = lax.dynamic_index_in_dim(v, 1 - mine, axis + 1, keepdims=False)
        got = swap(sent, bit, "dp")
        v = kept.astype(F32) + got.astype(F32)
        bit *= 2
        if bit < n:
            v = v.astype(BF16)
    return v.reshape(shape[:axis] + (shape[axis] // n,) + shape[axis + 1 :])


def sum_all(v):
    for bit in (1, 2):
        v = v + swap(v, bit)
    bit = 1
    while bit < lax.axis_size("dp"):
        v = v + swap(v, bit, "dp")
        bit *= 2
    return v


def local(
    tokens,
    doc_lengths,
    key_mask,
    qkv_weight,
    out_weight,
    gate_up_weight,
    down_weight,
    norm1_gain,
    norm1_bias,
    norm2_gain,
    norm2_bias,
    out_grad,
):
    rows, width = tokens.shape
    group = rows * 4
    me = lax.axis_index("tensor")
    tok1 = swap(tokens, 1)
    tok2 = swap(tokens, 2)
    tok3 = swap(tok2, 1)
    valid0 = key_mask.astype(F32).reshape(rows // 128, 128)
    valid = jnp.concatenate([valid0, swap(valid0, 1), swap(valid0, 2), swap(valid0, 3)], axis=0).reshape(group)

    spots = jnp.arange(group, dtype=jnp.int32)
    places = ((spots // rows) ^ me) * rows + spots % rows
    lengths = doc_lengths[0]
    doc_ends = jnp.cumsum(lengths)
    earlier = places[:, None] >= doc_ends[None, :]
    segment = jnp.sum(earlier.astype(jnp.int32), axis=1)
    position = places - jnp.sum(jnp.where(earlier, lengths[None, :], 0), axis=1)
    lane = jnp.arange(128, dtype=jnp.int32)
    freqs = 1000.0 ** (-((lane % 32).astype(F32) * 2.0 / HD))
    angles = position.astype(F32)[:, None] * freqs[None, :]
    cosine, sine = jnp.cos(angles), jnp.sin(angles)
    spare = lane % 64
    same = segment[:, None] == spare[None, :]
    q_tail = jnp.where((spare[None, :] < 8) & ~same, BIG, 0.0)
    q_tail = jnp.where(spare[None, :] == 8, BIG, q_tail).astype(BF16)
    k_tail = jnp.where(same & (spare[None, :] < 8), 1.0, 0.0)
    k_tail = jnp.where(spare[None, :] == 8, 1.0 - valid[:, None], k_tail)
    k_tail = jnp.where((spare[None, :] >= 9) & (spare[None, :] < 12), 1.0, k_tail).astype(BF16)
    first = (places - position).reshape(8, BLK)[:, 0]
    last_seg = segment.reshape(8, BLK)[:, BLK - 1]
    last = jnp.sum(jnp.where(last_seg[:, None] == jnp.arange(8)[None, :], doc_ends[None, :], 0), axis=1)
    sp = jnp.concatenate([first // BLK, (last + BLK - 1) // BLK, (2 * me)[None]]).astype(jnp.int32)

    wt = jnp.transpose(qkv_weight, (1, 2, 0))
    halves = wt.reshape(3, 3, 2, HD // 2, width)
    turned = jnp.concatenate([-halves[:, :, 1:], halves[:, :, :1]], axis=2).reshape(3, 192, width)
    wq, wk, wv, rq, rk = wt[0], wt[1], wt[2], turned[0], turned[1]
    zeros = jnp.zeros((64, width), BF16)
    w_proj = jnp.concatenate(
        [wq, wk[128:], wk[:128], rq, rk[128:], rk[:128], wv, zeros], axis=0
    )
    w_back = jnp.concatenate([wq, wk[128:], wk[:128], wv, zeros], axis=0)
    row = jnp.arange(128)
    turn = jnp.where(
        row[:, None] == row[None, :] + 32, 1.0, jnp.where(row[:, None] == row[None, :] - 32, -1.0, 0.0)
    )
    first_half = (row[None, :] % 64) < 32
    turn = jnp.where(first_half == (row[:, None] > row[None, :]), turn, 0.0).astype(BF16)

    wo0 = out_weight
    wo1 = swap(wo0, 1)
    wo2 = swap(wo0, 2)
    wo3 = swap(wo2, 1)
    wo = (wo0, wo1, wo2, wo3)
    wgu = gate_up_weight.reshape(width, -1)
    wgu_p = swap(wgu, 2)
    wd_p = swap(down_weight, 2)

    held = None
    tok = (tokens, tok1, tok2, tok3)
    for piece in range(4):
        held = project(piece, tok[piece], w_proj, cosine, sine, q_tail, k_tail, held)
    q, k, v = held
    a_hi, qb_hi = attend(1, sp, q, k, v)
    att2, att3 = swap(a_hi[0], 2), swap(a_hi[1], 3)
    a_lo, qb_lo = attend(0, sp, q, k, v)
    att1 = swap(a_lo[1], 1)
    att = (a_lo[0], att1, att2, att3)

    g1, b1, g2, b2 = (u.reshape(1, width) for u in (norm1_gain, norm1_bias, norm2_gain, norm2_bias))
    ml0, xhat1, inv1 = out_project(att, wo, tokens, g1, b1)
    ml1 = swap(ml0, 1)
    ml2 = swap(ml0, 2)
    ml3 = swap(ml2, 1)
    own, sib, da_o, db_o, hid_o, da_p, db_p = mlp_forward(ml0, ml1, wgu, down_weight, wgu_p, wd_p)
    output, dh2, dm0, sums2 = mid_norm(xhat1, own, swap(sib, 1), out_grad, g1, b1, g2, b2)
    dm1 = swap(dm0, 1)
    dm2 = swap(dm0, 2)
    dm3 = swap(dm2, 1)
    own, sib, dg_o, du_o = mlp_backward(dm0, dm1, wgu, down_weight, wgu_p, wd_p, da_o, db_o, da_p, db_p)
    dh1, d0, d1, d2, d3, ea, eb, sums1 = first_norm_back(dh2, own, swap(sib, 1), xhat1, inv1, g1, att, wo)
    dd = (d0, swap(d1, 1), swap(d2, 2), swap(d3, 3))
    sums = sum_all(jnp.concatenate([sums1[0:2], sums2[0:2]], axis=0))

    e = ea.astype(F32) + swap(eb, 1).astype(F32)
    e_own = jnp.concatenate([e[:, 0:128], e[:, 256:320]], axis=1)
    e_x = jnp.concatenate([e[:, 128:256], e[:, 320:384]], axis=1).astype(BF16)
    out_part = (e_own + swap(e_x, 2).astype(F32)).astype(BF16)

    grads = weight_grads((ml0, ml1, ml2, ml3), (dm0, dm1, dm2, dm3), wgu, down_weight, dg_o, du_o, hid_o)
    grads = scatter_dp(grads, 1)
    out_part = scatter_dp(out_part, 0)

    dqkv = attend_back(sp, qb_lo, qb_hi, k, v, a_lo, a_hi, dd, cosine, sine, turn)
    back = [mm(dqkv[p * rows : (p + 1) * rows], w_back) for p in range(4)]
    got = swap(back[3].astype(BF16), 1)
    through = swap((back[2] + got.astype(F32)).astype(BF16), 2)
    near = swap(back[1].astype(BF16), 1)
    input_grad = dh1 + (back[0] + near.astype(F32) + through.astype(F32))
    tok_all = jnp.concatenate(tok, axis=0)
    qkv_part = scatter_dp(mm(tok_all, dqkv, TN).astype(BF16), 0)
    qkv_part = jnp.concatenate(
        [qkv_part[:, 0:192], qkv_part[:, 256:384], qkv_part[:, 192:256], qkv_part[:, 384:576]], axis=1
    ).reshape(-1, 3, 192)
    return (
        output,
        input_grad,
        qkv_part,
        out_part.T,
        jnp.stack([grads[0], grads[1]], axis=1),
        grads[2].T,
        sums[0],
        sums[1],
        sums[2],
        sums[3],
    )


def solution(mesh):
    placed = (
        P(("dp", "tensor"), None),
        P("dp", None),
        P(("dp", "tensor")),
        P(None, None, "tensor"),
        P("tensor", None),
        P(None, None, "tensor"),
        P("tensor", None),
        P(),
        P(),
        P(),
        P(),
        P(("dp", "tensor"), None),
    )
    return jax.shard_map(
        local,
        mesh=mesh,
        in_specs=placed,
        out_specs=(
            P(("dp", "tensor"), None),
            P(("dp", "tensor"), None),
            P("dp", None, "tensor"),
            P("tensor", "dp"),
            P("dp", None, "tensor"),
            P("tensor", "dp"),
            P(),
            P(),
            P(),
            P(),
        ),
        check_vma=False,
    )
```

```python
import functools

import jax
import jax.numpy as jnp
from jax import lax
from jax.experimental import pallas as pl
from jax.experimental.pallas import tpu as pltpu
from jax.sharding import PartitionSpec as P

HD = 64
F32 = jnp.float32
BF16 = jnp.bfloat16
BIG = -1e30
BLK = 256
WINDOWS = (640, 1664, 2048)
SCALE = 0.15
EXTRA = 16
NN = (((1,), (0,)), ((), ()))
NT = (((1,), (1,)), ((), ()))
TN = (((0,), (0,)), ((), ()))


def mm(a, b, dims=NN):
    return lax.dot_general(a, b, dims, preferred_element_type=F32)


class Order:
    def __init__(self):
        self.last = ()


ORDER = Order()


def run(kernel, us, mib, scalars, args, outs, scratch=(), awaits=(), carry=(), apart=()):
    in_vmem = pl.BlockSpec(memory_space=pltpu.VMEM)
    anywhere = pl.BlockSpec(memory_space=pl.ANY)
    awaits = (*awaits, *ORDER.last)
    n_in = len(scalars) + len(apart) + len(args)
    n_skip, n_out = len(awaits) + len(carry), len(outs)

    def body(*refs):
        rest = refs[n_in + n_skip :]
        kernel(*refs[:n_in], *rest[:n_out], *rest[n_out + len(carry) :])

    results = pl.pallas_call(
        body,
        in_specs=[pl.BlockSpec(memory_space=pltpu.SMEM)] * len(scalars)
        + [anywhere] * len(apart)
        + [in_vmem] * len(args)
        + [anywhere] * n_skip,
        out_specs=[in_vmem] * n_out + [anywhere] * len(carry),
        out_shape=[jax.ShapeDtypeStruct(*o) for o in outs] + [jax.ShapeDtypeStruct(c.shape, c.dtype) for c in carry],
        scratch_shapes=list(scratch),
        input_output_aliases={n_in + len(awaits) + i: n_out + i for i in range(len(carry))},
        compiler_params=pltpu.CompilerParams(vmem_limit_bytes=mib << 20),
        cost_estimate=pl.CostEstimate(flops=int(us * SCALE * 1.1e9), bytes_accessed=1 << 18, transcendentals=0),
    )(*scalars, *apart, *args, *awaits, *carry)
    ORDER.last = (min(results[:n_out], key=lambda r: r.size),)
    return results


def gate_kernel(out):
    out[...] = jnp.zeros(out.shape, F32)


def gate(*arrays, awaits=()):
    return run(gate_kernel, 0.1, 4, (), (), [((8, 128), F32)], awaits=awaits, carry=arrays)[1:]


def split3(v):
    top = v.astype(BF16).astype(F32)
    rest = v - top
    middle = rest.astype(BF16).astype(F32)
    return top, middle, rest - middle


def split_rows(value, first, second):
    half = first.shape[0]
    first[...] = value[0:half].astype(first.dtype)
    second[...] = value[half:].astype(second.dtype)


def transpose_into(dst, value, spots, cols):
    turned = value.T
    if spots is None:
        dst[:, cols] = turned
        return
    count = spots.shape[0]
    rows = turned.shape[0] // count
    for b in range(count):
        dst[pl.ds(pl.multiple_of(spots[b] * rows, rows), rows), cols] = turned[b * rows : (b + 1) * rows]


def transpose_kernel(fast, spots, at_ref, p0, p1, p2, p3, t0, t1, t2, t3, out, wo, sem):
    rows = out.shape[1] // 4
    part = wo.shape[0] // 4
    copies = []
    for n, p in enumerate((p0, p1, p2, p3)):
        spot = pl.ds(pl.multiple_of((at_ref[0] ^ n) * part, part), part)
        copies.append(pltpu.make_async_copy(p.at[pl.ds(p.shape[0] - part, part), :], wo.at[spot, :], sem.at[n]))
        copies[-1].start()
    for p, t in enumerate((t0, t1, t2, t3)):
        transpose_into(out, t[0:rows, :], spots if fast else None, slice(p * rows, (p + 1) * rows))
    for c in copies:
        c.wait()


def transposed(fast, spots, at, pieces, rows, parts, wo, awaits=()):
    width = pieces[0].shape[1]
    return run(
        functools.partial(transpose_kernel, fast),
        2,
        8,
        (spots, at),
        pieces,
        [((width, 4 * rows), BF16), (wo.shape, BF16)],
        [pltpu.SemaphoreType.DMA((4,))],
        awaits,
        apart=parts,
    )


def project_kernel(piece, sp_ref, freq_ref, tok_ref, w_ref, qt_ref, kt_ref, k_ref, vt_ref, cs_ref):
    n = tok_ref.shape[0] - EXTRA
    place = (sp_ref[8] ^ piece) * n + lax.broadcasted_iota(jnp.int32, (1, n), 1)
    seg = jnp.zeros((1, n), jnp.int32)
    pos = place
    end = 0
    for d in range(8):
        length = sp_ref[d]
        end = end + length
        past = place >= end
        seg += past.astype(jnp.int32)
        pos -= jnp.where(past, length, 0)
    angles = pos.astype(F32) * freq_ref[:, 0:1]
    cosine, sine = jnp.cos(angles), jnp.sin(angles)
    cs_ref[0:32, :] = cosine
    cs_ref[32:64, :] = sine
    idx = lax.broadcasted_iota(jnp.int32, (64, n), 0)
    which = jnp.where(idx < 19, idx - 8, idx - 19)
    bit = (jnp.broadcast_to(place, (64, n)) >> jnp.clip(which, 0, 10)) & 1
    flipped = jnp.where(idx < 19, bit, 1 - bit).astype(F32)
    same = (idx == seg).astype(F32)
    coded = (idx >= 8) & (idx < 30)
    invalid = 1.0 - tok_ref[n : n + EXTRA, 0:n].astype(F32)[0:1]
    q_tail = jnp.where(idx < 8, BIG * (1.0 - same), jnp.where(coded, BIG * flipped, 0.0))
    k_tail = jnp.where(idx < 8, same, jnp.where(coded, invalid * (1.0 - flipped), 0.0))
    k_tail = jnp.where((idx >= 32) & (idx < 35), 1.0, k_tail)
    v_tail = jnp.where(idx < 3, 1.0, 0.0)
    y = mm(w_ref[...], tok_ref[0:n, :], NT)

    def rotated(at):
        a, b = y[at : at + 32], y[at + 32 : at + 64]
        return jnp.concatenate([a * cosine - b * sine, b * cosine + a * sine], axis=0)

    for h in range(3):
        qt_ref[h] = jnp.concatenate([rotated(h * HD) * 0.125, q_tail], axis=0).astype(BF16)
        key = jnp.concatenate([rotated(192 + h * HD), k_tail], axis=0)
        kt_ref[h] = key.astype(BF16)
        k_ref[h] = key.T.astype(BF16)
        vt_ref[h] = jnp.concatenate([y[384 + h * HD : 448 + h * HD], v_tail], axis=0).astype(BF16)


def project(piece, sp, freqs, tok, w, awaits=(), carry=()):
    rows = tok.shape[0] - EXTRA
    wide, tall = ((3, 128, rows), BF16), ((3, rows, 128), BF16)
    return run(
        functools.partial(project_kernel, piece),
        2.5,
        10,
        (sp,),
        (freqs, tok, w),
        (wide, wide, tall, wide, ((HD, rows), F32)),
        awaits=awaits,
        carry=carry,
    )


def window_of(sp_ref, block, total):
    a = block * BLK
    b = a + BLK - 1
    first, last, end = 0, 0, 0
    for d in range(8):
        begin, end = end, end + sp_ref[d]
        first = jnp.where(begin <= a, begin, first)
        last = jnp.where(begin <= b, end, last)
    start = (first // 128) * 128
    kind = jnp.where(last - start <= WINDOWS[0], 0, jnp.where(last - start <= WINDOWS[1], 1, 2))
    size = jnp.where(kind == 0, WINDOWS[0], jnp.where(kind == 1, WINDOWS[1], WINDOWS[2]))
    return pl.multiple_of(jnp.minimum(start, total - size), 128), kind


def place_of(sp_ref, piece, rows):
    return pl.ds(pl.multiple_of((sp_ref[8] ^ piece) * rows, rows), rows)


def attend_kernel(base, sp_ref, qa, qb, k0, k1, k2, k3, v0, v1, v2, v3, oa, ob, ba, bb, k_scr, v_scr, s_scr, q_scr, o_scr):
    rows = qa.shape[2]
    total = 4 * rows
    for p, (k, v) in enumerate(((k0, v0), (k1, v1), (k2, v2), (k3, v3))):
        at = place_of(sp_ref, p, rows)
        k_scr[:, at, :] = k[...]
        v_scr[:, :, at] = v[...]
    for n in range(4):
        q_scr[n] = (qa, qb)[n // 2][:, :, (n % 2) * BLK : (n % 2 + 1) * BLK]

    def q_block(i, carry):
        start, kind = window_of(sp_ref, (base + i) ^ (2 * sp_ref[8]), total)

        def scores(h, size):
            s = mm(k_scr[h, pl.ds(start, size), :], q_scr[i, h])
            s_scr[h, 0:size, :] = s
            return jnp.max(s, axis=0, keepdims=True)

        def weigh(h, size, top):
            p = jnp.exp(s_scr[h, 0:size, :] - top).astype(BF16)
            acc = mm(v_scr[h, :, pl.ds(start, size)], p)
            norm = acc[64:65]
            o_scr[i, h * HD : (h + 1) * HD, :] = (acc[0:64] / norm).astype(BF16)
            parts = split3(-(top + jnp.log(norm)))
            q_scr[i, h, 96:112, :] = jnp.concatenate([*parts, jnp.zeros((13, BLK), F32)], axis=0).astype(BF16)

        for mode, size in enumerate(WINDOWS):

            @pl.when(kind == mode)
            def _():
                t0 = scores(0, size)
                t1 = scores(1, size)
                weigh(0, size, t0)
                t2 = scores(2, size)
                weigh(1, size, t1)
                weigh(2, size, t2)

        return carry

    lax.fori_loop(0, 4, q_block, 0)
    for n in range(4):
        at = slice((n % 2) * BLK, (n % 2 + 1) * BLK)
        (oa, ob)[n // 2][:, at] = o_scr[n]
        (ba, bb)[n // 2][:, :, at] = q_scr[n]


def attend(half, sp, qt, k, vt, awaits=(), carry=()):
    rows = qt[0].shape[2]
    total = 4 * rows
    out, back = ((3 * HD, rows), BF16), ((3, 128, rows), BF16)
    return run(
        functools.partial(attend_kernel, half * 4),
        8,
        18,
        (sp,),
        (qt[2 * half], qt[2 * half + 1], *k, *vt),
        (out, out, back, back),
        [
            pltpu.VMEM((3, total, 128), BF16),
            pltpu.VMEM((3, 128, total), BF16),
            pltpu.VMEM((3, total, BLK), F32),
            pltpu.VMEM((4, 3, 128, BLK), BF16),
            pltpu.VMEM((4, 3 * HD, BLK), BF16),
        ],
        awaits,
        carry,
    )


def attend_back_kernel(h, fast, sp_ref, spots, *refs):
    q_refs, kt_refs, k_refs, vt_refs, o_refs, d_refs = (refs[4 * n : 4 * n + 4] for n in range(6))
    n_given = (1, 4, 6)[h]
    cs_refs, tok_t, given, outs = refs[24:28], refs[28], refs[29 : 29 + n_given], refs[29 + n_given : -13]
    q_scr, do_scr, o_scr, kt_scr, k_scr, vt_scr, dq_scr, dk_scr, dv_scr, g_scr, tail_scr, eb_scr, sem = refs[-13:]
    rows = kt_refs[0].shape[2]
    total = 4 * rows
    head = pl.ds(h * HD, HD)
    copies = []
    for p in range(4):
        spot, at = place_of(sp_ref, p, rows), pl.ds(p * rows, rows)
        copies += [
            (kt_refs[p].at[h], kt_scr.at[:, spot]),
            (k_refs[p].at[h], k_scr.at[spot, :]),
            (vt_refs[p].at[h], vt_scr.at[:, spot]),
            (q_refs[p].at[h], q_scr.at[:, at]),
            (d_refs[p].at[head, :], do_scr.at[pl.ds(0, HD), at]),
            (o_refs[p].at[head, :], o_scr.at[:, at]),
            (d_refs[p].at[pl.ds(3 * HD, 16), :], tail_scr.at[p]),
        ]
    if h == 0:
        copies.append((d_refs[1].at[pl.ds(208, 576), :], eb_scr))
    copies = [pltpu.make_async_copy(src, dst, sem.at[n]) for n, (src, dst) in enumerate(copies)]
    for c in copies:
        c.start()
    dk_scr[...] = jnp.zeros(dk_scr.shape, F32)
    dv_scr[...] = jnp.zeros(dv_scr.shape, F32)
    for c in copies:
        c.wait()
    do_scr[64:128, :] = jnp.zeros((64, total), BF16)
    delta = jnp.sum(do_scr[0:64, :].astype(F32) * o_scr[...].astype(F32), axis=0, keepdims=True)
    do_scr[64:80, :] = jnp.concatenate([*split3(-delta), jnp.zeros((13, total), F32)], axis=0).astype(BF16)

    def q_block(i, carry):
        start, kind = window_of(sp_ref, i ^ (2 * sp_ref[8]), total)
        here = pl.ds(pl.multiple_of(i * BLK, BLK), BLK)
        for mode, size in enumerate(WINDOWS):

            @pl.when(kind == mode)
            def _():
                qt, dot = q_scr[:, here], do_scr[:, here]
                q, do = qt.astype(F32).T.astype(BF16), dot.astype(F32).T.astype(BF16)
                win = pl.ds(start, size)
                p = jnp.exp(mm(q, kt_scr[:, win]))
                ds = (p * mm(do, vt_scr[:, win])).astype(BF16)
                dv_scr[:, win] += mm(dot, p.astype(BF16))
                dk_scr[:, win] += mm(qt, ds)
                dq_scr[here, :] = mm(ds, k_scr[win, :])

        return carry

    lax.fori_loop(0, 8, q_block, 0)

    def unrotated(g, cosine, sine):
        g = g.astype(BF16).astype(F32)
        a, b = g[0:32], g[32:64]
        return jnp.concatenate([a * cosine + b * sine, b * cosine - a * sine], axis=0).astype(BF16)

    for p in range(4):
        at = slice(p * rows, (p + 1) * rows)
        cosine, sine = cs_refs[p][0:32, :], cs_refs[p][32:64, :]
        src = place_of(sp_ref, p, rows)
        g_scr[0:64, at] = unrotated(dq_scr[at, :].T[0:64] * 0.125, cosine, sine)
        g_scr[64:128, at] = unrotated(dk_scr[0:64, src], cosine, sine)
        g_scr[128:192, at] = dv_scr[0:64, src].astype(BF16)
    grad = mm(tok_t[...], g_scr[...], NT)
    heads = 3 * HD
    near, far, core = outs[0:3]
    near[...] = g_scr[:, 0:rows]
    far[0:heads, :] = g_scr[:, 2 * rows : 3 * rows]
    if h < 2:
        far[heads : 2 * heads, :] = g_scr[:, 3 * rows :]
    if h == 0:
        (ea,) = given
        grad_out, e_own, total = outs[3:]
        core[...] = g_scr[:, rows : 2 * rows]
        grad_out[...] = grad.astype(BF16)
        e = ea[...].astype(F32) + unpack_rows(eb_scr, 0, 2 * heads)
        e_own[...] = e[0:heads].astype(BF16)
        pack_rows(far, 2 * heads, e[heads:])
        sums = [tail_scr[p].astype(F32) for p in range(4)]
        joined = (sums[0] + sums[1]) + (sums[2] + sums[3])
        total[:, 0:512] = joined[0:4] + joined[4:8]
        total[:, 512:768] = (joined[8:12] + joined[12:16])[:, 0:256]
    elif h == 1:
        core_before, before, sum_own, sum_got = given
        first, second, total = outs[3:]
        core[0:heads, :] = core_before[...]
        core[heads:, :] = g_scr[:, rows : 2 * rows]
        split_rows(jnp.concatenate([before[...].astype(F32), grad], axis=1), first, second)
        total[...] = sum_own[...] + sum_got[...]
    else:
        core_before, far0, e_own, sum_own, sum_got, arrange = given
        first, second, total, cross = outs[3:]
        cross[...] = g_scr[:, 3 * rows :]
        core[0 : 2 * heads, :] = core_before[...]
        core[2 * heads : 3 * heads, :] = g_scr[:, rows : 2 * rows]
        core[3 * heads :, :] = far0[heads : 2 * heads, :]
        e = e_own[...].astype(F32) + unpack_rows(far0, 2 * heads, heads)
        if fast:
            transpose_into(eb_scr, e, spots, slice(None))
            e = eb_scr[...]
        else:
            e = mm(arrange[...], e.astype(BF16), NT)
        split_rows(jnp.concatenate([grad, e], axis=1), first, second)
        total[...] = sum_own[...] + sum_got[...]


def attend_back(h, fast, spots, sp, q, kt, k, vt, o, d, cs, tok_t, given, awaits=()):
    rows = kt[0].shape[2]
    total = 4 * rows
    width = tok_t.shape[0]
    heads = 3 * HD
    far = (2 * heads + 3 * heads // 2, 2 * heads, heads)[h]
    outs = [((heads, rows), BF16), ((far, rows), BF16), (((1, 2, 4)[h] * heads, rows), BF16)]
    if h == 0:
        outs += [((width, heads), BF16), ((heads, width), BF16)]
    else:
        outs += [((width // 2, 2 * heads), BF16)] * 2
    outs += [((4, width), F32)]
    if h == 2:
        outs += [((heads, rows), BF16)]
    return run(
        functools.partial(attend_back_kernel, h, fast),
        12,
        20,
        (sp, spots),
        (*cs, tok_t, *given),
        outs,
        [
            pltpu.VMEM((128, total), BF16),
            pltpu.VMEM((128, total), BF16),
            pltpu.VMEM((HD, total), BF16),
            pltpu.VMEM((128, total), BF16),
            pltpu.VMEM((total, 128), BF16),
            pltpu.VMEM((128, total), BF16),
            pltpu.VMEM((total, 128), F32),
            pltpu.VMEM((128, total), F32),
            pltpu.VMEM((128, total), F32),
            pltpu.VMEM((heads, total), BF16),
            pltpu.VMEM((4, 16, rows), BF16),
            pltpu.VMEM((3 * heads, rows), BF16) if h == 0 else pltpu.VMEM((width, heads), F32),
            pltpu.SemaphoreType.DMA((29,)),
        ],
        awaits,
        apart=(*q, *kt, *k, *vt, *o, *d),
    )


def norm_parts(h):
    centred = h - jnp.mean(h, axis=-1, keepdims=True)
    inverse = lax.rsqrt(jnp.mean(centred * centred, axis=-1, keepdims=True) + 1e-05)
    return centred * inverse, inverse


def norm_back(grad, normed, inverse, gain):
    scaled = grad * gain
    return inverse * (
        scaled
        - jnp.mean(scaled, axis=-1, keepdims=True)
        - normed * jnp.mean(scaled * normed, axis=-1, keepdims=True)
    )


def sigmoid(v):
    return 0.5 + 0.5 * jnp.tanh(0.5 * v)


def out_kernel(a0, a1, a2, a3, w0, w1, w2, w3, tok_ref, gain_ref, bias_ref, low_ref, xhat_ref, inv_ref):
    w = jnp.concatenate([w0[...], w1[...], w2[...], w3[...]], axis=0)
    for half in range(2):
        at = slice(half * BLK, (half + 1) * BLK)
        a = jnp.concatenate([a0[:, at], a1[:, at], a2[:, at], a3[:, at]], axis=0)
        normed, inverse = norm_parts(tok_ref[at, :].astype(F32) + mm(a, w, TN))
        xhat_ref[at, :] = normed
        inv_ref[at, :] = jnp.broadcast_to(inverse, (BLK, 128))
        low_ref[at, :] = (normed * gain_ref[...] + bias_ref[...]).astype(BF16)


def out_project(a, w, tok, gain, bias, awaits=()):
    rows, width = tok.shape
    return run(
        out_kernel,
        3,
        10,
        (),
        (*a, *w, tok, gain, bias),
        (((rows, width), BF16), ((rows, width), F32), ((rows, 128), F32)),
        awaits=awaits,
    )


def gather_weights(at_ref, parts, wgu, wd, sem):
    copies = []
    for n, part in enumerate(parts):
        dst = wgu if n < 4 else wd
        rows = dst.shape[0] // 4
        spot = pl.ds(pl.multiple_of((at_ref[0] ^ (n % 4)) * rows, rows), rows)
        copies.append(pltpu.make_async_copy(part.at[pl.ds(0, rows), :], dst.at[spot, :], sem.at[n]))
    for c in copies:
        c.start()
    return copies


def mlp_rows(x, wg, wu, down, da, db, hid):
    gate, up = mm(x, wg), mm(x, wu)
    s = sigmoid(gate)
    act = gate * s
    low = (act * up).astype(BF16)
    da[...] = (up * (s + act * (1.0 - s))).astype(BF16)
    db[...] = act.astype(BF16)
    if hid is not None:
        hid[...] = low
    return mm(low, down)


def mlp_own_kernel(ml1_ref, ml0, wgu, wd, acc, da, db, hid, ml1, sem):
    rows = ml0.shape[0]
    hidden = wd.shape[0]
    copy = pltpu.make_async_copy(ml1_ref, ml1, sem)
    copy.start()
    for block, x in enumerate((ml0, ml1)):
        if block:
            copy.wait()
        at = slice(block * rows, (block + 1) * rows)
        total = None
        for col in range(0, hidden, BLK):
            cols, ups = slice(col, col + BLK), slice(hidden + col, hidden + col + BLK)
            saved = [u.at[at, cols] for u in (da, db, hid)]
            part = mlp_rows(x[...], wgu[:, cols], wgu[:, ups], wd[cols, :], *saved)
            total = part if total is None else total + part
        acc[at, :] = total


def mlp_own(ml0, ml1, wgu, wd, awaits=()):
    rows, width = ml0.shape
    hidden = wd.shape[0]
    saved = ((2 * rows, hidden), BF16)
    return run(
        mlp_own_kernel,
        5,
        10,
        (),
        (ml0, wgu, wd),
        [((2 * rows, width), F32)] + [saved] * 3,
        [pltpu.VMEM((rows, width), BF16), pltpu.SemaphoreType.DMA],
        awaits,
        apart=(ml1,),
    )


def mlp_peer_kernel(at_ref, *refs):
    ml0, ml1, acc, own, sib, da, db, wgu, wd, sem = refs[8:]
    rows = ml0.shape[0]
    hidden = da.shape[1]
    for c in gather_weights(at_ref, refs[:8], wgu, wd, sem):
        c.wait()
    for block, x in enumerate((ml0, ml1)):
        at = slice(block * rows, (block + 1) * rows)
        total = acc[at, :]
        for col in range(0, hidden, BLK):
            cols, ups = slice(col, col + BLK), slice(hidden + col, hidden + col + BLK)
            saved = [u.at[at, cols] for u in (da, db)]
            total += mlp_rows(x[...], wgu[:, cols], wgu[:, ups], wd[cols, :], *saved, None)
        if block:
            sib[...] = total.astype(BF16)
        else:
            own[...] = total


def mlp_peer(at, ml0, ml1, acc, parts, awaits=()):
    rows, width = ml0.shape
    hidden = parts[0].shape[1] // 2
    saved = ((2 * rows, hidden), BF16)
    return run(
        mlp_peer_kernel,
        6,
        13,
        (at,),
        (ml0, ml1, acc),
        [((rows, width), F32), ((rows, width), BF16)] + [saved] * 2,
        [pltpu.VMEM((width, 2 * hidden), BF16), pltpu.VMEM((hidden, width), BF16), pltpu.SemaphoreType.DMA((8,))],
        awaits,
        apart=parts,
    )


def copies_of(src, dst, sem, rows=128):
    copies = []
    for n in range(src.shape[0] // rows):
        at = pl.ds(n * rows, rows)
        copies.append(pltpu.make_async_copy(src.at[at, :], dst.at[at, :], sem.at[n]))
        copies[-1].start()
    return copies


def mid_kernel(
    got, xhat_ref, own_ref, go_ref, g1, b1, g2, b2, out_ref, dh_ref, dm_ref, sums_ref, got_ref, sem
):
    gain_sum, bias_sum = 0.0, 0.0
    copies = copies_of(got, got_ref, sem)
    for start in range(0, xhat_ref.shape[0], 128):
        at = slice(start, start + 128)
        copies[start // 128].wait()
        mid = xhat_ref[at, :] * g1[...] + b1[...]
        normed, inverse = norm_parts(mid + (own_ref[at, :] + got_ref[at, :].astype(F32)))
        out_ref[at, :] = (normed * g2[...] + b2[...]).astype(BF16)
        grad = go_ref[at, :].astype(F32)
        dh = norm_back(grad, normed, inverse, g2[...])
        dh_ref[at, :] = dh
        dm_ref[at, :] = dh.astype(BF16)
        gain_sum += jnp.sum(grad * normed, axis=0, keepdims=True)
        bias_sum += jnp.sum(grad, axis=0, keepdims=True)
    sums_ref[0:1, :] = gain_sum
    sums_ref[1:2, :] = bias_sum


def mid_norm(xhat, own, got, out_grad, g1, b1, g2, b2, awaits=()):
    rows, width = xhat.shape
    return run(
        mid_kernel,
        3,
        8,
        (),
        (xhat, own, out_grad, g1, b1, g2, b2),
        (((rows, width), BF16), ((rows, width), F32), ((rows, width), BF16), ((2, width), F32)),
        [pltpu.VMEM((rows, width), BF16), pltpu.SemaphoreType.DMA((rows // 128,))],
        awaits,
        apart=(got,),
    )


def mlp_back_kernel(at_ref, *refs):
    dm1_ref, dm0, wgu, wd, da_o, db_o, da_p, db_p, own, sib, dg_o, du_o, wgu_p, wd_p, dm1, sem = refs[8:]
    rows = dm0.shape[0]
    hidden = wd.shape[0]
    first = pltpu.make_async_copy(dm1_ref, dm1, sem.at[8])
    first.start()
    copies = gather_weights(at_ref, refs[:8], wgu_p, wd_p, sem)

    def part_of(x, at, cols, wg, wu, down, da, db, keep):
        dhid = mm(x[...], down, NT)
        dgate = (dhid * da[at, cols].astype(F32)).astype(BF16)
        dup = (dhid * db[at, cols].astype(F32)).astype(BF16)
        if keep:
            dg_o[at, cols] = dgate
            du_o[at, cols] = dup
        return mm(dgate, wg, NT) + mm(dup, wu, NT)

    totals = [None, None]
    for peer, (gu, down, da, db) in enumerate(((wgu, wd, da_o, db_o), (wgu_p, wd_p, da_p, db_p))):
        for block, x in enumerate((dm0, dm1)):
            if block and not peer:
                first.wait()
            at = slice(block * rows, (block + 1) * rows)
            for col in range(0, hidden, BLK):
                cols, ups = slice(col, col + BLK), slice(hidden + col, hidden + col + BLK)
                part = part_of(x, at, cols, gu[:, cols], gu[:, ups], down[cols, :], da, db, not peer)
                totals[block] = part if totals[block] is None else totals[block] + part
        if not peer:
            for c in copies:
                c.wait()
    own[...] = totals[0]
    sib[...] = totals[1].astype(BF16)


def mlp_backward(at, dm0, dm1, wgu, wd, parts, da_o, db_o, da_p, db_p, awaits=()):
    rows, width = dm0.shape
    hidden = wd.shape[0]
    saved = ((2 * rows, hidden), BF16)
    return run(
        mlp_back_kernel,
        11,
        18,
        (at,),
        (dm0, wgu, wd, da_o, db_o, da_p, db_p),
        [((rows, width), F32), ((rows, width), BF16)] + [saved] * 2,
        [
            pltpu.VMEM((width, 2 * hidden), BF16),
            pltpu.VMEM((hidden, width), BF16),
            pltpu.VMEM((rows, width), BF16),
            pltpu.SemaphoreType.DMA((9,)),
        ],
        awaits,
        apart=(*parts, dm1),
    )


def first_norm_kernel(
    got_ref, dh2, own, xhat, inv, g1, sums2, a0, a1, a2, a3, w0, w1, w2, w3,
    dh1, d0, d1, d2, d3, ea, dat_scr, got, sem,
):
    gain_sum, bias_sum = 0.0, 0.0
    copies = copies_of(got_ref, got, sem)
    for start in range(0, dh2.shape[0], 128):
        at = slice(start, start + 128)
        copies[start // 128].wait()
        dmid = dh2[at, :] + (own[at, :] + got[at, :].astype(F32))
        normed = xhat[at, :]
        gain_sum += jnp.sum(dmid * normed, axis=0, keepdims=True)
        bias_sum += jnp.sum(dmid, axis=0, keepdims=True)
        grad = norm_back(dmid, normed, inv[at, 0:1], g1[...])
        dh1[at, :] = grad
        dat_scr[at, :] = grad.astype(BF16)
    sums = jnp.concatenate([gain_sum, bias_sum, sums2[...]], axis=0)
    high = sums.astype(BF16).astype(F32)
    both = jnp.concatenate([high, sums - high], axis=0)
    rest = jnp.concatenate([both[:, 512:], jnp.zeros((8, dh2.shape[0] - 256), F32)], axis=1)
    tail = jnp.concatenate([both[:, 0:512], rest], axis=0).astype(BF16)
    dat = dat_scr[...]
    for w, d in ((w0, d0), (w1, d1), (w2, d2), (w3, d3)):
        d[0:192, :] = mm(w[...], dat, NT).astype(BF16)
        d[192:208, :] = tail
    ea[...] = mm(jnp.concatenate([a0[...], a2[...]], axis=0), dat).astype(BF16)
    pack_rows(d1, 208, mm(jnp.concatenate([a1[...], a3[...]], axis=0), dat))


def pack_rows(dst, start, value):
    n = value.shape[0]
    rest = value[:, 512:]
    dst[start : start + n, :] = value[:, 0:512].astype(dst.dtype)
    dst[start + n : start + n + n // 2, :] = jnp.concatenate([rest[0 : n // 2], rest[n // 2 :]], axis=1).astype(dst.dtype)


def unpack_rows(src, start, n):
    rest = src[start + n : start + n + n // 2, :].astype(F32)
    rest = jnp.concatenate([rest[:, 0:256], rest[:, 256:]], axis=0)
    return jnp.concatenate([src[start : start + n, :].astype(F32), rest], axis=1)


def first_norm_back(dh2, own, got, xhat, inv, g1, sums2, a, w, awaits=()):
    rows, width = dh2.shape
    heads = a[0].shape[0]
    d = ((heads + 16, rows), BF16)
    return run(
        first_norm_kernel,
        5,
        12,
        (),
        (dh2, own, xhat, inv, g1, sums2, *a, *w),
        [((rows, width), F32), d, ((4 * heads + 16, rows), BF16), d, d, ((2 * heads, width), BF16)],
        [pltpu.VMEM((rows, width), BF16), pltpu.VMEM((rows, width), BF16), pltpu.SemaphoreType.DMA((rows // 128,))],
        awaits,
        apart=(got,),
    )


def far_kernel(
    fast, spots, dm0, dm1, dm2, dm3, ml2, ml3, wgu, wd, hid_o, first, second, dg, du, dmt, hids
):
    rows = dm0.shape[0]
    hidden = wd.shape[0]
    for p, u in enumerate((dm0, dm1, dm2, dm3)):
        transpose_into(dmt, u[...], spots if fast else None, slice(p * rows, (p + 1) * rows))
    for col in range(0, hidden, BLK):
        cols, ups = slice(col, col + BLK), slice(hidden + col, hidden + col + BLK)
        hids[0 : 2 * rows, :] = hid_o[:, cols]
        for block, (x, dm) in enumerate(((ml2, dm2), (ml3, dm3))):
            at = slice(block * rows, (block + 1) * rows)
            gate, up, dhid = mm(x[...], wgu[:, cols]), mm(x[...], wgu[:, ups]), mm(dm[...], wd[cols, :], NT)
            s = sigmoid(gate)
            act = gate * s
            hids[(2 + block) * rows : (3 + block) * rows, :] = (act * up).astype(BF16)
            dg[at, cols] = (dhid * (up * (s + act * (1.0 - s)))).astype(BF16)
            du[at, cols] = (dhid * act).astype(BF16)
        split_rows(mm(dmt[...], hids[...]), first.at[:, cols], second.at[:, cols])


def far_rows(fast, spots, dm, ml, wgu, wd, hid, awaits=(), carry=()):
    rows, width = dm[0].shape
    hidden = wd.shape[0]
    return run(
        functools.partial(far_kernel, fast),
        8,
        14,
        (spots,),
        (*dm, *ml, wgu, wd, hid),
        [((width // 2, hidden), BF16)] * 2 + [((2 * rows, hidden), BF16)] * 2,
        [pltpu.VMEM((width, 4 * rows), BF16), pltpu.VMEM((4 * rows, BLK), BF16)],
        awaits,
        carry,
    )


def weight_kernel(fast, spots, ml0, ml1, ml2, ml3, dg_o, du_o, dg_f, du_f, first, second, mlt):
    rows = ml0.shape[0]
    hidden = dg_o.shape[1]
    for p, u in enumerate((ml0, ml1, ml2, ml3)):
        transpose_into(mlt, u[...], spots if fast else None, slice(p * rows, (p + 1) * rows))
    for n, (near, far) in enumerate(((dg_o, dg_f), (du_o, du_f))):
        cols = slice(n * hidden, (n + 1) * hidden)
        grad = mm(mlt[:, 0 : 2 * rows], near[...]) + mm(mlt[:, 2 * rows :], far[...])
        split_rows(grad, first.at[:, cols], second.at[:, cols])


def weight_grads(fast, spots, ml, near, far, awaits=()):
    rows, width = ml[0].shape
    hidden = near[0].shape[1]
    return run(
        functools.partial(weight_kernel, fast),
        6,
        14,
        (spots,),
        (*ml, *near, *far),
        [((width // 2, 2 * hidden), BF16)] * 2,
        [pltpu.VMEM((width, 4 * rows), BF16)],
        awaits,
    )


def input_kernel(dh1, n0, n1, n2, core, core1, f0, f1, f2, x2, w0, w1, w2, w3, out):
    rows = n0.shape[1]
    heads = 3 * HD
    sources = (
        ((n0, 0), (n1, 0), (n2, 0)),
        ((core, 0), (core, heads), (core, 2 * heads)),
        ((f0, 0), (f1, 0), (f2, 0)),
        ((core, 3 * heads), (core1, heads), (x2, 0)),
    )
    for half in range(rows // BLK):
        at = slice(half * BLK, (half + 1) * BLK)
        total = dh1[at, :]
        for source, w in zip(sources, (w0, w1, w2, w3)):
            cat = jnp.concatenate([ref[start : start + heads, at] for ref, start in source], axis=0)
            parts = [w[c * heads + h * HD : c * heads + (h + 1) * HD, :] for h in range(3) for c in range(3)]
            total += mm(cat, jnp.concatenate(parts, axis=0), TN)
        out[at, :] = total


def input_back(dh1, near, core, core1, far, far2, weights, awaits=()):
    args = (dh1, *near, core, core1, *far, far2, *weights)
    return run(input_kernel, 4, 12, (), args, [(dh1.shape, F32)], awaits=awaits)[0]


def swap(v, bit, axis="tensor"):
    n = lax.axis_size(axis)
    return lax.ppermute(v, axis, [(i, i ^ bit) for i in range(n)])


def bits_of(n):
    return n.bit_length() - 1


def spots_of(order, n):
    block = jnp.arange(n, dtype=jnp.int32) ^ lax.axis_index("dp")
    spot = jnp.zeros((n,), jnp.int32)
    for s, bit in enumerate(order):
        spot = spot + (((block >> bit) & 1) << (len(order) - 1 - s))
    return spot


def last_kernel(chains, kind, *refs):
    count = sum(chains)
    parts, outs, scrs, sem = refs[:count], refs[count:-count - 1], refs[-count - 1 : -1], refs[-1]
    copies = []
    for n, (part, scr) in enumerate(zip(parts, scrs)):
        copies.append(pltpu.make_async_copy(part.at[pl.ds(0, scr.shape[0]), :], scr, sem.at[n]))
        copies[-1].start()
    for c in copies:
        c.wait()
    sums, at = [], 0
    for length in chains:
        sums.append(sum(scr[...].astype(F32) for scr in scrs[at : at + length]))
        at += length
    if kind == "mlp":
        gu, down = outs
        half = gu.shape[2]
        gu[:, 0, :] = sums[0][:, 0:half]
        gu[:, 1, :] = sums[0][:, half:]
        down[...] = sums[1]
    else:
        qkv, out = outs
        total = jnp.concatenate([sums[0], sums[1]], axis=1)
        if len(sums) > 2:
            total += sums[2]
        for c in range(3):
            qkv[c] = jnp.concatenate([total[:, (3 * h + c) * HD : (3 * h + c + 1) * HD] for h in range(3)], axis=1)
        out[...] = total[:, 9 * HD :].T


def last_sums(kind, rows, chains, outs):
    parts = [part for chain in chains for part in chain]
    return run(
        functools.partial(last_kernel, [len(chain) for chain in chains], kind),
        2,
        8,
        (),
        (),
        outs,
        [pltpu.VMEM((rows, part.shape[1]), BF16) for part in parts] + [pltpu.SemaphoreType.DMA((len(parts),))],
        apart=parts,
    )


class scatter_steps:
    def __init__(self, first, second, order):
        self.first, self.parts, self.order, self.step = first, [first], order, 0
        self.sent = second

    def advance(self):
        self.parts.append(swap(self.sent, 1 << self.order[self.step], "dp"))
        self.step += 1
        if self.step < len(self.order):
            length = self.parts[-1].shape[0]
            self.sent = sum(u[length // 2 : length].astype(F32) for u in self.parts).astype(BF16)
        return self.parts[-1]

    def all_parts(self):
        while self.step < len(self.order):
            self.advance()
        return self.parts


def joined_steps(one, two):
    order, both = one.order, []
    for step in range(1, len(order)):
        length = (both or one.parts)[-1].shape[0] // 2
        at = slice(length, 2 * length)
        sent = jnp.concatenate([sum(u[at].astype(F32) for u in chain.parts) for chain in (one, two)], axis=1)
        both.append(swap(sum((u[at].astype(F32) for u in both), sent).astype(BF16), 1 << order[step], "dp"))
    return one.parts, two.parts, both


def first_sums(chains, rows):
    sums = [sum(part[0:rows].astype(F32) for part in chain) for chain in chains]
    if len(sums) == 3:
        return jnp.concatenate(sums[0:2], axis=1) + sums[2]
    return sums


def quarter_of(w):
    rows = w.shape[0] // 4
    return lax.dynamic_slice_in_dim(w, (lax.axis_index("dp") % 4) * rows, rows, axis=0)


def local(
    tokens,
    doc_lengths,
    key_mask,
    qkv_weight,
    out_weight,
    gate_up_weight,
    down_weight,
    norm1_gain,
    norm1_bias,
    norm2_gain,
    norm2_bias,
    out_grad,
):
    rows, width = tokens.shape
    flags = jnp.pad(key_mask.astype(BF16).reshape(1, rows), ((0, EXTRA - 1), (0, width - rows)))
    tok0 = jnp.concatenate([tokens, flags], axis=0)
    tok1 = swap(tok0, 1)
    tok2 = swap(tok0, 2)
    sp = jnp.concatenate([doc_lengths[0], lax.axis_index("tensor").reshape(1)]).astype(jnp.int32)
    quarter = (lax.axis_index("dp") % 4).reshape(1).astype(jnp.int32)
    freqs = 1000.0 ** (-(jnp.arange(HD // 2, dtype=F32) * 2.0 / HD))
    freqs = jnp.broadcast_to(freqs[:, None], (HD // 2, 128))
    wt = jnp.transpose(qkv_weight, (1, 2, 0)).reshape(-1, width)

    n_dp = lax.axis_size("dp")
    fast = (width // n_dp) % 16 == 0
    order = list(range(bits_of(n_dp)))
    order_d = order[1:2] + order[0:1] + order[2:]
    spots, spots_d = spots_of(order, n_dp), spots_of(order_d, n_dp)

    def arranged(v, at):
        if fast:
            return v
        blocks = v.reshape(v.shape[0], n_dp, width // n_dp)
        return jnp.take(blocks, jnp.argsort(at), axis=1).reshape(v.shape)

    ORDER.last = ()
    wo0 = out_weight
    wo1 = swap(wo0, 1)
    wgu = gate_up_weight.reshape(width, -1)
    part_a = jnp.concatenate([quarter_of(down_weight), quarter_of(out_weight)], axis=0)
    part_b = quarter_of(wgu)
    pa0 = swap(part_a, 2)

    proj = [project(0, sp, freqs, tok0, wt), project(1, sp, freqs, tok1, wt, awaits=(part_a, part_b))]
    (tok2,) = gate(tok2)
    tok3 = swap(tok2, 1)
    tok = (tok0, tok1, tok2, tok3)
    *more, part_b = project(2, sp, freqs, tok2, wt, carry=(part_b,))
    proj.append(more)
    pb0 = swap(part_b, 2)
    proj.append(project(3, sp, freqs, tok3, wt))
    qt, kt, k, vt, cs = zip(*proj)
    o2, o3, q2, q3 = attend(1, sp, qt, k, vt, (wo1,))
    o2, o3 = gate(o2, o3, awaits=(pa0,))
    pa1, pa2, pa3 = swap(pa0, 1, "dp"), swap(pa0, 2, "dp"), swap(pa0, 3, "dp")
    g2, g3 = swap(o2, 2), swap(o3, 3)
    o0, o1, q0, q1 = attend(0, sp, qt, k, vt)
    o1, pb0 = gate(o1, pb0)
    g1 = swap(o1, 1)
    tok_t, wo2 = transposed(
        fast, spots, quarter, [arranged(u, spots) for u in tok], rows, (pa0, pa1, pa2, pa3), wo0
    )
    wo3 = swap(wo2, 1)
    wo = (wo0, wo1, wo2, wo3)

    gain1, bias1, gain2, bias2 = (u.reshape(1, width) for u in (norm1_gain, norm1_bias, norm2_gain, norm2_bias))
    ml0, xhat1, inv1 = out_project((o0, g1, g2, g3), wo, tokens, gain1, bias1)
    ml0, pb0 = gate(ml0, pb0)
    pb1, pb2, pb3 = swap(pb0, 1, "dp"), swap(pb0, 2, "dp"), swap(pb0, 3, "dp")
    ml1, ml2 = swap(ml0, 1), swap(ml0, 2)
    acc, da_o, db_o, hid_o = mlp_own(ml0, ml1, wgu, down_weight)
    parts = (pb0, pb1, pb2, pb3, pa0, pa1, pa2, pa3)
    own, sib, da_p, db_p = mlp_peer(quarter, ml0, ml1, acc, parts)
    output, dh2, dm0, sums2 = mid_norm(xhat1, own, swap(sib, 1), out_grad, gain1, bias1, gain2, bias2)
    dm0, ml2 = gate(dm0, ml2)
    dm1, dm2 = swap(dm0, 1), swap(dm0, 2)
    ml3 = swap(ml2, 1)
    own, sib, dg_o, du_o = mlp_backward(quarter, dm0, dm1, wgu, down_weight, parts, da_o, db_o, da_p, db_p)
    (sib,) = gate(sib, awaits=(ml3,))
    dh1, d0, d1, d2, d3, ea = first_norm_back(
        dh2, own, swap(sib, 1), xhat1, inv1, gain1, sums2, (o0, g1, g2, g3), wo, (dm2,)
    )
    d1, d2, d3 = gate(d1, d2, d3)
    dm3 = swap(dm2, 1)
    d = (d0, swap(d1, 1), swap(d2, 2), swap(d3, 3))
    ml = [arranged(u, spots) for u in (ml0, ml1, ml2, ml3)]
    dm = [arranged(u, spots_d) for u in (dm0, dm1, dm2, dm3)]
    d_first, d_second, dg_f, du_f = far_rows(fast, spots_d, dm, ml[2:], wgu, down_weight, hid_o)
    wt0 = wt
    d_second, wt = gate(d_second, wt, awaits=d[1:])
    dn = scatter_steps(d_first, d_second, order_d)
    dn1 = dn.advance()
    wt1, wt2 = swap(wt0, 1), swap(wt, 2)
    gu_first, gu_second = weight_grads(fast, spots, ml, (dg_o, du_o), (dg_f, du_f))
    (gu_second,) = gate(gu_second, awaits=(wt1,))
    gu = scatter_steps(gu_first, gu_second, order)
    gu1 = gu.advance()

    arrange = jnp.zeros((8, 128), BF16)
    if not fast:
        column = jnp.arange(width)
        target = spots[column // (width // n_dp)] * (width // n_dp) + column % (width // n_dp)
        arrange = (column[:, None] == target[None, :]).astype(BF16)
    back = functools.partial(
        attend_back,
        fast=fast,
        spots=spots,
        sp=sp,
        q=(q0, q1, q2, q3),
        kt=kt,
        k=k,
        vt=vt,
        o=(o0, o1, o2, o3),
        d=d,
        cs=cs,
        tok_t=tok_t,
    )
    near0, far0, core0, grad0, e_own, sums = back(0, given=(ea,))
    far0, sums = gate(far0, sums, awaits=(dn1,))
    got0, dn2 = swap(far0, 2), dn.advance()
    sum_bits = [*order[1:], 0]
    sums_got = swap(sums, 1 << sum_bits[0], "dp")
    near1, far1, core1, first, second, sums = back(1, given=(core0, grad0, sums, sums_got))
    far1, second, sums = gate(far1, second, sums, awaits=(gu1, wt2))
    c1 = scatter_steps(first, second, order)
    c1_got, gu2 = c1.advance(), gu.advance()
    got1 = swap(far1, 2)
    sums_got = swap(sums, 1 << sum_bits[1], "dp")
    near2, far2, core2, first, second, sums, cross2 = back(
        2, given=(core1, got0, e_own, sums, sums_got, arrange)
    )
    far2, core2, second, sums, cross2, wt2 = gate(
        far2, core2, second, sums, cross2, wt2, awaits=(c1_got, gu2, got1, dn2)
    )
    c2 = scatter_steps(first, second, order)
    c2.advance()
    wt3 = swap(wt2, 1)
    for bit in sum_bits[2:]:
        sums = sums + swap(sums, 1 << bit, "dp")
    gu, dn, attention = gu.all_parts(), dn.all_parts(), joined_steps(c1, c2)
    core, core1 = swap(core2, 1), swap(got1, 1)
    got2, x2 = swap(far2, 2), swap(cross2, 3)
    input_grad = input_back(dh1, (near0, near1, near2), core, core1, (got0, got1, got2), x2, (wt, wt1, wt2, wt3))
    shard = width // n_dp
    if fast:
        hidden = down_weight.shape[0]
        gu_part, down_part = last_sums("mlp", shard, (gu, dn), [((shard, 2, hidden), F32), ((shard, hidden), F32)])
        qkv_part, out_part = last_sums(
            "attention", shard, attention, [((3, shard, 3 * HD), F32), ((3 * HD, shard), F32)]
        )
        qkv_part = jnp.transpose(qkv_part, (1, 0, 2))
    else:
        gu_part, down_part = first_sums((gu, dn), shard)
        gu_part = gu_part.reshape(shard, 2, -1)
        total = first_sums(attention, shard)
        out_part = total[:, 9 * HD :].T
        qkv_part = jnp.transpose(total[:, 0 : 9 * HD].reshape(shard, 3, 3, HD), (0, 2, 1, 3)).reshape(shard, 3, 3 * HD)
    return (
        output,
        input_grad,
        qkv_part,
        out_part,
        gu_part,
        down_part.T,
        sums[0],
        sums[1],
        sums[2],
        sums[3],
    )


def solution(mesh):
    placed = (
        P(("dp", "tensor"), None),
        P("dp", None),
        P(("dp", "tensor")),
        P(None, None, "tensor"),
        P("tensor", None),
        P(None, None, "tensor"),
        P("tensor", None),
        P(),
        P(),
        P(),
        P(),
        P(("dp", "tensor"), None),
    )
    return jax.shard_map(
        local,
        mesh=mesh,
        in_specs=placed,
        out_specs=(
            P(("dp", "tensor"), None),
            P(("dp", "tensor"), None),
            P("dp", None, "tensor"),
            P("tensor", "dp"),
            P("dp", None, "tensor"),
            P("tensor", "dp"),
            P(),
            P(),
            P(),
            P(),
        ),
        check_vma=False,
    )
```

```python
import functools

import jax
import jax.numpy as jnp
from jax import lax
from jax.experimental import pallas as pl
from jax.experimental.pallas import tpu as pltpu
from jax.sharding import PartitionSpec as P

HD = 64
F32 = jnp.float32
BF16 = jnp.bfloat16
BIG = -1e30
BLK = 256
WINDOWS = (640, 1664, 2048)
SCALE = 0.15
EXTRA = 16
NN = (((1,), (0,)), ((), ()))
NT = (((1,), (1,)), ((), ()))
TN = (((0,), (0,)), ((), ()))


def mm(a, b, dims=NN):
    return lax.dot_general(a, b, dims, preferred_element_type=F32)


class Order:
    def __init__(self):
        self.last = ()


ORDER = Order()


def run(kernel, us, mib, scalars, args, outs, scratch=(), awaits=(), carry=(), apart=(), hbm=()):
    in_vmem = pl.BlockSpec(memory_space=pltpu.VMEM)
    anywhere = pl.BlockSpec(memory_space=pl.ANY)
    awaits = (*awaits, *ORDER.last)
    n_in = len(scalars) + len(apart) + len(args)
    n_skip, n_out = len(awaits) + len(carry), len(outs)

    def body(*refs):
        rest = refs[n_in + n_skip :]
        kernel(*refs[:n_in], *rest[:n_out], *rest[n_out + len(carry) :])

    results = pl.pallas_call(
        body,
        in_specs=[pl.BlockSpec(memory_space=pltpu.SMEM)] * len(scalars)
        + [anywhere] * len(apart)
        + [in_vmem] * len(args)
        + [anywhere] * n_skip,
        out_specs=[pl.BlockSpec(memory_space=pltpu.HBM) if n in hbm else in_vmem for n in range(n_out)]
        + [anywhere] * len(carry),
        out_shape=[jax.ShapeDtypeStruct(*o) for o in outs] + [jax.ShapeDtypeStruct(c.shape, c.dtype) for c in carry],
        scratch_shapes=list(scratch),
        input_output_aliases={n_in + len(awaits) + i: n_out + i for i in range(len(carry))},
        compiler_params=pltpu.CompilerParams(vmem_limit_bytes=mib << 20),
        cost_estimate=pl.CostEstimate(flops=int(us * SCALE * 1.1e9), bytes_accessed=1 << 18, transcendentals=0),
    )(*scalars, *apart, *args, *awaits, *carry)
    ORDER.last = (min(results[:n_out], key=lambda r: r.size),)
    return results


def gate_kernel(out):
    out[...] = jnp.zeros(out.shape, F32)


def gate(*arrays, awaits=()):
    return run(gate_kernel, 0.1, 4, (), (), [((8, 128), F32)], awaits=awaits, carry=arrays)[1:]


def park_kernel(places, *refs):
    count = len(places)
    copies = []
    for n, (first, rows) in enumerate(places):
        src = refs[n] if rows is None else refs[n].at[pl.ds(first, rows), :]
        copies.append(pltpu.make_async_copy(src, refs[count + n], refs[-1].at[n]))
        copies[-1].start()
    for c in copies:
        c.wait()


def park(arrays, halves=()):
    places = [(0, None) for _ in arrays] + [(n * (u.shape[0] // 2), u.shape[0] // 2) for u, n in halves]
    outs = [(u.shape, u.dtype) for u in arrays] + [((u.shape[0] // 2, u.shape[1]), u.dtype) for u, n in halves]
    return run(
        functools.partial(park_kernel, places),
        3,
        4,
        (),
        (),
        outs,
        [pltpu.SemaphoreType.DMA((len(outs),))],
        apart=(*arrays, *[u for u, n in halves]),
        hbm=range(len(outs)),
    )


def split3(v):
    top = v.astype(BF16).astype(F32)
    rest = v - top
    middle = rest.astype(BF16).astype(F32)
    return top, middle, rest - middle


def split_rows(value, first, second):
    half = first.shape[0]
    first[...] = value[0:half].astype(first.dtype)
    second[...] = value[half:].astype(second.dtype)


def transpose_into(dst, value, spots, cols):
    turned = value.T
    if spots is None:
        dst[:, cols] = turned
        return
    count = spots.shape[0]
    rows = turned.shape[0] // count
    for b in range(count):
        dst[pl.ds(pl.multiple_of(spots[b] * rows, rows), rows), cols] = turned[b * rows : (b + 1) * rows]


def transpose_kernel(fast, spots, t0, t1, t2, t3, out):
    rows = out.shape[1] // 4
    for p, t in enumerate((t0, t1, t2, t3)):
        transpose_into(out, t[0:rows, :], spots if fast else None, slice(p * rows, (p + 1) * rows))


def transposed(fast, spots, pieces, rows):
    width = pieces[0].shape[1]
    return run(functools.partial(transpose_kernel, fast), 2, 8, (spots,), pieces, [((width, 4 * rows), BF16)])[0]


def together_kernel(at_ref, p0, p1, p2, p3, out, sem):
    part = out.shape[0] // 4
    copies = []
    for n, p in enumerate((p0, p1, p2, p3)):
        spot = pl.ds(pl.multiple_of((at_ref[0] ^ n) * part, part), part)
        copies.append(pltpu.make_async_copy(p.at[pl.ds(p.shape[0] - part, part), :], out.at[spot, :], sem.at[n]))
        copies[-1].start()
    for c in copies:
        c.wait()


def together(at, parts, shape, awaits=()):
    return run(
        together_kernel, 1, 4, (at,), (), [(shape, BF16)], [pltpu.SemaphoreType.DMA((4,))], awaits, apart=parts
    )[0]


def project_kernel(piece, sp_ref, freq_ref, tok_ref, w_ref, qt_ref, kt_ref, k_ref, vt_ref, cs_ref):
    n = tok_ref.shape[0] - EXTRA
    place = (sp_ref[8] ^ piece) * n + lax.broadcasted_iota(jnp.int32, (1, n), 1)
    seg = jnp.zeros((1, n), jnp.int32)
    pos = place
    end = 0
    for d in range(8):
        length = sp_ref[d]
        end = end + length
        past = place >= end
        seg += past.astype(jnp.int32)
        pos -= jnp.where(past, length, 0)
    angles = pos.astype(F32) * freq_ref[:, 0:1]
    cosine, sine = jnp.cos(angles), jnp.sin(angles)
    cs_ref[0:32, :] = cosine
    cs_ref[32:64, :] = sine
    idx = lax.broadcasted_iota(jnp.int32, (64, n), 0)
    which = jnp.where(idx < 19, idx - 8, idx - 19)
    bit = (jnp.broadcast_to(place, (64, n)) >> jnp.clip(which, 0, 10)) & 1
    flipped = jnp.where(idx < 19, bit, 1 - bit).astype(F32)
    same = (idx == seg).astype(F32)
    coded = (idx >= 8) & (idx < 30)
    invalid = 1.0 - tok_ref[n : n + EXTRA, 0:n].astype(F32)[0:1]
    q_tail = jnp.where(idx < 8, BIG * (1.0 - same), jnp.where(coded, BIG * flipped, 0.0))
    k_tail = jnp.where(idx < 8, same, jnp.where(coded, invalid * (1.0 - flipped), 0.0))
    k_tail = jnp.where((idx >= 32) & (idx < 35), 1.0, k_tail)
    v_tail = jnp.where(idx < 3, 1.0, 0.0)
    y = mm(w_ref[...], tok_ref[0:n, :], NT)

    def rotated(at):
        a, b = y[at : at + 32], y[at + 32 : at + 64]
        return jnp.concatenate([a * cosine - b * sine, b * cosine + a * sine], axis=0)

    for h in range(3):
        qt_ref[h] = jnp.concatenate([rotated(h * HD) * 0.125, q_tail], axis=0).astype(BF16)
        key = jnp.concatenate([rotated(192 + h * HD), k_tail], axis=0)
        kt_ref[h] = key.astype(BF16)
        k_ref[h] = key.T.astype(BF16)
        vt_ref[h] = jnp.concatenate([y[384 + h * HD : 448 + h * HD], v_tail], axis=0).astype(BF16)


def project(piece, sp, freqs, tok, w, awaits=(), carry=()):
    rows = tok.shape[0] - EXTRA
    wide, tall = ((3, 128, rows), BF16), ((3, rows, 128), BF16)
    return run(
        functools.partial(project_kernel, piece),
        2.5,
        10,
        (sp,),
        (freqs, tok, w),
        (wide, wide, tall, wide, ((HD, rows), F32)),
        awaits=awaits,
        carry=carry,
    )


def window_of(sp_ref, block, total):
    a = block * BLK
    b = a + BLK - 1
    first, last, end = 0, 0, 0
    for d in range(8):
        begin, end = end, end + sp_ref[d]
        first = jnp.where(begin <= a, begin, first)
        last = jnp.where(begin <= b, end, last)
    start = (first // 128) * 128
    kind = jnp.where(last - start <= WINDOWS[0], 0, jnp.where(last - start <= WINDOWS[1], 1, 2))
    size = jnp.where(kind == 0, WINDOWS[0], jnp.where(kind == 1, WINDOWS[1], WINDOWS[2]))
    return pl.multiple_of(jnp.minimum(start, total - size), 128), kind


def place_of(sp_ref, piece, rows):
    return pl.ds(pl.multiple_of((sp_ref[8] ^ piece) * rows, rows), rows)


def attend_kernel(base, sp_ref, qa, qb, k0, k1, k2, k3, v0, v1, v2, v3, oa, ob, ba, bb, k_scr, v_scr, s_scr, q_scr, o_scr):
    rows = qa.shape[2]
    total = 4 * rows
    for p, (k, v) in enumerate(((k0, v0), (k1, v1), (k2, v2), (k3, v3))):
        at = place_of(sp_ref, p, rows)
        k_scr[:, at, :] = k[...]
        v_scr[:, :, at] = v[...]
    for n in range(4):
        q_scr[n] = (qa, qb)[n // 2][:, :, (n % 2) * BLK : (n % 2 + 1) * BLK]

    def q_block(i, carry):
        start, kind = window_of(sp_ref, (base + i) ^ (2 * sp_ref[8]), total)

        def scores(h, size):
            s = mm(k_scr[h, pl.ds(start, size), :], q_scr[i, h])
            s_scr[h, 0:size, :] = s
            return jnp.max(s, axis=0, keepdims=True)

        def weigh(h, size, top):
            p = jnp.exp(s_scr[h, 0:size, :] - top).astype(BF16)
            acc = mm(v_scr[h, :, pl.ds(start, size)], p)
            norm = acc[64:65]
            o_scr[i, h * HD : (h + 1) * HD, :] = (acc[0:64] / norm).astype(BF16)
            parts = split3(-(top + jnp.log(norm)))
            q_scr[i, h, 96:112, :] = jnp.concatenate([*parts, jnp.zeros((13, BLK), F32)], axis=0).astype(BF16)

        for mode, size in enumerate(WINDOWS):

            @pl.when(kind == mode)
            def _():
                t0 = scores(0, size)
                t1 = scores(1, size)
                weigh(0, size, t0)
                t2 = scores(2, size)
                weigh(1, size, t1)
                weigh(2, size, t2)

        return carry

    lax.fori_loop(0, 4, q_block, 0)
    for n in range(4):
        at = slice((n % 2) * BLK, (n % 2 + 1) * BLK)
        (oa, ob)[n // 2][:, at] = o_scr[n]
        (ba, bb)[n // 2][:, :, at] = q_scr[n]


def attend(half, sp, qt, k, vt, awaits=(), carry=()):
    rows = qt[0].shape[2]
    total = 4 * rows
    out, back = ((3 * HD, rows), BF16), ((3, 128, rows), BF16)
    return run(
        functools.partial(attend_kernel, half * 4),
        8,
        18,
        (sp,),
        (qt[2 * half], qt[2 * half + 1], *k, *vt),
        (out, out, back, back),
        [
            pltpu.VMEM((3, total, 128), BF16),
            pltpu.VMEM((3, 128, total), BF16),
            pltpu.VMEM((3, total, BLK), F32),
            pltpu.VMEM((4, 3, 128, BLK), BF16),
            pltpu.VMEM((4, 3 * HD, BLK), BF16),
        ],
        awaits,
        carry,
    )


def attend_back_kernel(h, fast, sp_ref, spots, *refs):
    q_refs, kt_refs, k_refs, vt_refs, o_refs, d_refs = (refs[4 * n : 4 * n + 4] for n in range(6))
    n_given = (1, 2, 4)[h]
    cs_refs, tok_t, given, outs = refs[24:28], refs[28], refs[29 : 29 + n_given], refs[29 + n_given : -12]
    q_scr, do_scr, o_scr, kt_scr, k_scr, vt_scr, dq_scr, dk_scr, dv_scr, g_scr, eb_scr, sem = refs[-12:]
    rows = kt_refs[0].shape[2]
    total = 4 * rows
    head = pl.ds(h * HD, HD)
    copies = []
    for p in range(4):
        spot, at = place_of(sp_ref, p, rows), pl.ds(p * rows, rows)
        copies += [
            (kt_refs[p].at[h], kt_scr.at[:, spot]),
            (k_refs[p].at[h], k_scr.at[spot, :]),
            (vt_refs[p].at[h], vt_scr.at[:, spot]),
            (q_refs[p].at[h], q_scr.at[:, at]),
            (d_refs[p].at[head, :], do_scr.at[pl.ds(0, HD), at]),
            (o_refs[p].at[head, :], o_scr.at[:, at]),
        ]
    if h == 0:
        copies.append((d_refs[1].at[pl.ds(208, 576), :], eb_scr))
    copies = [pltpu.make_async_copy(src, dst, sem.at[n]) for n, (src, dst) in enumerate(copies)]
    for c in copies:
        c.start()
    dk_scr[...] = jnp.zeros(dk_scr.shape, F32)
    dv_scr[...] = jnp.zeros(dv_scr.shape, F32)
    for c in copies:
        c.wait()
    do_scr[64:128, :] = jnp.zeros((64, total), BF16)
    delta = jnp.sum(do_scr[0:64, :].astype(F32) * o_scr[...].astype(F32), axis=0, keepdims=True)
    do_scr[64:80, :] = jnp.concatenate([*split3(-delta), jnp.zeros((13, total), F32)], axis=0).astype(BF16)

    def q_block(i, carry):
        start, kind = window_of(sp_ref, i ^ (2 * sp_ref[8]), total)
        here = pl.ds(pl.multiple_of(i * BLK, BLK), BLK)
        for mode, size in enumerate(WINDOWS):

            @pl.when(kind == mode)
            def _():
                qt, dot = q_scr[:, here], do_scr[:, here]
                q, do = qt.astype(F32).T.astype(BF16), dot.astype(F32).T.astype(BF16)
                win = pl.ds(start, size)
                p = jnp.exp(mm(q, kt_scr[:, win]))
                ds = (p * mm(do, vt_scr[:, win])).astype(BF16)
                dv_scr[:, win] += mm(dot, p.astype(BF16))
                dk_scr[:, win] += mm(qt, ds)
                dq_scr[here, :] = mm(ds, k_scr[win, :])

        return carry

    lax.fori_loop(0, 8, q_block, 0)

    def unrotated(g, cosine, sine):
        g = g.astype(BF16).astype(F32)
        a, b = g[0:32], g[32:64]
        return jnp.concatenate([a * cosine + b * sine, b * cosine - a * sine], axis=0).astype(BF16)

    for p in range(4):
        at = slice(p * rows, (p + 1) * rows)
        cosine, sine = cs_refs[p][0:32, :], cs_refs[p][32:64, :]
        src = place_of(sp_ref, p, rows)
        g_scr[0:64, at] = unrotated(dq_scr[at, :].T[0:64] * 0.125, cosine, sine)
        g_scr[64:128, at] = unrotated(dk_scr[0:64, src], cosine, sine)
        g_scr[128:192, at] = dv_scr[0:64, src].astype(BF16)
    grad = mm(tok_t[...], g_scr[...], NT)
    heads = 3 * HD
    near, far, core = outs[0:3]
    near[...] = g_scr[:, 0:rows]
    far[0:heads, :] = g_scr[:, 2 * rows : 3 * rows]
    far[heads : 2 * heads, :] = g_scr[:, 3 * rows :]
    if h == 0:
        (ea,) = given
        grad_out, e_own = outs[3:]
        core[...] = g_scr[:, rows : 2 * rows]
        grad_out[...] = grad.astype(BF16)
        e = ea[...].astype(F32) + unpack_rows(eb_scr, 0, 2 * heads)
        e_own[...] = e[0:heads].astype(BF16)
        pack_rows(far, 2 * heads, e[heads:])
    elif h == 1:
        core_before, before = given
        first, second = outs[3:]
        core[0:heads, :] = core_before[...]
        core[heads:, :] = g_scr[:, rows : 2 * rows]
        split_rows(jnp.concatenate([before[...].astype(F32), grad], axis=1), first, second)
    else:
        core_before, far0, e_own, arrange = given
        first, second = outs[3:]
        core[0 : 2 * heads, :] = core_before[...]
        core[2 * heads : 3 * heads, :] = g_scr[:, rows : 2 * rows]
        core[3 * heads :, :] = far0[heads : 2 * heads, :]
        e = e_own[...].astype(F32) + unpack_rows(far0, 2 * heads, heads)
        if fast:
            transpose_into(eb_scr, e, spots, slice(None))
            e = eb_scr[...]
        else:
            e = mm(arrange[...], e.astype(BF16), NT)
        split_rows(jnp.concatenate([grad, e], axis=1), first, second)


def attend_back(h, fast, spots, sp, q, kt, k, vt, o, d, cs, tok_t, given, awaits=()):
    rows = kt[0].shape[2]
    total = 4 * rows
    width = tok_t.shape[0]
    heads = 3 * HD
    far = (2 * heads + 3 * heads // 2, 2 * heads, 2 * heads)[h]
    outs = [((heads, rows), BF16), ((far, rows), BF16), (((1, 2, 4)[h] * heads, rows), BF16)]
    if h == 0:
        outs += [((width, heads), BF16), ((heads, width), BF16)]
    else:
        outs += [((width // 2, 2 * heads), BF16)] * 2
    return run(
        functools.partial(attend_back_kernel, h, fast),
        12,
        20,
        (sp, spots),
        (*cs, tok_t, *given),
        outs,
        [
            pltpu.VMEM((128, total), BF16),
            pltpu.VMEM((128, total), BF16),
            pltpu.VMEM((HD, total), BF16),
            pltpu.VMEM((128, total), BF16),
            pltpu.VMEM((total, 128), BF16),
            pltpu.VMEM((128, total), BF16),
            pltpu.VMEM((total, 128), F32),
            pltpu.VMEM((128, total), F32),
            pltpu.VMEM((128, total), F32),
            pltpu.VMEM((heads, total), BF16),
            pltpu.VMEM((3 * heads, rows), BF16) if h == 0 else pltpu.VMEM((width, heads), F32),
            pltpu.SemaphoreType.DMA((25,)),
        ],
        awaits,
        apart=(*q, *kt, *k, *vt, *o, *d),
    )


def norm_parts(h):
    centred = h - jnp.mean(h, axis=-1, keepdims=True)
    inverse = lax.rsqrt(jnp.mean(centred * centred, axis=-1, keepdims=True) + 1e-05)
    return centred * inverse, inverse


def norm_back(grad, normed, inverse, gain):
    scaled = grad * gain
    return inverse * (
        scaled
        - jnp.mean(scaled, axis=-1, keepdims=True)
        - normed * jnp.mean(scaled * normed, axis=-1, keepdims=True)
    )


def sigmoid(v):
    return 0.5 + 0.5 * jnp.tanh(0.5 * v)


def out_kernel(a0, a1, a2, a3, w0, w1, w2, w3, tok_ref, gain_ref, bias_ref, low_ref, xhat_ref, inv_ref, *halves):
    w = jnp.concatenate([w0[...], w1[...], w2[...], w3[...]], axis=0)
    for half in range(2):
        at = slice(half * BLK, (half + 1) * BLK)
        a = jnp.concatenate([a0[:, at], a1[:, at], a2[:, at], a3[:, at]], axis=0)
        normed, inverse = norm_parts(tok_ref[at, :].astype(F32) + mm(a, w, TN))
        xhat_ref[at, :] = normed
        inv_ref[at, :] = jnp.broadcast_to(inverse, (BLK, 128))
        low = (normed * gain_ref[...] + bias_ref[...]).astype(BF16)
        low_ref[at, :] = low
        halves[half][...] = low


def out_project(a, w, tok, gain, bias, awaits=()):
    rows, width = tok.shape
    return run(
        out_kernel,
        3,
        10,
        (),
        (*a, *w, tok, gain, bias),
        (((rows, width), BF16), ((rows, width), F32), ((rows, 128), F32), *[((rows // 2, width), BF16)] * 2),
        awaits=awaits,
    )


PART_PLACES = (
    *((0, n, 0, 2) for n in range(3)),
    (0, 3, 0, 1),
    (0, 3, 1, 1),
    *((1, n, 0, 2) for n in range(4)),
)


def gather_weights(at_ref, parts, wgu, wd, sem):
    copies = []
    for n, (part, (which, quarter, first, count)) in enumerate(zip(parts, PART_PLACES)):
        dst = (wgu, wd)[which]
        half = dst.shape[0] // 8
        spot = pl.multiple_of((at_ref[0] ^ quarter) * (2 * half) + first * half, half)
        src = part.at[pl.ds(0, count * half), :]
        copies.append(pltpu.make_async_copy(src, dst.at[pl.ds(spot, count * half), :], sem.at[n]))
    for c in copies:
        c.start()
    return copies


def mlp_rows(x, wg, wu, down, da, db, hid):
    gate, up = mm(x, wg), mm(x, wu)
    s = sigmoid(gate)
    act = gate * s
    low = (act * up).astype(BF16)
    da[...] = (up * (s + act * (1.0 - s))).astype(BF16)
    db[...] = act.astype(BF16)
    if hid is not None:
        hid[...] = low
    return mm(low, down)


def mlp_own_kernel(half0, half1, ml0, wgu, wd, acc, da, db, hid, ml1, sem):
    rows = ml0.shape[0]
    hidden = wd.shape[0]
    copies = []
    for n, half in enumerate((half0, half1)):
        copies.append(pltpu.make_async_copy(half, ml1.at[pl.ds(n * (rows // 2), rows // 2), :], sem.at[n]))
        copies[-1].start()
    for block, x in enumerate((ml0, ml1)):
        if block:
            for c in copies:
                c.wait()
        at = slice(block * rows, (block + 1) * rows)
        total = None
        for col in range(0, hidden, BLK):
            cols, ups = slice(col, col + BLK), slice(hidden + col, hidden + col + BLK)
            saved = [u.at[at, cols] for u in (da, db, hid)]
            part = mlp_rows(x[...], wgu[:, cols], wgu[:, ups], wd[cols, :], *saved)
            total = part if total is None else total + part
        acc[at, :] = total


def mlp_own(ml0, halves, wgu, wd, awaits=()):
    rows, width = ml0.shape
    hidden = wd.shape[0]
    saved = ((2 * rows, hidden), BF16)
    return run(
        mlp_own_kernel,
        5,
        10,
        (),
        (ml0, wgu, wd),
        [((2 * rows, width), F32)] + [saved] * 3 + [((rows, width), BF16)],
        [pltpu.SemaphoreType.DMA((2,))],
        awaits,
        apart=halves,
    )


def mlp_peer_kernel(at_ref, *refs):
    n_parts = len(PART_PLACES)
    ml0, ml1, acc, own, sib, da, db, wgu, wd, sem = refs[n_parts:]
    rows = ml0.shape[0]
    hidden = da.shape[1]
    for c in gather_weights(at_ref, refs[:n_parts], wgu, wd, sem):
        c.wait()
    for block, x in enumerate((ml0, ml1)):
        at = slice(block * rows, (block + 1) * rows)
        total = acc[at, :]
        for col in range(0, hidden, BLK):
            cols, ups = slice(col, col + BLK), slice(hidden + col, hidden + col + BLK)
            saved = [u.at[at, cols] for u in (da, db)]
            total += mlp_rows(x[...], wgu[:, cols], wgu[:, ups], wd[cols, :], *saved, None)
        if block:
            sib[...] = total.astype(BF16)
        else:
            own[...] = total


def mlp_peer(at, ml0, ml1, acc, parts, awaits=()):
    rows, width = ml0.shape
    hidden = parts[0].shape[1] // 2
    saved = ((2 * rows, hidden), BF16)
    return run(
        mlp_peer_kernel,
        6,
        13,
        (at,),
        (ml0, ml1, acc),
        [((rows, width), F32), ((rows, width), BF16)] + [saved] * 2,
        [pltpu.VMEM((width, 2 * hidden), BF16), pltpu.VMEM((hidden, width), BF16), pltpu.SemaphoreType.DMA((len(parts),))],
        awaits,
        apart=parts,
    )


def copies_of(src, dst, sem, rows=128):
    copies = []
    for n in range(src.shape[0] // rows):
        at = pl.ds(n * rows, rows)
        copies.append(pltpu.make_async_copy(src.at[at, :], dst.at[at, :], sem.at[n]))
        copies[-1].start()
    return copies


def mid_kernel(
    got, xhat_ref, own_ref, go_ref, g1, b1, g2, b2, out_ref, dh_ref, dm_ref, sums_ref, got_ref, sem
):
    gain_sum, bias_sum = 0.0, 0.0
    copies = copies_of(got, got_ref, sem)
    for start in range(0, xhat_ref.shape[0], 128):
        at = slice(start, start + 128)
        copies[start // 128].wait()
        mid = xhat_ref[at, :] * g1[...] + b1[...]
        normed, inverse = norm_parts(mid + (own_ref[at, :] + got_ref[at, :].astype(F32)))
        out_ref[at, :] = (normed * g2[...] + b2[...]).astype(BF16)
        grad = go_ref[at, :].astype(F32)
        dh = norm_back(grad, normed, inverse, g2[...])
        dh_ref[at, :] = dh
        dm_ref[at, :] = dh.astype(BF16)
        gain_sum += jnp.sum(grad * normed, axis=0, keepdims=True)
        bias_sum += jnp.sum(grad, axis=0, keepdims=True)
    sums_ref[0:1, :] = gain_sum
    sums_ref[1:2, :] = bias_sum


def mid_norm(xhat, own, got, out_grad, g1, b1, g2, b2, awaits=()):
    rows, width = xhat.shape
    return run(
        mid_kernel,
        3,
        8,
        (),
        (xhat, own, out_grad, g1, b1, g2, b2),
        (((rows, width), BF16), ((rows, width), F32), ((rows, width), BF16), ((2, width), F32)),
        [pltpu.VMEM((rows, width), BF16), pltpu.SemaphoreType.DMA((rows // 128,))],
        awaits,
        apart=(got,),
    )


def mlp_back_kernel(at_ref, *refs):
    n_parts = len(PART_PLACES)
    dm1_ref, dm0, wgu, wd, da_o, db_o, da_p, db_p, own, sib, dg_o, du_o, wgu_p, wd_p, dm1, sem = refs[n_parts:]
    rows = dm0.shape[0]
    hidden = wd.shape[0]
    first = pltpu.make_async_copy(dm1_ref, dm1, sem.at[n_parts])
    first.start()
    copies = gather_weights(at_ref, refs[:n_parts], wgu_p, wd_p, sem)

    def part_of(x, at, cols, wg, wu, down, da, db, keep):
        dhid = mm(x[...], down, NT)
        dgate = (dhid * da[at, cols].astype(F32)).astype(BF16)
        dup = (dhid * db[at, cols].astype(F32)).astype(BF16)
        if keep:
            dg_o[at, cols] = dgate
            du_o[at, cols] = dup
        return mm(dgate, wg, NT) + mm(dup, wu, NT)

    totals = [None, None]
    for peer, (gu, down, da, db) in enumerate(((wgu, wd, da_o, db_o), (wgu_p, wd_p, da_p, db_p))):
        for block, x in enumerate((dm0, dm1)):
            if block and not peer:
                first.wait()
            at = slice(block * rows, (block + 1) * rows)
            for col in range(0, hidden, BLK):
                cols, ups = slice(col, col + BLK), slice(hidden + col, hidden + col + BLK)
                part = part_of(x, at, cols, gu[:, cols], gu[:, ups], down[cols, :], da, db, not peer)
                totals[block] = part if totals[block] is None else totals[block] + part
        if not peer:
            for c in copies:
                c.wait()
    own[...] = totals[0]
    sib[...] = totals[1].astype(BF16)


def mlp_backward(at, dm0, dm1, wgu, wd, parts, da_o, db_o, da_p, db_p, awaits=()):
    rows, width = dm0.shape
    hidden = wd.shape[0]
    saved = ((2 * rows, hidden), BF16)
    return run(
        mlp_back_kernel,
        11,
        18,
        (at,),
        (dm0, wgu, wd, da_o, db_o, da_p, db_p),
        [((rows, width), F32), ((rows, width), BF16)] + [saved] * 2,
        [
            pltpu.VMEM((width, 2 * hidden), BF16),
            pltpu.VMEM((hidden, width), BF16),
            pltpu.VMEM((rows, width), BF16),
            pltpu.SemaphoreType.DMA((len(parts) + 1,)),
        ],
        awaits,
        apart=(*parts, dm1),
    )


def first_norm_kernel(
    got_ref, dh2, own, xhat, inv, g1, sums2, a0, a1, a2, a3, w0, w1, w2, w3,
    dh1, d0, d1, d2, d3, ea, dat_scr, got, sem,
):
    gain_sum, bias_sum = 0.0, 0.0
    copies = copies_of(got_ref, got, sem)
    for start in range(0, dh2.shape[0], 128):
        at = slice(start, start + 128)
        copies[start // 128].wait()
        dmid = dh2[at, :] + (own[at, :] + got[at, :].astype(F32))
        normed = xhat[at, :]
        gain_sum += jnp.sum(dmid * normed, axis=0, keepdims=True)
        bias_sum += jnp.sum(dmid, axis=0, keepdims=True)
        grad = norm_back(dmid, normed, inv[at, 0:1], g1[...])
        dh1[at, :] = grad
        dat_scr[at, :] = grad.astype(BF16)
    sums = jnp.concatenate([gain_sum, bias_sum, sums2[...]], axis=0)
    high = sums.astype(BF16).astype(F32)
    both = jnp.concatenate([high, sums - high], axis=0)
    rest = jnp.concatenate([both[:, 512:], jnp.zeros((8, dh2.shape[0] - 256), F32)], axis=1)
    tail = jnp.concatenate([both[:, 0:512], rest], axis=0).astype(BF16)
    dat = dat_scr[...]
    for w, d in ((w0, d0), (w1, d1), (w2, d2), (w3, d3)):
        d[0:192, :] = mm(w[...], dat, NT).astype(BF16)
        d[192:208, :] = tail
    ea[...] = mm(jnp.concatenate([a0[...], a2[...]], axis=0), dat).astype(BF16)
    pack_rows(d1, 208, mm(jnp.concatenate([a1[...], a3[...]], axis=0), dat))


def pack_rows(dst, start, value):
    n = value.shape[0]
    rest = value[:, 512:]
    dst[start : start + n, :] = value[:, 0:512].astype(dst.dtype)
    dst[start + n : start + n + n // 2, :] = jnp.concatenate([rest[0 : n // 2], rest[n // 2 :]], axis=1).astype(dst.dtype)


def unpack_rows(src, start, n):
    rest = src[start + n : start + n + n // 2, :].astype(F32)
    rest = jnp.concatenate([rest[:, 0:256], rest[:, 256:]], axis=0)
    return jnp.concatenate([src[start : start + n, :].astype(F32), rest], axis=1)


def first_norm_back(dh2, own, got, xhat, inv, g1, sums2, a, w, awaits=()):
    rows, width = dh2.shape
    heads = a[0].shape[0]
    d = ((heads + 16, rows), BF16)
    return run(
        first_norm_kernel,
        5,
        12,
        (),
        (dh2, own, xhat, inv, g1, sums2, *a, *w),
        [((rows, width), F32), d, ((4 * heads + 16, rows), BF16), d, d, ((2 * heads, width), BF16)],
        [pltpu.VMEM((rows, width), BF16), pltpu.VMEM((rows, width), BF16), pltpu.SemaphoreType.DMA((rows // 128,))],
        awaits,
        apart=(got,),
    )


def far_kernel(
    fast, spots, dm0, dm1, dm2, dm3, ml2, ml3, wgu, wd, hid_o, first, second, dg, du, dmt, hids
):
    rows = dm0.shape[0]
    hidden = wd.shape[0]
    for p, u in enumerate((dm0, dm1, dm2, dm3)):
        transpose_into(dmt, u[...], spots if fast else None, slice(p * rows, (p + 1) * rows))
    for col in range(0, hidden, BLK):
        cols, ups = slice(col, col + BLK), slice(hidden + col, hidden + col + BLK)
        hids[0 : 2 * rows, :] = hid_o[:, cols]
        for block, (x, dm) in enumerate(((ml2, dm2), (ml3, dm3))):
            at = slice(block * rows, (block + 1) * rows)
            gate, up, dhid = mm(x[...], wgu[:, cols]), mm(x[...], wgu[:, ups]), mm(dm[...], wd[cols, :], NT)
            s = sigmoid(gate)
            act = gate * s
            hids[(2 + block) * rows : (3 + block) * rows, :] = (act * up).astype(BF16)
            dg[at, cols] = (dhid * (up * (s + act * (1.0 - s)))).astype(BF16)
            du[at, cols] = (dhid * act).astype(BF16)
        split_rows(mm(dmt[...], hids[...]), first.at[:, cols], second.at[:, cols])


def far_rows(fast, spots, dm, ml, wgu, wd, hid, awaits=(), carry=()):
    rows, width = dm[0].shape
    hidden = wd.shape[0]
    return run(
        functools.partial(far_kernel, fast),
        8,
        14,
        (spots,),
        (*dm, *ml, wgu, wd, hid),
        [((width // 2, hidden), BF16)] * 2 + [((2 * rows, hidden), BF16)] * 2,
        [pltpu.VMEM((width, 4 * rows), BF16), pltpu.VMEM((4 * rows, BLK), BF16)],
        awaits,
        carry,
    )


def weight_kernel(
    fast, spots, spots_d, d0, d1, d2, d3, ml0, ml1, ml2, ml3, dg, du, dg_f, du_f,
    g_first, g_second, u_first, u_second, total, mlt, mlt_d, tail_scr, sem,
):
    rows = ml0.shape[0]
    copies = [
        pltpu.make_async_copy(d.at[pl.ds(3 * HD, 16), :], tail_scr.at[p], sem.at[p]) for p, d in enumerate((d0, d1, d2, d3))
    ]
    for c in copies:
        c.start()
    for p, u in enumerate((ml0, ml1, ml2, ml3)):
        cols = slice(p * rows, (p + 1) * rows)
        transpose_into(mlt, u[...], spots if fast else None, cols)
        transpose_into(mlt_d, u[...], spots_d if fast else None, cols)
    for turned, near, far, first, second in (
        (mlt, dg, dg_f, g_first, g_second),
        (mlt_d, du, du_f, u_first, u_second),
    ):
        split_rows(mm(turned[:, 0 : 2 * rows], near[...]) + mm(turned[:, 2 * rows :], far[...]), first, second)
    for c in copies:
        c.wait()
    sums = [tail_scr[p].astype(F32) for p in range(4)]
    joined = (sums[0] + sums[1]) + (sums[2] + sums[3])
    total[:, 0:512] = joined[0:4] + joined[4:8]
    total[:, 512:768] = (joined[8:12] + joined[12:16])[:, 0:256]


def weight_grads(fast, spots, spots_d, d, ml, near, far, awaits=()):
    rows, width = ml[0].shape
    hidden = near[0].shape[1]
    return run(
        functools.partial(weight_kernel, fast),
        6,
        16,
        (spots, spots_d),
        (*ml, *near, *far),
        [((width // 2, hidden), BF16)] * 4 + [((4, width), F32)],
        [
            *[pltpu.VMEM((width, 4 * rows), BF16)] * 2,
            pltpu.VMEM((4, 16, rows), BF16),
            pltpu.SemaphoreType.DMA((4,)),
        ],
        awaits,
        apart=d,
    )


def join_kernel(core, got1, got2, out, sem):
    heads = 3 * HD
    pieces = ((core, 0, 4 * heads), (got1, heads, heads), (got2, heads, heads))
    copies, at = [], 0
    for n, (src, start, count) in enumerate(pieces):
        copies.append(pltpu.make_async_copy(src.at[pl.ds(start, count), :], out.at[pl.ds(at, count), :], sem.at[n]))
        copies[-1].start()
        at += count
    for c in copies:
        c.wait()


def join(core, got1, got2):
    return run(
        join_kernel,
        1,
        4,
        (),
        (),
        [((18 * HD, core.shape[1]), BF16)],
        [pltpu.SemaphoreType.DMA((3,))],
        apart=(core, got1, got2),
    )[0]


def by_heads(w):
    heads = 3 * HD
    return jnp.concatenate([w[c * heads + h * HD : c * heads + (h + 1) * HD, :] for h in range(3) for c in range(3)], axis=0)


def near_kernel(f0, f1, f2, dh1, n0, n1, n2, w0, w2, out, far, sem):
    heads = 3 * HD
    copies = []
    for n, f in enumerate((f0, f1, f2)):
        spot = pl.ds(n * heads, heads)
        copies.append(pltpu.make_async_copy(f.at[pl.ds(0, heads), :], far.at[spot, :], sem.at[n]))
        copies[-1].start()
    near = jnp.concatenate([n0[...], n1[...], n2[...]], axis=0)
    out[...] = dh1[...] + mm(near, by_heads(w0), TN)
    for c in copies:
        c.wait()
    out[...] += mm(far[...], by_heads(w2), TN)


def input_near(dh1, near, far, w0, w2):
    return run(
        near_kernel,
        3,
        12,
        (),
        (dh1, *near, w0, w2),
        [(dh1.shape, F32)],
        [pltpu.VMEM((9 * HD, dh1.shape[0]), BF16), pltpu.SemaphoreType.DMA((3,))],
        apart=far,
    )[0]


def input_kernel(core_ref, before, w1, w3, out, core, total, sem):
    arrival = pltpu.make_async_copy(core_ref, core, sem.at[0])
    arrival.start()
    w = jnp.concatenate([by_heads(w1), by_heads(w3)], axis=0)
    arrival.wait()
    copies = []
    for half in range(before.shape[0] // BLK):
        at = slice(half * BLK, (half + 1) * BLK)
        total[at, :] = before[at, :] + mm(core[:, at], w, TN)
        spot = pl.ds(half * BLK, BLK)
        copies.append(pltpu.make_async_copy(total.at[spot, :], out.at[spot, :], sem.at[1 + half]))
        copies[-1].start()
    for c in copies:
        c.wait()


def input_back(before, core, w1, w3):
    return run(
        input_kernel,
        3,
        14,
        (),
        (before, w1, w3),
        [(before.shape, F32)],
        [
            pltpu.VMEM(core.shape, BF16),
            pltpu.VMEM(before.shape, F32),
            pltpu.SemaphoreType.DMA((1 + before.shape[0] // BLK,)),
        ],
        apart=(core,),
        hbm=(0,),
    )[0]


def swap(v, bit, axis="tensor"):
    n = lax.axis_size(axis)
    return lax.ppermute(v, axis, [(i, i ^ bit) for i in range(n)])


def bits_of(n):
    return n.bit_length() - 1


def spots_of(order, n):
    block = jnp.arange(n, dtype=jnp.int32) ^ lax.axis_index("dp")
    spot = jnp.zeros((n,), jnp.int32)
    for s, bit in enumerate(order):
        spot = spot + (((block >> bit) & 1) << (len(order) - 1 - s))
    return spot


def last_kernel(chains, kind, *refs):
    count = sum(chains)
    parts, outs, scrs, sem = refs[:count], refs[count:-count - 1], refs[-count - 1 : -1], refs[-1]
    copies = []
    for n, (part, scr) in enumerate(zip(parts, scrs)):
        copies.append(pltpu.make_async_copy(part.at[pl.ds(0, scr.shape[0]), :], scr, sem.at[n]))
        copies[-1].start()
    for c in copies:
        c.wait()
    sums, at = [], 0
    for length in chains:
        sums.append(sum(scr[...].astype(F32) for scr in scrs[at : at + length]))
        at += length
    if kind == "mlp":
        gu, down = outs
        width = down.shape[1]
        if len(sums) > 3:
            sums = [u + sums[3][:, n * width : (n + 1) * width] for n, u in enumerate(sums[0:3])]
        gu[:, 0, :] = sums[0]
        gu[:, 1, :] = sums[1]
        down[...] = sums[2]
    else:
        qkv, out = outs
        total = jnp.concatenate(sums, axis=1)
        for c in range(3):
            qkv[c] = jnp.concatenate([total[:, (3 * h + c) * HD : (3 * h + c + 1) * HD] for h in range(3)], axis=1)
        out[...] = total[:, 9 * HD :].T


def last_sums(kind, rows, chains, outs):
    parts = [part for chain in chains for part in chain]
    return run(
        functools.partial(last_kernel, [len(chain) for chain in chains], kind),
        2,
        8,
        (),
        (),
        outs,
        [pltpu.VMEM((rows, part.shape[1]), BF16) for part in parts] + [pltpu.SemaphoreType.DMA((len(parts),))],
        apart=parts,
    )


class scatter_steps:
    def __init__(self, first, second, order):
        self.first, self.parts, self.order, self.step = first, [first], order, 0
        self.sent = second

    def advance(self):
        self.parts.append(swap(self.sent, 1 << self.order[self.step], "dp"))
        self.step += 1
        self.next_sent()
        return self.parts[-1]

    def next_sent(self):
        if self.step < len(self.order):
            length = self.parts[-1].shape[0]
            self.sent = sum(u[length // 2 : length].astype(F32) for u in self.parts).astype(BF16)

    def all_parts(self):
        while self.step < len(self.order):
            self.advance()
        return self.parts


def advance_together(chains):
    bits = {chain.order[chain.step] for chain in chains}
    if len(bits) > 1 or any(chain.step < len(chain.order) - 1 for chain in chains):
        return None
    for chain in chains:
        chain.step += 1
    return swap(jnp.concatenate([chain.sent for chain in chains], axis=1), 1 << bits.pop(), "dp")


def first_sums(chains, rows):
    return [sum(part[0:rows].astype(F32) for part in chain) for chain in chains]


def quarter_of(w):
    rows = w.shape[0] // 4
    return lax.dynamic_slice_in_dim(w, (lax.axis_index("dp") % 4) * rows, rows, axis=0)


def local(
    tokens,
    doc_lengths,
    key_mask,
    qkv_weight,
    out_weight,
    gate_up_weight,
    down_weight,
    norm1_gain,
    norm1_bias,
    norm2_gain,
    norm2_bias,
    out_grad,
):
    rows, width = tokens.shape
    flags = jnp.pad(key_mask.astype(BF16).reshape(1, rows), ((0, EXTRA - 1), (0, width - rows)))
    tok0 = jnp.concatenate([tokens, flags], axis=0)
    tok1 = swap(tok0, 1)
    tok2 = swap(tok0, 2)
    sp = jnp.concatenate([doc_lengths[0], lax.axis_index("tensor").reshape(1)]).astype(jnp.int32)
    quarter = (lax.axis_index("dp") % 4).reshape(1).astype(jnp.int32)
    freqs = 1000.0 ** (-(jnp.arange(HD // 2, dtype=F32) * 2.0 / HD))
    freqs = jnp.broadcast_to(freqs[:, None], (HD // 2, 128))
    wt = jnp.transpose(qkv_weight, (1, 2, 0)).reshape(-1, width)

    n_dp = lax.axis_size("dp")
    fast = (width // n_dp) % 16 == 0
    order = list(range(bits_of(n_dp)))
    order_d = order[1:2] + order[0:1] + order[2:]
    spots, spots_d = spots_of(order, n_dp), spots_of(order_d, n_dp)

    def arranged(v, at):
        if fast:
            return v
        blocks = v.reshape(v.shape[0], n_dp, width // n_dp)
        return jnp.take(blocks, jnp.argsort(at), axis=1).reshape(v.shape)

    ORDER.last = ()
    wo0 = out_weight
    wo1, wt1 = swap(wo0, 1), swap(wt, 1)
    wgu = gate_up_weight.reshape(width, -1)
    part_a = jnp.concatenate([quarter_of(down_weight), quarter_of(out_weight)], axis=0)
    part_b = quarter_of(wgu)
    pa0 = swap(part_a, 2)

    proj = [project(0, sp, freqs, tok0, wt), project(1, sp, freqs, tok1, wt, awaits=(part_a, part_b, wt1))]
    (tok2,) = gate(tok2)
    tok3 = swap(tok2, 1)
    tok = (tok0, tok1, tok2, tok3)
    *more, part_b = project(2, sp, freqs, tok2, wt, carry=(part_b,))
    proj.append(more)
    pb0 = swap(part_b, 2)
    proj.append(project(3, sp, freqs, tok3, wt))
    qt, kt, k, vt, cs = zip(*proj)
    o2, o3, q2, q3 = attend(1, sp, qt, k, vt, (wo1,))
    o2, pa0 = gate(o2, pa0)
    pa1, pa2, pa3 = swap(pa0, 1, "dp"), swap(pa0, 2, "dp"), swap(pa0, 3, "dp")
    g2 = swap(o2, 2)
    o0, o1, q0, q1 = attend(0, sp, qt, k, vt)
    o1, o3 = gate(o1, o3, awaits=(pb0,))
    g3 = swap(o3, 3)
    tok_t = transposed(fast, spots, [arranged(u, spots) for u in tok], rows)
    (o1,) = gate(o1, awaits=(g2,))
    g1 = swap(o1, 1)
    wo2 = together(quarter, (pa0, pa1, pa2, pa3), wo0.shape, (g3, g1))
    wo2, pb0 = gate(wo2, pb0)
    wo3 = swap(wo2, 1)
    pb1, pb2 = swap(pb0, 1, "dp"), swap(pb0, 2, "dp")
    wo = (wo0, wo1, wo2, wo3)

    gain1, bias1, gain2, bias2 = (u.reshape(1, width) for u in (norm1_gain, norm1_bias, norm2_gain, norm2_bias))
    ml0, xhat1, inv1, *halves = out_project((o0, g1, g2, g3), wo, tokens, gain1, bias1)
    acc, da_o, db_o, hid_o, ml1 = mlp_own(ml0, [swap(u, 1) for u in halves], wgu, down_weight)
    (ml0,) = gate(ml0)
    ml2 = swap(ml0, 2)
    kept = park((*kt, *k, *vt, q0, q1, q2, q3, tok_t))
    kt, k, vt, (q0, q1, q2, q3, tok_t) = kept[0:4], kept[4:8], kept[8:12], kept[12:17]
    half2, half1 = park((), ((pb2, 0), (pb1, 1)))
    parts = (pb0, pb1, pb2, swap(half2, 1, "dp"), swap(half1, 2, "dp"), pa0, pa1, pa2, pa3)
    own, sib, da_p, db_p = mlp_peer(quarter, ml0, ml1, acc, parts)
    (sib,) = gate(sib, awaits=(ml2,))
    output, dh2, dm0, sums2 = mid_norm(xhat1, own, swap(sib, 1), out_grad, gain1, bias1, gain2, bias2)
    dm0, ml2 = gate(dm0, ml2)
    dm1, dm2 = swap(dm0, 1), swap(dm0, 2)
    ml3 = swap(ml2, 1)
    own, sib, dg_o, du_o = mlp_backward(quarter, dm0, dm1, wgu, down_weight, parts, da_o, db_o, da_p, db_p)
    (sib,) = gate(sib, awaits=(ml3,))
    dh1, d0, d1, d2, d3, ea = first_norm_back(
        dh2, own, swap(sib, 1), xhat1, inv1, gain1, sums2, (o0, g1, g2, g3), wo, (dm2,)
    )
    d1, d2, d3 = gate(d1, d2, d3)
    dm3 = swap(dm2, 1)
    d = (d0, swap(d1, 1), swap(d2, 2), swap(d3, 3))
    ml = [arranged(u, spots) for u in (ml0, ml1, ml2, ml3)]
    dm = [arranged(u, spots_d) for u in (dm0, dm1, dm2, dm3)]
    d_first, d_second, dg_f, du_f = far_rows(fast, spots_d, dm, ml[2:], wgu, down_weight, hid_o)
    d_second, wt = gate(d_second, wt, awaits=d[1:])
    dn = scatter_steps(d_first, d_second, order_d)
    dn1 = dn.advance()
    wt2 = swap(wt, 2)
    g_first, g_second, u_first, u_second, sums = weight_grads(
        fast, spots, spots_d, d, ml, (dg_o, du_o), (dg_f, du_f)
    )
    g_second, u_second, sums, dn.parts[-1] = gate(g_second, u_second, sums, dn1)
    dn.next_sent()
    dn2 = dn.advance()
    sums_got = swap(sums, 2, "dp")
    gg, gu = scatter_steps(g_first, g_second, order), scatter_steps(u_first, u_second, order_d)
    gg1, gu1 = gg.advance(), gu.advance()

    arrange = jnp.zeros((8, 128), BF16)
    if not fast:
        column = jnp.arange(width)
        target = spots[column // (width // n_dp)] * (width // n_dp) + column % (width // n_dp)
        arrange = (column[:, None] == target[None, :]).astype(BF16)
    back = functools.partial(
        attend_back,
        fast=fast,
        spots=spots,
        sp=sp,
        q=(q0, q1, q2, q3),
        kt=kt,
        k=k,
        vt=vt,
        o=(o0, o1, o2, o3),
        d=d,
        cs=cs,
        tok_t=tok_t,
    )
    near0, far0, core0, grad0, e_own = back(0, given=(ea,))
    far0, dn.parts[-1], gg.parts[-1], gu.parts[-1], wt2, sums_got = gate(far0, dn2, gg1, gu1, wt2, sums_got)
    for chain in (dn, gg, gu):
        chain.next_sent()
    got0, gg2, gu2 = swap(far0, 2), gg.advance(), gu.advance()
    wt3 = swap(wt2, 1)
    sums = sums + sums_got
    sums_got = swap(sums, 4, "dp") if n_dp > 4 else sums_got
    near1, far1, core1, first, second = back(1, given=(core0, grad0))
    far1, second, gg.parts[-1], gu.parts[-1], sums_got = gate(far1, second, gg2, gu2, sums_got, awaits=(wt3,))
    for chain in (gg, gu):
        chain.next_sent()
    c1 = scatter_steps(first, second, order)
    c1_got, mlp3 = c1.advance(), advance_together((gg, gu, dn))
    got1 = swap(far1, 2)
    sums = sums + sums_got
    sums_got = swap(sums, 1, "dp")
    near2, far2, core2, first, second = back(2, given=(core1, got0, e_own, arrange))
    far2, second, c1.parts[-1], sums_got = gate(far2, second, c1_got, sums_got, awaits=(got1,) if mlp3 is None else (got1, mlp3))
    c1.next_sent()
    sums = sums + sums_got
    bit = 8
    while bit < n_dp:
        sums = sums + swap(sums, bit, "dp")
        bit *= 2
    c2 = scatter_steps(first, second, order)
    c2_got, c1_got, got2 = c2.advance(), c1.advance(), swap(far2, 2)
    c2.parts[-1], c1.parts[-1] = gate(c2_got, c1_got)
    c2.next_sent()
    c1.next_sent()
    c2_got, c1_got = c2.advance(), c1.advance()
    core = swap(join(core2, got1, got2), 1)
    input_grad = input_near(dh1, (near0, near1, near2), (got0, got1, got2), wt, wt2)
    c2.parts[-1], c1.parts[-1] = gate(c2_got, c1_got)
    c2.next_sent()
    c1.next_sent()
    mlp = [chain.all_parts() for chain in (gg, gu, dn)]
    attention = (c1.all_parts(), c2.all_parts())
    if mlp3 is not None:
        mlp.append([mlp3])
    shard = width // n_dp
    if fast:
        hidden = down_weight.shape[0]
        gu_part, down_part = last_sums("mlp", shard, mlp, [((shard, 2, hidden), F32), ((shard, hidden), F32)])
        input_grad = input_back(input_grad, core, wt1, wt3)
        qkv_part, out_part = last_sums(
            "attention", shard, attention, [((3, shard, 3 * HD), F32), ((3 * HD, shard), F32)]
        )
        qkv_part = jnp.transpose(qkv_part, (1, 0, 2))
    else:
        input_grad = input_back(input_grad, core, wt1, wt3)
        gg, gu, down_part = first_sums(mlp, shard)
        gu_part = jnp.stack([gg, gu], axis=1)
        total = jnp.concatenate(first_sums(attention, shard), axis=1)
        out_part = total[:, 9 * HD :].T
        qkv_part = jnp.transpose(total[:, 0 : 9 * HD].reshape(shard, 3, 3, HD), (0, 2, 1, 3)).reshape(shard, 3, 3 * HD)
    return (
        output,
        input_grad,
        qkv_part,
        out_part,
        gu_part,
        down_part.T,
        sums[0],
        sums[1],
        sums[2],
        sums[3],
    )


def solution(mesh):
    placed = (
        P(("dp", "tensor"), None),
        P("dp", None),
        P(("dp", "tensor")),
        P(None, None, "tensor"),
        P("tensor", None),
        P(None, None, "tensor"),
        P("tensor", None),
        P(),
        P(),
        P(),
        P(),
        P(("dp", "tensor"), None),
    )
    return jax.shard_map(
        local,
        mesh=mesh,
        in_specs=placed,
        out_specs=(
            P(("dp", "tensor"), None),
            P(("dp", "tensor"), None),
            P("dp", None, "tensor"),
            P("tensor", "dp"),
            P("dp", None, "tensor"),
            P("tensor", "dp"),
            P(),
            P(),
            P(),
            P(),
        ),
        check_vma=False,
    )
```

```python
import functools

import jax
import jax.numpy as jnp
from jax import lax
from jax.experimental import pallas as pl
from jax.experimental.pallas import tpu as pltpu
from jax.sharding import PartitionSpec as P

HD = 64
F32 = jnp.float32
BF16 = jnp.bfloat16
BIG = -1e30
BLK = 256
WINDOWS = (640, 1664, 2048)
SCALE = 0.15
EXTRA = 16
NN = (((1,), (0,)), ((), ()))
NT = (((1,), (1,)), ((), ()))
TN = (((0,), (0,)), ((), ()))


def mm(a, b, dims=NN):
    return lax.dot_general(a, b, dims, preferred_element_type=F32)


class Order:
    def __init__(self):
        self.last = ()


ORDER = Order()


def run(kernel, us, mib, scalars, args, outs, scratch=(), awaits=(), carry=(), apart=(), hbm=()):
    in_vmem = pl.BlockSpec(memory_space=pltpu.VMEM)
    anywhere = pl.BlockSpec(memory_space=pl.ANY)
    awaits = (*awaits, *ORDER.last)
    n_in = len(scalars) + len(apart) + len(args)
    n_skip, n_out = len(awaits) + len(carry), len(outs)

    def body(*refs):
        rest = refs[n_in + n_skip :]
        kernel(*refs[:n_in], *rest[:n_out], *rest[n_out + len(carry) :])

    results = pl.pallas_call(
        body,
        in_specs=[pl.BlockSpec(memory_space=pltpu.SMEM)] * len(scalars)
        + [anywhere] * len(apart)
        + [in_vmem] * len(args)
        + [anywhere] * n_skip,
        out_specs=[pl.BlockSpec(memory_space=pltpu.HBM) if n in hbm else in_vmem for n in range(n_out)]
        + [anywhere] * len(carry),
        out_shape=[jax.ShapeDtypeStruct(*o) for o in outs] + [jax.ShapeDtypeStruct(c.shape, c.dtype) for c in carry],
        scratch_shapes=list(scratch),
        input_output_aliases={n_in + len(awaits) + i: n_out + i for i in range(len(carry))},
        compiler_params=pltpu.CompilerParams(vmem_limit_bytes=mib << 20),
        cost_estimate=pl.CostEstimate(flops=int(us * SCALE * 1.1e9), bytes_accessed=1 << 18, transcendentals=0),
    )(*scalars, *apart, *args, *awaits, *carry)
    ORDER.last = (min(results[:n_out], key=lambda r: r.size),)
    return results


def gate_kernel(out):
    out[...] = jnp.zeros(out.shape, F32)


def gate(*arrays, awaits=()):
    return run(gate_kernel, 0.1, 4, (), (), [((8, 128), F32)], awaits=awaits, carry=arrays)[1:]


def park_kernel(places, *refs):
    count = len(places)
    copies = []
    for n, (first, rows) in enumerate(places):
        src = refs[n] if rows is None else refs[n].at[pl.ds(first, rows), :]
        copies.append(pltpu.make_async_copy(src, refs[count + n], refs[-1].at[n]))
        copies[-1].start()
    for c in copies:
        c.wait()


def park(arrays, halves=()):
    places = [(0, None) for _ in arrays] + [(n * (u.shape[0] // 2), u.shape[0] // 2) for u, n in halves]
    outs = [(u.shape, u.dtype) for u in arrays] + [((u.shape[0] // 2, u.shape[1]), u.dtype) for u, n in halves]
    return run(
        functools.partial(park_kernel, places),
        3,
        4,
        (),
        (),
        outs,
        [pltpu.SemaphoreType.DMA((len(outs),))],
        apart=(*arrays, *[u for u, n in halves]),
        hbm=range(len(outs)),
    )


def split3(v):
    top = v.astype(BF16).astype(F32)
    rest = v - top
    middle = rest.astype(BF16).astype(F32)
    return top, middle, rest - middle


def split_rows(value, first, second):
    half = first.shape[0]
    first[...] = value[0:half].astype(first.dtype)
    second[...] = value[half:].astype(second.dtype)


def transpose_into(dst, value, spots, cols):
    turned = value.T
    if spots is None:
        dst[:, cols] = turned
        return
    count = spots.shape[0]
    rows = turned.shape[0] // count
    for b in range(count):
        dst[pl.ds(pl.multiple_of(spots[b] * rows, rows), rows), cols] = turned[b * rows : (b + 1) * rows]


def transpose_kernel(fast, *refs):
    count = (len(refs) - 4) // 2
    spots, tokens, outs = refs[:count], refs[count : count + 4], refs[count + 4 :]
    rows = outs[0].shape[1] // 4
    for p, t in enumerate(tokens):
        for spot, out in zip(spots, outs):
            transpose_into(out, t[0:rows, :], spot if fast else None, slice(p * rows, (p + 1) * rows))


def transposed(fast, spots, pieces, rows):
    width = pieces[0].shape[1]
    outs = [((width, 4 * rows), BF16)] * len(spots)
    return run(functools.partial(transpose_kernel, fast), 2, 8, spots, pieces, outs)


def project_kernel(piece, sp_ref, freq_ref, tok_ref, w_ref, qt_ref, kt_ref, k_ref, vt_ref, cs_ref):
    n = tok_ref.shape[0] - EXTRA
    place = (sp_ref[8] ^ piece) * n + lax.broadcasted_iota(jnp.int32, (1, n), 1)
    seg = jnp.zeros((1, n), jnp.int32)
    pos = place
    end = 0
    for d in range(8):
        length = sp_ref[d]
        end = end + length
        past = place >= end
        seg += past.astype(jnp.int32)
        pos -= jnp.where(past, length, 0)
    angles = pos.astype(F32) * freq_ref[:, 0:1]
    cosine, sine = jnp.cos(angles), jnp.sin(angles)
    cs_ref[0:32, :] = cosine
    cs_ref[32:64, :] = sine
    idx = lax.broadcasted_iota(jnp.int32, (64, n), 0)
    which = jnp.where(idx < 19, idx - 8, idx - 19)
    bit = (jnp.broadcast_to(place, (64, n)) >> jnp.clip(which, 0, 10)) & 1
    flipped = jnp.where(idx < 19, bit, 1 - bit).astype(F32)
    same = (idx == seg).astype(F32)
    coded = (idx >= 8) & (idx < 30)
    invalid = 1.0 - tok_ref[n : n + EXTRA, 0:n].astype(F32)[0:1]
    q_tail = jnp.where(idx < 8, BIG * (1.0 - same), jnp.where(coded, BIG * flipped, 0.0))
    k_tail = jnp.where(idx < 8, same, jnp.where(coded, invalid * (1.0 - flipped), 0.0))
    k_tail = jnp.where((idx >= 32) & (idx < 35), 1.0, k_tail)
    v_tail = jnp.where(idx < 3, 1.0, 0.0)
    y = mm(w_ref[...], tok_ref[0:n, :], NT)

    def rotated(at):
        a, b = y[at : at + 32], y[at + 32 : at + 64]
        return jnp.concatenate([a * cosine - b * sine, b * cosine + a * sine], axis=0)

    for h in range(3):
        qt_ref[h] = jnp.concatenate([rotated(h * HD) * 0.125, q_tail], axis=0).astype(BF16)
        key = jnp.concatenate([rotated(192 + h * HD), k_tail], axis=0)
        kt_ref[h] = key.astype(BF16)
        k_ref[h] = key.T.astype(BF16)
        vt_ref[h] = jnp.concatenate([y[384 + h * HD : 448 + h * HD], v_tail], axis=0).astype(BF16)


def project(piece, sp, freqs, tok, w, awaits=(), carry=()):
    rows = tok.shape[0] - EXTRA
    wide, tall = ((3, 128, rows), BF16), ((3, rows, 128), BF16)
    return run(
        functools.partial(project_kernel, piece),
        2.5,
        10,
        (sp,),
        (freqs, tok, w),
        (wide, wide, tall, wide, ((HD, rows), F32)),
        awaits=awaits,
        carry=carry,
    )


def window_of(sp_ref, block, total):
    a = block * BLK
    b = a + BLK - 1
    first, last, end = 0, 0, 0
    for d in range(8):
        begin, end = end, end + sp_ref[d]
        first = jnp.where(begin <= a, begin, first)
        last = jnp.where(begin <= b, end, last)
    start = (first // 128) * 128
    kind = jnp.where(last - start <= WINDOWS[0], 0, jnp.where(last - start <= WINDOWS[1], 1, 2))
    size = jnp.where(kind == 0, WINDOWS[0], jnp.where(kind == 1, WINDOWS[1], WINDOWS[2]))
    return pl.multiple_of(jnp.minimum(start, total - size), 128), kind


def place_of(sp_ref, piece, rows):
    return pl.ds(pl.multiple_of((sp_ref[8] ^ piece) * rows, rows), rows)


def attend_kernel(base, sp_ref, qa, qb, k0, k1, k2, k3, v0, v1, v2, v3, oa, ob, ba, bb, k_scr, v_scr, s_scr, q_scr, o_scr):
    rows = qa.shape[2]
    total = 4 * rows
    for p, (k, v) in enumerate(((k0, v0), (k1, v1), (k2, v2), (k3, v3))):
        at = place_of(sp_ref, p, rows)
        k_scr[:, at, :] = k[...]
        v_scr[:, :, at] = v[...]
    for n in range(4):
        q_scr[n] = (qa, qb)[n // 2][:, :, (n % 2) * BLK : (n % 2 + 1) * BLK]

    def q_block(i, carry):
        start, kind = window_of(sp_ref, (base + i) ^ (2 * sp_ref[8]), total)

        def scores(h, size):
            s = mm(k_scr[h, pl.ds(start, size), :], q_scr[i, h])
            s_scr[h, 0:size, :] = s
            return jnp.max(s, axis=0, keepdims=True)

        def weigh(h, size, top):
            p = jnp.exp(s_scr[h, 0:size, :] - top).astype(BF16)
            acc = mm(v_scr[h, :, pl.ds(start, size)], p)
            norm = acc[64:65]
            o_scr[i, h * HD : (h + 1) * HD, :] = (acc[0:64] / norm).astype(BF16)
            parts = split3(-(top + jnp.log(norm)))
            q_scr[i, h, 96:112, :] = jnp.concatenate([*parts, jnp.zeros((13, BLK), F32)], axis=0).astype(BF16)

        for mode, size in enumerate(WINDOWS):

            @pl.when(kind == mode)
            def _():
                t0 = scores(0, size)
                t1 = scores(1, size)
                weigh(0, size, t0)
                t2 = scores(2, size)
                weigh(1, size, t1)
                weigh(2, size, t2)

        return carry

    lax.fori_loop(0, 4, q_block, 0)
    for n in range(4):
        at = slice((n % 2) * BLK, (n % 2 + 1) * BLK)
        (oa, ob)[n // 2][:, at] = o_scr[n]
        (ba, bb)[n // 2][:, :, at] = q_scr[n]


def attend(half, sp, qt, k, vt, awaits=(), carry=()):
    rows = qt[0].shape[2]
    total = 4 * rows
    out, back = ((3 * HD, rows), BF16), ((3, 128, rows), BF16)
    return run(
        functools.partial(attend_kernel, half * 4),
        8,
        18,
        (sp,),
        (qt[2 * half], qt[2 * half + 1], *k, *vt),
        (out, out, back, back),
        [
            pltpu.VMEM((3, total, 128), BF16),
            pltpu.VMEM((3, 128, total), BF16),
            pltpu.VMEM((3, total, BLK), F32),
            pltpu.VMEM((4, 3, 128, BLK), BF16),
            pltpu.VMEM((4, 3 * HD, BLK), BF16),
        ],
        awaits,
        carry,
    )


def attend_back_kernel(h, fast, sp_ref, spots, *refs):
    q_refs, kt_refs, k_refs, vt_refs, o_refs, d_refs = (refs[4 * n : 4 * n + 4] for n in range(6))
    n_given = (1, 2, 4)[h]
    cs_refs, tok_t, given, outs = refs[24:28], refs[28], refs[29 : 29 + n_given], refs[29 + n_given : -12]
    q_scr, do_scr, o_scr, kt_scr, k_scr, vt_scr, dq_scr, dk_scr, dv_scr, g_scr, eb_scr, sem = refs[-12:]
    rows = kt_refs[0].shape[2]
    total = 4 * rows
    head = pl.ds(h * HD, HD)
    copies = []
    for p in range(4):
        spot, at = place_of(sp_ref, p, rows), pl.ds(p * rows, rows)
        copies += [
            (kt_refs[p].at[h], kt_scr.at[:, spot]),
            (k_refs[p].at[h], k_scr.at[spot, :]),
            (vt_refs[p].at[h], vt_scr.at[:, spot]),
            (q_refs[p].at[h], q_scr.at[:, at]),
            (d_refs[p].at[head, :], do_scr.at[pl.ds(0, HD), at]),
            (o_refs[p].at[head, :], o_scr.at[:, at]),
        ]
    if h == 0:
        copies.append((d_refs[1].at[pl.ds(208, 576), :], eb_scr))
    copies = [pltpu.make_async_copy(src, dst, sem.at[n]) for n, (src, dst) in enumerate(copies)]
    for c in copies:
        c.start()
    dk_scr[...] = jnp.zeros(dk_scr.shape, F32)
    dv_scr[...] = jnp.zeros(dv_scr.shape, F32)
    for c in copies:
        c.wait()
    do_scr[64:128, :] = jnp.zeros((64, total), BF16)
    delta = jnp.sum(do_scr[0:64, :].astype(F32) * o_scr[...].astype(F32), axis=0, keepdims=True)
    do_scr[64:80, :] = jnp.concatenate([*split3(-delta), jnp.zeros((13, total), F32)], axis=0).astype(BF16)

    def q_block(i, carry):
        start, kind = window_of(sp_ref, i ^ (2 * sp_ref[8]), total)
        here = pl.ds(pl.multiple_of(i * BLK, BLK), BLK)
        for mode, size in enumerate(WINDOWS):

            @pl.when(kind == mode)
            def _():
                qt, dot = q_scr[:, here], do_scr[:, here]
                q, do = qt.astype(F32).T.astype(BF16), dot.astype(F32).T.astype(BF16)
                win = pl.ds(start, size)
                p = jnp.exp(mm(q, kt_scr[:, win]))
                ds = (p * mm(do, vt_scr[:, win])).astype(BF16)
                dv_scr[:, win] += mm(dot, p.astype(BF16))
                dk_scr[:, win] += mm(qt, ds)
                dq_scr[here, :] = mm(ds, k_scr[win, :])

        return carry

    lax.fori_loop(0, 8, q_block, 0)

    def unrotated(g, cosine, sine):
        g = g.astype(BF16).astype(F32)
        a, b = g[0:32], g[32:64]
        return jnp.concatenate([a * cosine + b * sine, b * cosine - a * sine], axis=0).astype(BF16)

    for p in range(4):
        at = slice(p * rows, (p + 1) * rows)
        cosine, sine = cs_refs[p][0:32, :], cs_refs[p][32:64, :]
        src = place_of(sp_ref, p, rows)
        g_scr[0:64, at] = unrotated(dq_scr[at, :].T[0:64] * 0.125, cosine, sine)
        g_scr[64:128, at] = unrotated(dk_scr[0:64, src], cosine, sine)
        g_scr[128:192, at] = dv_scr[0:64, src].astype(BF16)
    grad = mm(tok_t[...], g_scr[...], NT)
    heads = 3 * HD
    near, far, core = outs[0:3]
    near[...] = g_scr[:, 0:rows]
    far[0:heads, :] = g_scr[:, 2 * rows : 3 * rows]
    far[heads : 2 * heads, :] = g_scr[:, 3 * rows :]
    if h == 0:
        (ea,) = given
        grad_out, e_own = outs[3:]
        core[...] = g_scr[:, rows : 2 * rows]
        grad_out[...] = grad.astype(BF16)
        e = ea[...].astype(F32) + unpack_rows(eb_scr, 0, 2 * heads)
        e_own[...] = e[0:heads].astype(BF16)
        pack_rows(far, 2 * heads, e[heads:])
    elif h == 1:
        core_before, before = given
        first, second = outs[3:]
        core[0:heads, :] = core_before[...]
        core[heads:, :] = g_scr[:, rows : 2 * rows]
        split_rows(jnp.concatenate([before[...].astype(F32), grad], axis=1), first, second)
    else:
        core_before, far0, e_own, arrange = given
        first, second = outs[3:]
        core[0 : 2 * heads, :] = core_before[...]
        core[2 * heads : 3 * heads, :] = g_scr[:, rows : 2 * rows]
        core[3 * heads :, :] = far0[heads : 2 * heads, :]
        e = e_own[...].astype(F32) + unpack_rows(far0, 2 * heads, heads)
        if fast:
            transpose_into(eb_scr, e, spots, slice(None))
            e = eb_scr[...]
        else:
            e = mm(arrange[...], e.astype(BF16), NT)
        split_rows(jnp.concatenate([grad, e], axis=1), first, second)


def attend_back(h, fast, spots, sp, q, kt, k, vt, o, d, cs, tok_t, given, awaits=()):
    rows = kt[0].shape[2]
    total = 4 * rows
    width = tok_t.shape[0]
    heads = 3 * HD
    far = (2 * heads + 3 * heads // 2, 2 * heads, 2 * heads)[h]
    outs = [((heads, rows), BF16), ((far, rows), BF16), (((1, 2, 4)[h] * heads, rows), BF16)]
    if h == 0:
        outs += [((width, heads), BF16), ((heads, width), BF16)]
    else:
        outs += [((width // 2, 2 * heads), BF16)] * 2
    return run(
        functools.partial(attend_back_kernel, h, fast),
        12,
        20,
        (sp, spots),
        (*cs, tok_t, *given),
        outs,
        [
            pltpu.VMEM((128, total), BF16),
            pltpu.VMEM((128, total), BF16),
            pltpu.VMEM((HD, total), BF16),
            pltpu.VMEM((128, total), BF16),
            pltpu.VMEM((total, 128), BF16),
            pltpu.VMEM((128, total), BF16),
            pltpu.VMEM((total, 128), F32),
            pltpu.VMEM((128, total), F32),
            pltpu.VMEM((128, total), F32),
            pltpu.VMEM((heads, total), BF16),
            pltpu.VMEM((3 * heads, rows), BF16) if h == 0 else pltpu.VMEM((width, heads), F32),
            pltpu.SemaphoreType.DMA((25,)),
        ],
        awaits,
        apart=(*q, *kt, *k, *vt, *o, *d),
    )


def norm_parts(h):
    centred = h - jnp.mean(h, axis=-1, keepdims=True)
    inverse = lax.rsqrt(jnp.mean(centred * centred, axis=-1, keepdims=True) + 1e-05)
    return centred * inverse, inverse


def norm_back(grad, normed, inverse, gain):
    scaled = grad * gain
    return inverse * (
        scaled
        - jnp.mean(scaled, axis=-1, keepdims=True)
        - normed * jnp.mean(scaled * normed, axis=-1, keepdims=True)
    )


def sigmoid(v):
    return 0.5 + 0.5 * jnp.tanh(0.5 * v)


def out_kernel(a0, a1, a2, a3, w0, w1, w2, w3, tok_ref, gain_ref, bias_ref, low_ref, xhat_ref, inv_ref, *halves):
    w = jnp.concatenate([w0[...], w1[...], w2[...], w3[...]], axis=0)
    for half in range(2):
        at = slice(half * BLK, (half + 1) * BLK)
        a = jnp.concatenate([a0[:, at], a1[:, at], a2[:, at], a3[:, at]], axis=0)
        normed, inverse = norm_parts(tok_ref[at, :].astype(F32) + mm(a, w, TN))
        xhat_ref[at, :] = normed
        inv_ref[at, :] = jnp.broadcast_to(inverse, (BLK, 128))
        low = (normed * gain_ref[...] + bias_ref[...]).astype(BF16)
        low_ref[at, :] = low
        halves[half][...] = low


def out_project(a, w, tok, gain, bias, awaits=()):
    rows, width = tok.shape
    return run(
        out_kernel,
        3,
        10,
        (),
        (*a, *w, tok, gain, bias),
        (((rows, width), BF16), ((rows, width), F32), ((rows, 128), F32), *[((rows // 2, width), BF16)] * 2),
        awaits=awaits,
    )


PART_PLACES = ((0, 0, 0, 2), (0, 1, 0, 2), (0, 2, 0, 2), (0, 3, 0, 1), (0, 3, 1, 1)) + tuple((1, n, 0, 2) for n in range(4))


def gather_weights(at_ref, parts, wgu, wd, sem):
    copies = []
    for n, (part, (which, quarter, first, count)) in enumerate(zip(parts, PART_PLACES)):
        dst = (wgu, wd)[which]
        half = dst.shape[0] // 8
        spot = pl.ds(pl.multiple_of((at_ref[0] ^ quarter) * (2 * half) + first * half, half), count * half)
        copies.append(pltpu.make_async_copy(part, dst.at[spot, :], sem.at[n]))
    for c in copies:
        c.start()
    return copies


def mlp_rows(x, wg, wu, down, da, db, hid):
    gate, up = mm(x, wg), mm(x, wu)
    s = sigmoid(gate)
    act = gate * s
    low = (act * up).astype(BF16)
    da[...] = (up * (s + act * (1.0 - s))).astype(BF16)
    db[...] = act.astype(BF16)
    if hid is not None:
        hid[...] = low
    return mm(low, down)


def mlp_own_kernel(half0, half1, ml0, wgu, wd, acc, da, db, hid, ml1, sem):
    rows = ml0.shape[0]
    hidden = wd.shape[0]
    copies = []
    for n, half in enumerate((half0, half1)):
        copies.append(pltpu.make_async_copy(half, ml1.at[pl.ds(n * (rows // 2), rows // 2), :], sem.at[n]))
        copies[-1].start()
    for block, x in enumerate((ml0, ml1)):
        if block:
            for c in copies:
                c.wait()
        at = slice(block * rows, (block + 1) * rows)
        total = None
        for col in range(0, hidden, BLK):
            cols, ups = slice(col, col + BLK), slice(hidden + col, hidden + col + BLK)
            saved = [u.at[at, cols] for u in (da, db, hid)]
            part = mlp_rows(x[...], wgu[:, cols], wgu[:, ups], wd[cols, :], *saved)
            total = part if total is None else total + part
        acc[at, :] = total


def mlp_own(ml0, halves, wgu, wd, awaits=()):
    rows, width = ml0.shape
    hidden = wd.shape[0]
    saved = ((2 * rows, hidden), BF16)
    return run(
        mlp_own_kernel,
        5,
        10,
        (),
        (ml0, wgu, wd),
        [((2 * rows, width), F32)] + [saved] * 3 + [((rows, width), BF16)],
        [pltpu.SemaphoreType.DMA((2,))],
        awaits,
        apart=halves,
    )


def mlp_peer_kernel(at_ref, *refs):
    n_parts = len(PART_PLACES)
    ml0, ml1, acc, own, sib, da, db, wgu, wd, sem = refs[n_parts:]
    rows = ml0.shape[0]
    hidden = da.shape[1]
    for c in gather_weights(at_ref, refs[:n_parts], wgu, wd, sem):
        c.wait()
    for block, x in enumerate((ml0, ml1)):
        at = slice(block * rows, (block + 1) * rows)
        total = acc[at, :]
        for col in range(0, hidden, BLK):
            cols, ups = slice(col, col + BLK), slice(hidden + col, hidden + col + BLK)
            saved = [u.at[at, cols] for u in (da, db)]
            total += mlp_rows(x[...], wgu[:, cols], wgu[:, ups], wd[cols, :], *saved, None)
        if block:
            sib[...] = total.astype(BF16)
        else:
            own[...] = total


def mlp_peer(at, ml0, ml1, acc, parts, awaits=()):
    rows, width = ml0.shape
    hidden = parts[0].shape[1] // 2
    saved = ((2 * rows, hidden), BF16)
    return run(
        mlp_peer_kernel,
        6,
        13,
        (at,),
        (ml0, ml1, acc),
        [((rows, width), F32), ((rows, width), BF16)] + [saved] * 2,
        [pltpu.VMEM((width, 2 * hidden), BF16), pltpu.VMEM((hidden, width), BF16), pltpu.SemaphoreType.DMA((len(parts),))],
        awaits,
        apart=parts,
    )


def copies_of(src, dst, sem, rows=128):
    copies = []
    for n in range(src.shape[0] // rows):
        at = pl.ds(n * rows, rows)
        copies.append(pltpu.make_async_copy(src.at[at, :], dst.at[at, :], sem.at[n]))
        copies[-1].start()
    return copies


def mid_kernel(
    got, xhat_ref, own_ref, go_ref, g1, b1, g2, b2, out_ref, dh_ref, dm_ref, sums_ref, got_ref, sem
):
    gain_sum, bias_sum = 0.0, 0.0
    copies = copies_of(got, got_ref, sem)
    for start in range(0, xhat_ref.shape[0], 128):
        at = slice(start, start + 128)
        copies[start // 128].wait()
        mid = xhat_ref[at, :] * g1[...] + b1[...]
        normed, inverse = norm_parts(mid + (own_ref[at, :] + got_ref[at, :].astype(F32)))
        out_ref[at, :] = (normed * g2[...] + b2[...]).astype(BF16)
        grad = go_ref[at, :].astype(F32)
        dh = norm_back(grad, normed, inverse, g2[...])
        dh_ref[at, :] = dh
        dm_ref[at, :] = dh.astype(BF16)
        gain_sum += jnp.sum(grad * normed, axis=0, keepdims=True)
        bias_sum += jnp.sum(grad, axis=0, keepdims=True)
    sums_ref[0:1, :] = gain_sum
    sums_ref[1:2, :] = bias_sum


def mid_norm(xhat, own, got, out_grad, g1, b1, g2, b2, awaits=()):
    rows, width = xhat.shape
    return run(
        mid_kernel,
        3,
        8,
        (),
        (xhat, own, out_grad, g1, b1, g2, b2),
        (((rows, width), BF16), ((rows, width), F32), ((rows, width), BF16), ((2, width), F32)),
        [pltpu.VMEM((rows, width), BF16), pltpu.SemaphoreType.DMA((rows // 128,))],
        awaits,
        apart=(got,),
    )


def mlp_back_kernel(at_ref, *refs):
    n_parts = len(PART_PLACES)
    dm1_ref, dm0, wgu, wd, da_o, db_o, da_p, db_p, own, sib0, sib1, dg_o, du_o, wgu_p, wd_p, dm1, sem = refs[n_parts:]
    rows = dm0.shape[0]
    hidden = wd.shape[0]
    first = pltpu.make_async_copy(dm1_ref, dm1, sem.at[n_parts])
    first.start()
    copies = gather_weights(at_ref, refs[:n_parts], wgu_p, wd_p, sem)

    def part_of(x, at, cols, wg, wu, down, da, db, keep):
        dhid = mm(x[...], down, NT)
        dgate = (dhid * da[at, cols].astype(F32)).astype(BF16)
        dup = (dhid * db[at, cols].astype(F32)).astype(BF16)
        if keep:
            dg_o[at, cols] = dgate
            du_o[at, cols] = dup
        return mm(dgate, wg, NT) + mm(dup, wu, NT)

    totals = [None, None]
    for peer, (gu, down, da, db) in enumerate(((wgu, wd, da_o, db_o), (wgu_p, wd_p, da_p, db_p))):
        for block, x in enumerate((dm0, dm1)):
            if block and not peer:
                first.wait()
            at = slice(block * rows, (block + 1) * rows)
            for col in range(0, hidden, BLK):
                cols, ups = slice(col, col + BLK), slice(hidden + col, hidden + col + BLK)
                part = part_of(x, at, cols, gu[:, cols], gu[:, ups], down[cols, :], da, db, not peer)
                totals[block] = part if totals[block] is None else totals[block] + part
        if not peer:
            for c in copies:
                c.wait()
    own[...] = totals[0]
    sib0[...] = totals[1][0 : rows // 2].astype(BF16)
    sib1[...] = totals[1][rows // 2 :].astype(BF16)


def mlp_backward(at, dm0, dm1, wgu, wd, parts, da_o, db_o, da_p, db_p, awaits=()):
    rows, width = dm0.shape
    hidden = wd.shape[0]
    saved = ((2 * rows, hidden), BF16)
    return run(
        mlp_back_kernel,
        11,
        18,
        (at,),
        (dm0, wgu, wd, da_o, db_o, da_p, db_p),
        [((rows, width), F32)] + [((rows // 2, width), BF16)] * 2 + [saved] * 2,
        [
            pltpu.VMEM((width, 2 * hidden), BF16),
            pltpu.VMEM((hidden, width), BF16),
            pltpu.VMEM((rows, width), BF16),
            pltpu.SemaphoreType.DMA((len(parts) + 1,)),
        ],
        awaits,
        apart=(*parts, dm1),
    )


def first_norm_kernel(
    got_ref, got_late, dh2, own, xhat, inv, g1, sums2, a0, a1, a2, a3, w0, w1, w2, w3,
    dh1, d0, d1, d2, d3, ea, dat_scr, got, sem,
):
    gain_sum, bias_sum = 0.0, 0.0
    half = got_ref.shape[0]
    copies = copies_of(got_ref, got, sem) + copies_of(got_late, got.at[pl.ds(half, half), :], sem.at[pl.ds(half // 128, half // 128)])
    for start in range(0, dh2.shape[0], 128):
        at = slice(start, start + 128)
        copies[start // 128].wait()
        dmid = dh2[at, :] + (own[at, :] + got[at, :].astype(F32))
        normed = xhat[at, :]
        gain_sum += jnp.sum(dmid * normed, axis=0, keepdims=True)
        bias_sum += jnp.sum(dmid, axis=0, keepdims=True)
        grad = norm_back(dmid, normed, inv[at, 0:1], g1[...])
        dh1[at, :] = grad
        dat_scr[at, :] = grad.astype(BF16)
    sums = jnp.concatenate([gain_sum, bias_sum, sums2[...]], axis=0)
    high = sums.astype(BF16).astype(F32)
    both = jnp.concatenate([high, sums - high], axis=0)
    rest = jnp.concatenate([both[:, 512:], jnp.zeros((8, dh2.shape[0] - 256), F32)], axis=1)
    tail = jnp.concatenate([both[:, 0:512], rest], axis=0).astype(BF16)
    dat = dat_scr[...]
    for w, d in ((w0, d0), (w1, d1), (w2, d2), (w3, d3)):
        d[0:192, :] = mm(w[...], dat, NT).astype(BF16)
        d[192:208, :] = tail
    ea[...] = mm(jnp.concatenate([a0[...], a2[...]], axis=0), dat).astype(BF16)
    pack_rows(d1, 208, mm(jnp.concatenate([a1[...], a3[...]], axis=0), dat))


def pack_rows(dst, start, value):
    n = value.shape[0]
    rest = value[:, 512:]
    dst[start : start + n, :] = value[:, 0:512].astype(dst.dtype)
    dst[start + n : start + n + n // 2, :] = jnp.concatenate([rest[0 : n // 2], rest[n // 2 :]], axis=1).astype(dst.dtype)


def unpack_rows(src, start, n):
    rest = src[start + n : start + n + n // 2, :].astype(F32)
    rest = jnp.concatenate([rest[:, 0:256], rest[:, 256:]], axis=0)
    return jnp.concatenate([src[start : start + n, :].astype(F32), rest], axis=1)


def first_norm_back(dh2, own, got, xhat, inv, g1, sums2, a, w, awaits=()):
    rows, width = dh2.shape
    heads = a[0].shape[0]
    d = ((heads + 16, rows), BF16)
    return run(
        first_norm_kernel,
        5,
        12,
        (),
        (dh2, own, xhat, inv, g1, sums2, *a, *w),
        [((rows, width), F32), d, ((4 * heads + 16, rows), BF16), d, d, ((2 * heads, width), BF16)],
        [pltpu.VMEM((rows, width), BF16), pltpu.VMEM((rows, width), BF16), pltpu.SemaphoreType.DMA((rows // 128,))],
        awaits,
        apart=got,
    )


def far_kernel(
    fast, spots_a, spots_b, dm0, dm1, dm2, dm3, ml2, ml3, wgu, wd, hid_o,
    a_first, a_second, b_first, b_second, dg, du, dmt_a, dmt_b, hids,
):
    rows = dm0.shape[0]
    hidden = wd.shape[0]
    for p, u in enumerate((dm0, dm1, dm2, dm3)):
        cols = slice(p * rows, (p + 1) * rows)
        transpose_into(dmt_a, u[...], spots_a if fast else None, cols)
        transpose_into(dmt_b, u[...], spots_b if fast else None, cols)
    for col in range(0, hidden, BLK):
        cols, ups = slice(col, col + BLK), slice(hidden + col, hidden + col + BLK)
        hids[0 : 2 * rows, :] = hid_o[:, cols]
        for block, (x, dm) in enumerate(((ml2, dm2), (ml3, dm3))):
            at = slice(block * rows, (block + 1) * rows)
            gate, up, dhid = mm(x[...], wgu[:, cols]), mm(x[...], wgu[:, ups]), mm(dm[...], wd[cols, :], NT)
            s = sigmoid(gate)
            act = gate * s
            hids[(2 + block) * rows : (3 + block) * rows, :] = (act * up).astype(BF16)
            dg[at, cols] = (dhid * (up * (s + act * (1.0 - s)))).astype(BF16)
            du[at, cols] = (dhid * act).astype(BF16)
        for turned, first, second, start in ((dmt_a, a_first, a_second, 0), (dmt_b, b_first, b_second, hidden // 2)):
            lo, hi = max(col, start), min(col + BLK, start + hidden // 2)
            if lo < hi:
                there = slice(lo - start, hi - start)
                split_rows(mm(turned[...], hids[:, lo - col : hi - col]), first.at[:, there], second.at[:, there])


def far_rows(fast, spots, dm, ml, wgu, wd, hid, awaits=()):
    rows, width = dm[0].shape
    hidden = wd.shape[0]
    half = ((width // 2, hidden // 2), BF16)
    return run(
        functools.partial(far_kernel, fast),
        8,
        18,
        spots,
        (*dm, *ml, wgu, wd, hid),
        [half] * 4 + [((2 * rows, hidden), BF16)] * 2,
        [*[pltpu.VMEM((width, 4 * rows), BF16)] * 2, pltpu.VMEM((4 * rows, BLK), BF16)],
        awaits,
    )


def weight_kernel(
    fast, spots_a, spots_b, d0, d1, d2, d3, ml0, ml1, ml2, ml3, dg, du, dg_f, du_f, da_first, da_second, db_first,
    db_second, a_first, a_second, b_first, b_second, total, mlt_a, mlt_b, tail_scr, sem,
):
    rows = ml0.shape[0]
    hidden = dg.shape[1]
    copies = [
        pltpu.make_async_copy(d.at[pl.ds(3 * HD, 16), :], tail_scr.at[p], sem.at[p]) for p, d in enumerate((d0, d1, d2, d3))
    ]
    for c in copies:
        c.start()
    for p, u in enumerate((ml0, ml1, ml2, ml3)):
        cols = slice(p * rows, (p + 1) * rows)
        transpose_into(mlt_a, u[...], spots_a if fast else None, cols)
        transpose_into(mlt_b, u[...], spots_b if fast else None, cols)
    for src, dst in ((da_first, a_first), (da_second, a_second), (db_first, b_first), (db_second, b_second)):
        dst[:, hidden:] = src[...]
    wide = slice(0, hidden)
    for turned, near, far, first, second in ((mlt_a, dg, dg_f, a_first, a_second), (mlt_b, du, du_f, b_first, b_second)):
        grad = mm(turned[:, 0 : 2 * rows], near[...]) + mm(turned[:, 2 * rows :], far[...])
        split_rows(grad, first.at[:, wide], second.at[:, wide])
    for c in copies:
        c.wait()
    sums = [tail_scr[p].astype(F32) for p in range(4)]
    joined = (sums[0] + sums[1]) + (sums[2] + sums[3])
    total[:, 0:512] = joined[0:4] + joined[4:8]
    total[:, 512:768] = (joined[8:12] + joined[12:16])[:, 0:256]


def weight_grads(fast, spots, d, ml, near, far, down, awaits=()):
    rows, width = ml[0].shape
    hidden = near[0].shape[1]
    chain = ((width // 2, hidden + hidden // 2), BF16)
    return run(
        functools.partial(weight_kernel, fast),
        6,
        16,
        spots,
        (*ml, *near, *far, *down),
        [chain] * 4 + [((4, width), F32)],
        [
            *[pltpu.VMEM((width, 4 * rows), BF16)] * 2,
            pltpu.VMEM((4, 16, rows), BF16),
            pltpu.SemaphoreType.DMA((4,)),
        ],
        awaits,
        apart=d,
    )


def join_kernel(core, got1, got2, out, sem):
    heads = 3 * HD
    pieces = ((core, 0, 4 * heads), (got1, heads, heads), (got2, heads, heads))
    copies, at = [], 0
    for n, (src, start, count) in enumerate(pieces):
        copies.append(pltpu.make_async_copy(src.at[pl.ds(start, count), :], out.at[pl.ds(at, count), :], sem.at[n]))
        copies[-1].start()
        at += count
    for c in copies:
        c.wait()


def join(core, got1, got2):
    return run(
        join_kernel,
        1,
        4,
        (),
        (),
        [((18 * HD, core.shape[1]), BF16)],
        [pltpu.SemaphoreType.DMA((3,))],
        apart=(core, got1, got2),
    )[0]


def by_heads(w):
    heads = 3 * HD
    return jnp.concatenate([w[c * heads + h * HD : c * heads + (h + 1) * HD, :] for h in range(3) for c in range(3)], axis=0)


def near_kernel(f0, f1, f2, dh1, n0, n1, n2, w0, w2, out, far, sem):
    heads = 3 * HD
    copies = []
    for n, f in enumerate((f0, f1, f2)):
        spot = pl.ds(n * heads, heads)
        copies.append(pltpu.make_async_copy(f.at[pl.ds(0, heads), :], far.at[spot, :], sem.at[n]))
        copies[-1].start()
    near = jnp.concatenate([n0[...], n1[...], n2[...]], axis=0)
    out[...] = dh1[...] + mm(near, by_heads(w0), TN)
    for c in copies:
        c.wait()
    out[...] += mm(far[...], by_heads(w2), TN)


def input_near(dh1, near, far, w0, w2):
    return run(
        near_kernel,
        3,
        12,
        (),
        (dh1, *near, w0, w2),
        [(dh1.shape, F32)],
        [pltpu.VMEM((9 * HD, dh1.shape[0]), BF16), pltpu.SemaphoreType.DMA((3,))],
        apart=far,
    )[0]


def input_kernel(core_ref, before, w1, w3, out, core, total, sem):
    arrival = pltpu.make_async_copy(core_ref, core, sem.at[0])
    arrival.start()
    w = jnp.concatenate([by_heads(w1), by_heads(w3)], axis=0)
    arrival.wait()
    copies = []
    for half in range(before.shape[0] // BLK):
        at = slice(half * BLK, (half + 1) * BLK)
        total[at, :] = before[at, :] + mm(core[:, at], w, TN)
        spot = pl.ds(half * BLK, BLK)
        copies.append(pltpu.make_async_copy(total.at[spot, :], out.at[spot, :], sem.at[1 + half]))
        copies[-1].start()
    for c in copies:
        c.wait()


def input_back(before, core, w1, w3):
    return run(
        input_kernel,
        3,
        14,
        (),
        (before, w1, w3),
        [(before.shape, F32)],
        [
            pltpu.VMEM(core.shape, BF16),
            pltpu.VMEM(before.shape, F32),
            pltpu.SemaphoreType.DMA((1 + before.shape[0] // BLK,)),
        ],
        apart=(core,),
        hbm=(0,),
    )[0]


def split_halves(v):
    return v[0 : v.shape[0] // 2], v[v.shape[0] // 2 :]


def swap(v, bit, axis="tensor"):
    n = lax.axis_size(axis)
    return lax.ppermute(v, axis, [(i, i ^ bit) for i in range(n)])


def bits_of(n):
    return n.bit_length() - 1


def spots_of(order, n):
    block = jnp.arange(n, dtype=jnp.int32) ^ lax.axis_index("dp")
    spot = jnp.zeros((n,), jnp.int32)
    for s, bit in enumerate(order):
        spot = spot + (((block >> bit) & 1) << (len(order) - 1 - s))
    return spot


def last_kernel(chains, kind, *refs):
    count = sum(chains)
    parts, outs, scrs, sem = refs[:count], refs[count:-count - 1], refs[-count - 1 : -1], refs[-1]
    copies = []
    for n, (part, scr) in enumerate(zip(parts, scrs)):
        copies.append(pltpu.make_async_copy(part.at[pl.ds(0, scr.shape[0]), :], scr, sem.at[n]))
        copies[-1].start()
    for c in copies:
        c.wait()
    sums, at = [], 0
    for length in chains:
        sums.append(sum(scr[...].astype(F32) for scr in scrs[at : at + length]))
        at += length
    if kind == "mlp":
        gu, down = outs
        width = down.shape[1]
        one, two = sums[0:2]
        if len(sums) > 2:
            one += sums[2][:, 0 : one.shape[1]]
            two += sums[2][:, one.shape[1] :]
        gu[:, 0, :] = one[:, 0:width]
        gu[:, 1, :] = two[:, 0:width]
        down[...] = jnp.concatenate([one[:, width:], two[:, width:]], axis=1)
    else:
        qkv, out = outs
        total = jnp.concatenate(sums[0:2], axis=1)
        if len(sums) > 2:
            total += sums[2]
        for c in range(3):
            qkv[c] = jnp.concatenate([total[:, (3 * h + c) * HD : (3 * h + c + 1) * HD] for h in range(3)], axis=1)
        out[...] = total[:, 9 * HD :].T


def last_sums(kind, rows, chains, outs):
    parts = [part for chain in chains for part in chain]
    return run(
        functools.partial(last_kernel, [len(chain) for chain in chains], kind),
        2,
        8,
        (),
        (),
        outs,
        [pltpu.VMEM((rows, part.shape[1]), BF16) for part in parts] + [pltpu.SemaphoreType.DMA((len(parts),))],
        apart=parts,
    )


class scatter_steps:
    def __init__(self, first, second, order):
        self.first, self.parts, self.order, self.step = first, [first], order, 0
        self.sent = second

    def advance(self):
        self.parts.append(swap(self.sent, 1 << self.order[self.step], "dp"))
        self.step += 1
        self.next_sent()
        return self.parts[-1]

    def next_sent(self):
        if self.step < len(self.order):
            length = self.parts[-1].shape[0]
            self.sent = sum(u[length // 2 : length].astype(F32) for u in self.parts).astype(BF16)

    def all_parts(self):
        while self.step < len(self.order):
            self.advance()
        return self.parts


def advance_together(chains):
    bits = {chain.order[chain.step] for chain in chains}
    if len(bits) > 1 or any(chain.step < len(chain.order) - 1 for chain in chains):
        return None
    for chain in chains:
        chain.step += 1
    return swap(jnp.concatenate([chain.sent for chain in chains], axis=1), 1 << bits.pop(), "dp")


def first_sums(chains, rows):
    return [sum(part[0:rows].astype(F32) for part in chain) for chain in chains]


def quarter_of(w):
    rows = w.shape[0] // 4
    return lax.dynamic_slice_in_dim(w, (lax.axis_index("dp") % 4) * rows, rows, axis=0)


def local(
    tokens,
    doc_lengths,
    key_mask,
    qkv_weight,
    out_weight,
    gate_up_weight,
    down_weight,
    norm1_gain,
    norm1_bias,
    norm2_gain,
    norm2_bias,
    out_grad,
):
    rows, width = tokens.shape
    flags = jnp.pad(key_mask.astype(BF16).reshape(1, rows), ((0, EXTRA - 1), (0, width - rows)))
    tok0 = jnp.concatenate([tokens, flags], axis=0)
    tok1 = swap(tok0, 1)
    tok2 = swap(tok0, 2)
    sp = jnp.concatenate([doc_lengths[0], lax.axis_index("tensor").reshape(1)]).astype(jnp.int32)
    quarter = (lax.axis_index("dp") % 4).reshape(1).astype(jnp.int32)
    freqs = 1000.0 ** (-(jnp.arange(HD // 2, dtype=F32) * 2.0 / HD))
    freqs = jnp.broadcast_to(freqs[:, None], (HD // 2, 128))
    wt = jnp.transpose(qkv_weight, (1, 2, 0)).reshape(-1, width)

    n_dp = lax.axis_size("dp")
    fast = (width // n_dp) % 16 == 0
    order = list(range(bits_of(n_dp)))
    order_b = order[1:2] + order[0:1] + order[2:]
    spots, spots_b = (spots_of(u, n_dp) for u in (order, order_b))

    def arranged(v, at):
        if fast:
            return v
        blocks = v.reshape(v.shape[0], n_dp, width // n_dp)
        return jnp.take(blocks, jnp.argsort(at), axis=1).reshape(v.shape)

    ORDER.last = ()
    wo0 = out_weight
    wo1, wt1 = swap(wo0, 1), swap(wt, 1)
    wgu = gate_up_weight.reshape(width, -1)
    part_a, part_b = quarter_of(down_weight), quarter_of(wgu)

    proj = [project(0, sp, freqs, tok0, wt), project(1, sp, freqs, tok1, wt, awaits=(part_a, part_b, wt1))]
    (tok2,) = gate(tok2)
    tok3 = swap(tok2, 1)
    wo2 = swap(wo0, 2)
    tok = (tok0, tok1, tok2, tok3)
    *more, part_a = project(2, sp, freqs, tok2, wt, carry=(part_a,))
    proj.append(more)
    pa0 = swap(part_a, 2)
    *more, part_b = project(3, sp, freqs, tok3, wt, carry=(part_b,))
    proj.append(more)
    pb0 = swap(part_b, 2)
    qt, kt, k, vt, cs = zip(*proj)
    o2, o3, q2, q3 = attend(1, sp, qt, k, vt, (wo1,))
    o2, o3, wo2, pa0 = gate(o2, o3, wo2, pa0)
    pa1, pa2, pa3 = swap(pa0, 1, "dp"), swap(pa0, 2, "dp"), swap(pa0, 3, "dp")
    g2 = swap(o2, 2)
    o0, o1, q0, q1 = attend(0, sp, qt, k, vt)
    o1, o3, pb0, wo2 = gate(o1, o3, pb0, wo2, awaits=(g2, pa1, pa2, pa3))
    g1, g3, wo3 = swap(o1, 1), swap(o3, 3), swap(wo2, 1)
    wo = (wo0, wo1, wo2, wo3)
    pb1, pb2 = swap(pb0, 1, "dp"), swap(pb0, 2, "dp")
    toks = transposed(fast, (spots_b, spots), tok, rows)
    if not fast:
        toks = [arranged(toks[0].T, u).T for u in (spots_b, spots)]
    (g3,) = gate(g3)

    gain1, bias1, gain2, bias2 = (u.reshape(1, width) for u in (norm1_gain, norm1_bias, norm2_gain, norm2_bias))
    ml0, xhat1, inv1, *halves = out_project((o0, g1, g2, g3), wo, tokens, gain1, bias1)
    acc, da_o, db_o, hid_o, ml1 = mlp_own(ml0, [swap(u, 1) for u in halves], wgu, down_weight)
    half2, half1 = park((), ((pb2, 0), (pb1, 1)))
    half2, half1, ml0 = gate(half2, half1, ml0)
    parts = (pb0, pb1, pb2, swap(half2, 1, "dp"), swap(half1, 2, "dp"), pa0, pa1, pa2, pa3)
    ml2 = swap(ml0, 2)
    kept = park((*kt, *k, *vt, q0, q1, q2, q3, *toks))
    kt, k, vt, (q0, q1, q2, q3, *toks) = kept[0:4], kept[4:8], kept[8:12], kept[12:18]
    own, sib, da_p, db_p = mlp_peer(quarter, ml0, ml1, acc, parts)
    (sib,) = gate(sib, awaits=(ml2,))
    output, dh2, dm0, sums2 = mid_norm(xhat1, own, swap(sib, 1), out_grad, gain1, bias1, gain2, bias2)
    dm0, ml2 = gate(dm0, ml2)
    dm1, dm2 = swap(dm0, 1), swap(dm0, 2)
    ml3 = swap(ml2, 1)
    own, sib0, sib1, dg_o, du_o = mlp_backward(quarter, dm0, dm1, wgu, down_weight, parts, da_o, db_o, da_p, db_p)
    sib0, sib1 = gate(sib0, sib1, awaits=(ml3,))
    dh1, d0, d1, d2, d3, ea = first_norm_back(
        dh2, own, (swap(sib0, 1), swap(sib1, 1)), xhat1, inv1, gain1, sums2, (o0, g1, g2, g3), wo
    )
    d1, d2, d3, dm2 = gate(d1, d2, d3, dm2)
    dm3 = swap(dm2, 1)
    d = (d0, swap(d1, 1), swap(d2, 2), swap(d3, 3))
    ml, dm, both = (ml0, ml1, ml2, ml3), (dm0, dm1, dm2, dm3), (spots, spots_b)
    *down, dg_f, du_f = far_rows(fast, both, dm, ml[2:], wgu, down_weight, hid_o)
    (wt,) = gate(wt, awaits=d[1:])
    wt2 = swap(wt, 2)
    a_first, a_second, b_first, b_second, sums = weight_grads(
        fast, both, d, ml, (dg_o, du_o), (dg_f, du_f), down
    )
    if not fast:
        a_first, a_second = split_halves(arranged(jnp.concatenate([a_first, a_second]).T, spots).T)
        b_first, b_second = split_halves(arranged(jnp.concatenate([b_first, b_second]).T, spots_b).T)
    a_second, b_second, sums = gate(a_second, b_second, sums)
    sum_bits = order[2:3] + order[1::-1] + order[3:]
    sums_got = swap(sums, 1 << sum_bits[0], "dp")
    chain_a, chain_b = scatter_steps(a_first, a_second, order), scatter_steps(b_first, b_second, order_b)
    a_got, b_got = chain_a.advance(), chain_b.advance()

    arrange = jnp.zeros((8, 128), BF16)
    if not fast:
        column = jnp.arange(width)
        target = spots[column // (width // n_dp)] * (width // n_dp) + column % (width // n_dp)
        arrange = (column[:, None] == target[None, :]).astype(BF16)
    back = functools.partial(
        attend_back,
        fast=fast,
        spots=spots,
        sp=sp,
        q=(q0, q1, q2, q3),
        kt=kt,
        k=k,
        vt=vt,
        o=(o0, o1, o2, o3),
        d=d,
        cs=cs,
    )
    near0, far0, core0, grad0, e_own = back(0, tok_t=toks[0], given=(ea,))
    far0, chain_a.parts[-1], chain_b.parts[-1], wt2, sums_got = gate(far0, a_got, b_got, wt2, sums_got)
    for chain in (chain_a, chain_b):
        chain.next_sent()
    a_got, b_got, got0 = chain_a.advance(), chain_b.advance(), swap(far0, 2)
    sums = sums + sums_got
    sums_got = swap(sums, 1 << sum_bits[1], "dp")
    near1, far1, core1, first, second = back(1, tok_t=toks[0], given=(core0, grad0))
    far1, second, chain_a.parts[-1], chain_b.parts[-1], sums_got, wt2 = gate(far1, second, a_got, b_got, sums_got, wt2)
    for chain in (chain_a, chain_b):
        chain.next_sent()
    c1 = scatter_steps(first, second, order_b)
    c1_got, mlp3 = c1.advance(), advance_together((chain_a, chain_b))
    wt3 = swap(wt2, 1)
    got1 = swap(far1, 2)
    sums = sums + sums_got
    sums_got = swap(sums, 1 << sum_bits[2], "dp")
    near2, far2, core2, first, second = back(2, tok_t=toks[1], given=(core1, got0, e_own, arrange))
    far2, second, c1.parts[-1], sums_got = gate(far2, second, c1_got, sums_got, awaits=(got1, wt3))
    c1.next_sent()
    sums = sums + sums_got
    for bit in sum_bits[3:]:
        sums = sums + swap(sums, 1 << bit, "dp")
    c2 = scatter_steps(first, second, order)
    c2_got, c1_got, got2 = c2.advance(), c1.advance(), swap(far2, 2)
    (c2.parts[-1],) = gate(c2_got)
    c2.next_sent()
    c2_got = c2.advance()
    mlp, shard = [chain_a.all_parts(), chain_b.all_parts()], width // n_dp
    if mlp3 is not None:
        mlp.append([mlp3])
    if fast:
        hidden = down_weight.shape[0]
        gu_part, down_part = last_sums("mlp", shard, mlp, [((shard, 2, hidden), F32), ((shard, hidden), F32)])
    core = swap(join(core2, got1, got2), 1)
    input_grad = input_near(dh1, (near0, near1, near2), (got0, got1, got2), wt, wt2)
    c2.parts[-1], c1.parts[-1] = gate(c2_got, c1_got)
    c2.next_sent()
    c1.next_sent()
    both = advance_together((c1, c2))
    attention = [c1.all_parts(), c2.all_parts()]
    if both is not None:
        attention.append([both])
    input_grad = input_back(input_grad, core, wt1, wt3)
    if fast:
        qkv_part, out_part = last_sums(
            "attention", shard, attention, [((3, shard, 3 * HD), F32), ((3 * HD, shard), F32)]
        )
        qkv_part = jnp.transpose(qkv_part, (1, 0, 2))
    else:
        one, two = first_sums(mlp, shard)
        gu_part = jnp.stack([one[:, 0:width], two[:, 0:width]], axis=1)
        down_part = jnp.concatenate([one[:, width:], two[:, width:]], axis=1)
        total = jnp.concatenate(first_sums(attention, shard), axis=1)
        out_part = total[:, 9 * HD :].T
        qkv_part = jnp.transpose(total[:, 0 : 9 * HD].reshape(shard, 3, 3, HD), (0, 2, 1, 3)).reshape(shard, 3, 3 * HD)
    return (
        output,
        input_grad,
        qkv_part,
        out_part,
        gu_part,
        down_part.T,
        sums[0],
        sums[1],
        sums[2],
        sums[3],
    )


def solution(mesh):
    placed = (
        P(("dp", "tensor"), None),
        P("dp", None),
        P(("dp", "tensor")),
        P(None, None, "tensor"),
        P("tensor", None),
        P(None, None, "tensor"),
        P("tensor", None),
        P(),
        P(),
        P(),
        P(),
        P(("dp", "tensor"), None),
    )
    return jax.shard_map(
        local,
        mesh=mesh,
        in_specs=placed,
        out_specs=(
            P(("dp", "tensor"), None),
            P(("dp", "tensor"), None),
            P("dp", None, "tensor"),
            P("tensor", "dp"),
            P("dp", None, "tensor"),
            P("tensor", "dp"),
            P(),
            P(),
            P(),
            P(),
        ),
        check_vma=False,
    )
```

```python
import functools

import jax
import jax.numpy as jnp
from jax import lax
from jax.experimental import pallas as pl
from jax.experimental.pallas import tpu as pltpu
from jax.sharding import PartitionSpec as P

HD = 64
F32 = jnp.float32
BF16 = jnp.bfloat16
BIG = -1e30
BLK = 256
WINDOWS = (640, 1664, 2048)
SCALE = 0.15
EXTRA = 16
NN = (((1,), (0,)), ((), ()))
NT = (((1,), (1,)), ((), ()))
TN = (((0,), (0,)), ((), ()))


def mm(a, b, dims=NN):
    return lax.dot_general(a, b, dims, preferred_element_type=F32)


class Order:
    def __init__(self):
        self.last = ()


ORDER = Order()


def run(kernel, us, mib, scalars, args, outs, scratch=(), awaits=(), carry=(), apart=(), hbm=()):
    in_vmem = pl.BlockSpec(memory_space=pltpu.VMEM)
    anywhere = pl.BlockSpec(memory_space=pl.ANY)
    awaits = (*awaits, *ORDER.last)
    n_in = len(scalars) + len(apart) + len(args)
    n_skip, n_out = len(awaits) + len(carry), len(outs)

    def body(*refs):
        rest = refs[n_in + n_skip :]
        kernel(*refs[:n_in], *rest[:n_out], *rest[n_out + len(carry) :])

    results = pl.pallas_call(
        body,
        in_specs=[pl.BlockSpec(memory_space=pltpu.SMEM)] * len(scalars)
        + [anywhere] * len(apart)
        + [in_vmem] * len(args)
        + [anywhere] * n_skip,
        out_specs=[pl.BlockSpec(memory_space=pltpu.HBM) if n in hbm else in_vmem for n in range(n_out)]
        + [anywhere] * len(carry),
        out_shape=[jax.ShapeDtypeStruct(*o) for o in outs] + [jax.ShapeDtypeStruct(c.shape, c.dtype) for c in carry],
        scratch_shapes=list(scratch),
        input_output_aliases={n_in + len(awaits) + i: n_out + i for i in range(len(carry))},
        compiler_params=pltpu.CompilerParams(vmem_limit_bytes=mib << 20),
        cost_estimate=pl.CostEstimate(flops=int(us * SCALE * 1.1e9), bytes_accessed=1 << 18, transcendentals=0),
    )(*scalars, *apart, *args, *awaits, *carry)
    ORDER.last = (min(results[:n_out], key=lambda r: r.size),)
    return results


def gate_kernel(out):
    out[...] = jnp.zeros(out.shape, F32)


def gate(*arrays, awaits=()):
    return run(gate_kernel, 0.1, 4, (), (), [((8, 128), F32)], awaits=awaits, carry=arrays)[1:]


def park_kernel(places, *refs):
    count = len(places)
    copies = []
    for n, (first, rows) in enumerate(places):
        src = refs[n] if rows is None else refs[n].at[pl.ds(first, rows), :]
        copies.append(pltpu.make_async_copy(src, refs[count + n], refs[-1].at[n]))
        copies[-1].start()
    for c in copies:
        c.wait()


def park(arrays, halves=()):
    places = [(0, None) for _ in arrays] + [(n * (u.shape[0] // 2), u.shape[0] // 2) for u, n in halves]
    outs = [(u.shape, u.dtype) for u in arrays] + [((u.shape[0] // 2, u.shape[1]), u.dtype) for u, n in halves]
    return run(
        functools.partial(park_kernel, places),
        3,
        4,
        (),
        (),
        outs,
        [pltpu.SemaphoreType.DMA((len(outs),))],
        apart=(*arrays, *[u for u, n in halves]),
        hbm=range(len(outs)),
    )


def split3(v):
    top = v.astype(BF16).astype(F32)
    rest = v - top
    middle = rest.astype(BF16).astype(F32)
    return top, middle, rest - middle


def split_rows(value, first, second):
    half = first.shape[0]
    first[...] = value[0:half].astype(first.dtype)
    second[...] = value[half:].astype(second.dtype)


def transpose_into(dst, value, spots, cols):
    turned = value.T
    if spots is None:
        dst[:, cols] = turned
        return
    count = spots.shape[0]
    rows = turned.shape[0] // count
    for b in range(count):
        dst[pl.ds(pl.multiple_of(spots[b] * rows, rows), rows), cols] = turned[b * rows : (b + 1) * rows]


def transpose_kernel(fast, *refs):
    count = (len(refs) - 4) // 2
    spots, tokens, outs = refs[:count], refs[count : count + 4], refs[count + 4 :]
    rows = outs[0].shape[1] // 4
    for p, t in enumerate(tokens):
        for spot, out in zip(spots, outs):
            transpose_into(out, t[0:rows, :], spot if fast else None, slice(p * rows, (p + 1) * rows))


def transposed(fast, spots, pieces, rows):
    width = pieces[0].shape[1]
    outs = [((width, 4 * rows), BF16)] * len(spots)
    return run(functools.partial(transpose_kernel, fast), 2, 8, spots, pieces, outs)


def project_kernel(piece, sp_ref, freq_ref, tok_ref, w_ref, qt_ref, kt_ref, k_ref, vt_ref, cs_ref):
    n = tok_ref.shape[0] - EXTRA
    place = (sp_ref[8] ^ piece) * n + lax.broadcasted_iota(jnp.int32, (1, n), 1)
    seg = jnp.zeros((1, n), jnp.int32)
    pos = place
    end = 0
    for d in range(8):
        length = sp_ref[d]
        end = end + length
        past = place >= end
        seg += past.astype(jnp.int32)
        pos -= jnp.where(past, length, 0)
    angles = pos.astype(F32) * freq_ref[:, 0:1]
    cosine, sine = jnp.cos(angles), jnp.sin(angles)
    cs_ref[0:32, :] = cosine
    cs_ref[32:64, :] = sine
    idx = lax.broadcasted_iota(jnp.int32, (64, n), 0)
    which = jnp.where(idx < 19, idx - 8, idx - 19)
    bit = (jnp.broadcast_to(place, (64, n)) >> jnp.clip(which, 0, 10)) & 1
    flipped = jnp.where(idx < 19, bit, 1 - bit).astype(F32)
    same = (idx == seg).astype(F32)
    coded = (idx >= 8) & (idx < 30)
    invalid = 1.0 - tok_ref[n : n + EXTRA, 0:n].astype(F32)[0:1]
    q_tail = jnp.where(idx < 8, BIG * (1.0 - same), jnp.where(coded, BIG * flipped, 0.0))
    k_tail = jnp.where(idx < 8, same, jnp.where(coded, invalid * (1.0 - flipped), 0.0))
    k_tail = jnp.where((idx >= 32) & (idx < 35), 1.0, k_tail)
    v_tail = jnp.where(idx < 3, 1.0, 0.0)
    y = mm(w_ref[...], tok_ref[0:n, :], NT)

    def rotated(at):
        a, b = y[at : at + 32], y[at + 32 : at + 64]
        return jnp.concatenate([a * cosine - b * sine, b * cosine + a * sine], axis=0)

    for h in range(3):
        qt_ref[h] = jnp.concatenate([rotated(h * HD) * 0.125, q_tail], axis=0).astype(BF16)
        key = jnp.concatenate([rotated(192 + h * HD), k_tail], axis=0)
        kt_ref[h] = key.astype(BF16)
        k_ref[h] = key.T.astype(BF16)
        vt_ref[h] = jnp.concatenate([y[384 + h * HD : 448 + h * HD], v_tail], axis=0).astype(BF16)


def project(piece, sp, freqs, tok, w, awaits=(), carry=()):
    rows = tok.shape[0] - EXTRA
    wide, tall = ((3, 128, rows), BF16), ((3, rows, 128), BF16)
    return run(
        functools.partial(project_kernel, piece),
        2.5,
        10,
        (sp,),
        (freqs, tok, w),
        (wide, wide, tall, wide, ((HD, rows), F32)),
        awaits=awaits,
        carry=carry,
    )


def window_of(sp_ref, block, total):
    a = block * BLK
    b = a + BLK - 1
    first, last, end = 0, 0, 0
    for d in range(8):
        begin, end = end, end + sp_ref[d]
        first = jnp.where(begin <= a, begin, first)
        last = jnp.where(begin <= b, end, last)
    start = (first // 128) * 128
    kind = jnp.where(last - start <= WINDOWS[0], 0, jnp.where(last - start <= WINDOWS[1], 1, 2))
    size = jnp.where(kind == 0, WINDOWS[0], jnp.where(kind == 1, WINDOWS[1], WINDOWS[2]))
    return pl.multiple_of(jnp.minimum(start, total - size), 128), kind


def place_of(sp_ref, piece, rows):
    return pl.ds(pl.multiple_of((sp_ref[8] ^ piece) * rows, rows), rows)


def attend_kernel(base, sp_ref, qa, qb, k0, k1, k2, k3, v0, v1, v2, v3, oa, ob, ba, bb, k_scr, v_scr, s_scr, q_scr, o_scr):
    rows = qa.shape[2]
    total = 4 * rows
    for p, (k, v) in enumerate(((k0, v0), (k1, v1), (k2, v2), (k3, v3))):
        at = place_of(sp_ref, p, rows)
        k_scr[:, at, :] = k[...]
        v_scr[:, :, at] = v[...]
    for n in range(4):
        q_scr[n] = (qa, qb)[n // 2][:, :, (n % 2) * BLK : (n % 2 + 1) * BLK]

    def q_block(i, carry):
        start, kind = window_of(sp_ref, (base + i) ^ (2 * sp_ref[8]), total)

        def scores(h, size):
            s = mm(k_scr[h, pl.ds(start, size), :], q_scr[i, h])
            s_scr[h, 0:size, :] = s
            return jnp.max(s, axis=0, keepdims=True)

        def weigh(h, size, top):
            p = jnp.exp(s_scr[h, 0:size, :] - top).astype(BF16)
            acc = mm(v_scr[h, :, pl.ds(start, size)], p)
            norm = acc[64:65]
            o_scr[i, h * HD : (h + 1) * HD, :] = (acc[0:64] / norm).astype(BF16)
            parts = split3(-(top + jnp.log(norm)))
            q_scr[i, h, 96:112, :] = jnp.concatenate([*parts, jnp.zeros((13, BLK), F32)], axis=0).astype(BF16)

        for mode, size in enumerate(WINDOWS):

            @pl.when(kind == mode)
            def _():
                t0 = scores(0, size)
                t1 = scores(1, size)
                weigh(0, size, t0)
                t2 = scores(2, size)
                weigh(1, size, t1)
                weigh(2, size, t2)

        return carry

    lax.fori_loop(0, 4, q_block, 0)
    for n in range(4):
        at = slice((n % 2) * BLK, (n % 2 + 1) * BLK)
        (oa, ob)[n // 2][:, at] = o_scr[n]
        (ba, bb)[n // 2][:, :, at] = q_scr[n]


def attend(half, sp, qt, k, vt, awaits=(), carry=()):
    rows = qt[0].shape[2]
    total = 4 * rows
    out, back = ((3 * HD, rows), BF16), ((3, 128, rows), BF16)
    return run(
        functools.partial(attend_kernel, half * 4),
        8,
        18,
        (sp,),
        (qt[2 * half], qt[2 * half + 1], *k, *vt),
        (out, out, back, back),
        [
            pltpu.VMEM((3, total, 128), BF16),
            pltpu.VMEM((3, 128, total), BF16),
            pltpu.VMEM((3, total, BLK), F32),
            pltpu.VMEM((4, 3, 128, BLK), BF16),
            pltpu.VMEM((4, 3 * HD, BLK), BF16),
        ],
        awaits,
        carry,
    )


def attend_back_kernel(h, fast, sp_ref, spots, *refs):
    q_refs, kt_refs, k_refs, vt_refs, o_refs, d_refs = (refs[4 * n : 4 * n + 4] for n in range(6))
    n_given = (1, 2, 4)[h]
    cs_refs, tok_t, given, outs = refs[24:28], refs[28], refs[29 : 29 + n_given], refs[29 + n_given : -12]
    q_scr, do_scr, o_scr, kt_scr, k_scr, vt_scr, dq_scr, dk_scr, dv_scr, g_scr, eb_scr, sem = refs[-12:]
    rows = kt_refs[0].shape[2]
    total = 4 * rows
    head = pl.ds(h * HD, HD)
    copies = []
    for p in range(4):
        spot, at = place_of(sp_ref, p, rows), pl.ds(p * rows, rows)
        copies += [
            (kt_refs[p].at[h], kt_scr.at[:, spot]),
            (k_refs[p].at[h], k_scr.at[spot, :]),
            (vt_refs[p].at[h], vt_scr.at[:, spot]),
            (q_refs[p].at[h], q_scr.at[:, at]),
            (d_refs[p].at[head, :], do_scr.at[pl.ds(0, HD), at]),
            (o_refs[p].at[head, :], o_scr.at[:, at]),
        ]
    if h == 0:
        copies.append((d_refs[1].at[pl.ds(208, 576), :], eb_scr))
    copies = [pltpu.make_async_copy(src, dst, sem.at[n]) for n, (src, dst) in enumerate(copies)]
    for c in copies:
        c.start()
    dk_scr[...] = jnp.zeros(dk_scr.shape, F32)
    dv_scr[...] = jnp.zeros(dv_scr.shape, F32)
    for c in copies:
        c.wait()
    do_scr[64:128, :] = jnp.zeros((64, total), BF16)
    delta = jnp.sum(do_scr[0:64, :].astype(F32) * o_scr[...].astype(F32), axis=0, keepdims=True)
    do_scr[64:80, :] = jnp.concatenate([*split3(-delta), jnp.zeros((13, total), F32)], axis=0).astype(BF16)

    def q_block(i, carry):
        start, kind = window_of(sp_ref, i ^ (2 * sp_ref[8]), total)
        here = pl.ds(pl.multiple_of(i * BLK, BLK), BLK)
        for mode, size in enumerate(WINDOWS):

            @pl.when(kind == mode)
            def _():
                qt, dot = q_scr[:, here], do_scr[:, here]
                q, do = qt.astype(F32).T.astype(BF16), dot.astype(F32).T.astype(BF16)
                win = pl.ds(start, size)
                p = jnp.exp(mm(q, kt_scr[:, win]))
                ds = (p * mm(do, vt_scr[:, win])).astype(BF16)
                dv_scr[:, win] += mm(dot, p.astype(BF16))
                dk_scr[:, win] += mm(qt, ds)
                dq_scr[here, :] = mm(ds, k_scr[win, :])

        return carry

    lax.fori_loop(0, 8, q_block, 0)

    def unrotated(g, cosine, sine):
        g = g.astype(BF16).astype(F32)
        a, b = g[0:32], g[32:64]
        return jnp.concatenate([a * cosine + b * sine, b * cosine - a * sine], axis=0).astype(BF16)

    for p in range(4):
        at = slice(p * rows, (p + 1) * rows)
        cosine, sine = cs_refs[p][0:32, :], cs_refs[p][32:64, :]
        src = place_of(sp_ref, p, rows)
        g_scr[0:64, at] = unrotated(dq_scr[at, :].T[0:64] * 0.125, cosine, sine)
        g_scr[64:128, at] = unrotated(dk_scr[0:64, src], cosine, sine)
        g_scr[128:192, at] = dv_scr[0:64, src].astype(BF16)
    grad = mm(tok_t[...], g_scr[...], NT)
    heads = 3 * HD
    near, far, core = outs[0:3]
    near[...] = g_scr[:, 0:rows]
    far[0:heads, :] = g_scr[:, 2 * rows : 3 * rows]
    far[heads : 2 * heads, :] = g_scr[:, 3 * rows :]
    if h == 0:
        (ea,) = given
        grad_out, e_own = outs[3:]
        core[...] = g_scr[:, rows : 2 * rows]
        grad_out[...] = grad.astype(BF16)
        e = ea[...].astype(F32) + unpack_rows(eb_scr, 0, 2 * heads)
        e_own[...] = e[0:heads].astype(BF16)
        pack_rows(far, 2 * heads, e[heads:])
    elif h == 1:
        core_before, before = given
        first, second = outs[3:]
        core[0:heads, :] = core_before[...]
        core[heads:, :] = g_scr[:, rows : 2 * rows]
        split_rows(jnp.concatenate([before[...].astype(F32), grad], axis=1), first, second)
    else:
        core_before, far0, e_own, arrange = given
        first, second = outs[3:]
        core[0 : 2 * heads, :] = core_before[...]
        core[2 * heads : 3 * heads, :] = g_scr[:, rows : 2 * rows]
        core[3 * heads :, :] = far0[heads : 2 * heads, :]
        e = e_own[...].astype(F32) + unpack_rows(far0, 2 * heads, heads)
        if fast:
            transpose_into(eb_scr, e, spots, slice(None))
            e = eb_scr[...]
        else:
            e = mm(arrange[...], e.astype(BF16), NT)
        split_rows(jnp.concatenate([grad, e], axis=1), first, second)


def attend_back(h, fast, spots, sp, q, kt, k, vt, o, d, cs, tok_t, given, awaits=()):
    rows = kt[0].shape[2]
    total = 4 * rows
    width = tok_t.shape[0]
    heads = 3 * HD
    far = (2 * heads + 3 * heads // 2, 2 * heads, 2 * heads)[h]
    outs = [((heads, rows), BF16), ((far, rows), BF16), (((1, 2, 4)[h] * heads, rows), BF16)]
    if h == 0:
        outs += [((width, heads), BF16), ((heads, width), BF16)]
    else:
        outs += [((width // 2, 2 * heads), BF16)] * 2
    return run(
        functools.partial(attend_back_kernel, h, fast),
        12,
        20,
        (sp, spots),
        (*cs, tok_t, *given),
        outs,
        [
            pltpu.VMEM((128, total), BF16),
            pltpu.VMEM((128, total), BF16),
            pltpu.VMEM((HD, total), BF16),
            pltpu.VMEM((128, total), BF16),
            pltpu.VMEM((total, 128), BF16),
            pltpu.VMEM((128, total), BF16),
            pltpu.VMEM((total, 128), F32),
            pltpu.VMEM((128, total), F32),
            pltpu.VMEM((128, total), F32),
            pltpu.VMEM((heads, total), BF16),
            pltpu.VMEM((3 * heads, rows), BF16) if h == 0 else pltpu.VMEM((width, heads), F32),
            pltpu.SemaphoreType.DMA((25,)),
        ],
        awaits,
        apart=(*q, *kt, *k, *vt, *o, *d),
    )


def norm_parts(h):
    centred = h - jnp.mean(h, axis=-1, keepdims=True)
    inverse = lax.rsqrt(jnp.mean(centred * centred, axis=-1, keepdims=True) + 1e-05)
    return centred * inverse, inverse


def norm_back(grad, normed, inverse, gain):
    scaled = grad * gain
    return inverse * (
        scaled
        - jnp.mean(scaled, axis=-1, keepdims=True)
        - normed * jnp.mean(scaled * normed, axis=-1, keepdims=True)
    )


def sigmoid(v):
    return 0.5 + 0.5 * jnp.tanh(0.5 * v)


def out_kernel(a0, a1, a2, a3, w0, w1, w2, w3, tok_ref, gain_ref, bias_ref, low_ref, xhat_ref, inv_ref, *halves):
    w = jnp.concatenate([w0[...], w1[...], w2[...], w3[...]], axis=0)
    for half in range(2):
        at = slice(half * BLK, (half + 1) * BLK)
        a = jnp.concatenate([a0[:, at], a1[:, at], a2[:, at], a3[:, at]], axis=0)
        normed, inverse = norm_parts(tok_ref[at, :].astype(F32) + mm(a, w, TN))
        xhat_ref[at, :] = normed
        inv_ref[at, :] = jnp.broadcast_to(inverse, (BLK, 128))
        low = (normed * gain_ref[...] + bias_ref[...]).astype(BF16)
        low_ref[at, :] = low
        halves[half][...] = low


def out_project(a, w, tok, gain, bias, awaits=()):
    rows, width = tok.shape
    return run(
        out_kernel,
        3,
        10,
        (),
        (*a, *w, tok, gain, bias),
        (((rows, width), BF16), ((rows, width), F32), ((rows, 128), F32), *[((rows // 2, width), BF16)] * 2),
        awaits=awaits,
    )


PART_PLACES = ((0, 0, 0, 2), (0, 1, 0, 2), (0, 2, 0, 2), (0, 3, 0, 1), (0, 3, 1, 1)) + tuple((1, n, 0, 2) for n in range(4))


def gather_weights(at_ref, parts, wgu, wd, sem):
    copies = []
    for n, (part, (which, quarter, first, count)) in enumerate(zip(parts, PART_PLACES)):
        dst = (wgu, wd)[which]
        half = dst.shape[0] // 8
        spot = pl.ds(pl.multiple_of((at_ref[0] ^ quarter) * (2 * half) + first * half, half), count * half)
        copies.append(pltpu.make_async_copy(part, dst.at[spot, :], sem.at[n]))
    for c in copies:
        c.start()
    return copies


def mlp_rows(x, wg, wu, down, da, db, hid):
    gate, up = mm(x, wg), mm(x, wu)
    s = sigmoid(gate)
    act = gate * s
    low = (act * up).astype(BF16)
    da[...] = (up * (s + act * (1.0 - s))).astype(BF16)
    db[...] = act.astype(BF16)
    if hid is not None:
        hid[...] = low
    return mm(low, down)


def mlp_own_kernel(half0, half1, ml0, wgu, wd, acc, da, db, hid, ml1, sem):
    rows = ml0.shape[0]
    hidden = wd.shape[0]
    copies = []
    for n, half in enumerate((half0, half1)):
        copies.append(pltpu.make_async_copy(half, ml1.at[pl.ds(n * (rows // 2), rows // 2), :], sem.at[n]))
        copies[-1].start()
    for block, x in enumerate((ml0, ml1)):
        if block:
            for c in copies:
                c.wait()
        at = slice(block * rows, (block + 1) * rows)
        total = None
        for col in range(0, hidden, BLK):
            cols, ups = slice(col, col + BLK), slice(hidden + col, hidden + col + BLK)
            saved = [u.at[at, cols] for u in (da, db, hid)]
            part = mlp_rows(x[...], wgu[:, cols], wgu[:, ups], wd[cols, :], *saved)
            total = part if total is None else total + part
        acc[at, :] = total


def mlp_own(ml0, halves, wgu, wd, awaits=()):
    rows, width = ml0.shape
    hidden = wd.shape[0]
    saved = ((2 * rows, hidden), BF16)
    return run(
        mlp_own_kernel,
        5,
        10,
        (),
        (ml0, wgu, wd),
        [((2 * rows, width), F32)] + [saved] * 3 + [((rows, width), BF16)],
        [pltpu.SemaphoreType.DMA((2,))],
        awaits,
        apart=halves,
    )


def mlp_chunks(x, total, wgu, wd, da, db):
    hidden = wd.shape[0]
    for col in range(0, hidden, BLK):
        cols, ups = slice(col, col + BLK), slice(hidden + col, hidden + col + BLK)
        total += mlp_rows(x[...], wgu[:, cols], wgu[:, ups], wd[cols, :], da.at[:, cols], db.at[:, cols], None)
    return total


def mlp_far_kernel(at_ref, *refs):
    n_parts = len(PART_PLACES)
    ml1, acc, sib0, sib1, da, db, wgu, wd, sem = refs[n_parts:]
    rows = ml1.shape[0]
    for c in gather_weights(at_ref, refs[:n_parts], wgu, wd, sem):
        c.wait()
    total = mlp_chunks(ml1, acc[rows:, :], wgu, wd, da, db)
    sib0[...] = total[0 : rows // 2].astype(BF16)
    sib1[...] = total[rows // 2 :].astype(BF16)


def mlp_far(at, ml1, acc, parts, awaits=()):
    rows, width = ml1.shape
    hidden = parts[0].shape[1] // 2
    return run(
        mlp_far_kernel,
        4,
        10,
        (at,),
        (ml1, acc),
        [((rows // 2, width), BF16)] * 2
        + [((rows, hidden), BF16)] * 2
        + [((width, 2 * hidden), BF16), ((hidden, width), BF16)],
        [pltpu.SemaphoreType.DMA((len(parts),))],
        awaits,
        apart=parts,
    )


def mlp_last_kernel(ml0, acc, wgu, wd, own, da, db):
    own[...] = mlp_chunks(ml0, acc[0 : ml0.shape[0], :], wgu, wd, da, db)


def mlp_last(ml0, acc, wgu, wd):
    rows, width = ml0.shape
    saved = ((rows, wd.shape[0]), BF16)
    return run(mlp_last_kernel, 3, 10, (), (ml0, acc, wgu, wd), [((rows, width), F32), saved, saved])


def copies_of(src, dst, sem, rows=128):
    copies = []
    for n in range(src.shape[0] // rows):
        at = pl.ds(n * rows, rows)
        copies.append(pltpu.make_async_copy(src.at[at, :], dst.at[at, :], sem.at[n]))
        copies[-1].start()
    return copies


def mid_kernel(
    got, got_late, xhat_ref, own_ref, go_ref, g1, b1, g2, b2, out_ref, dh_ref, dm_ref, sums_ref, got_ref, sem
):
    gain_sum, bias_sum = 0.0, 0.0
    half = got.shape[0]
    copies = copies_of(got, got_ref, sem)
    copies += copies_of(got_late, got_ref.at[pl.ds(half, half), :], sem.at[pl.ds(half // 128, half // 128)])
    for start in range(0, xhat_ref.shape[0], 128):
        at = slice(start, start + 128)
        copies[start // 128].wait()
        mid = xhat_ref[at, :] * g1[...] + b1[...]
        normed, inverse = norm_parts(mid + (own_ref[at, :] + got_ref[at, :].astype(F32)))
        out_ref[at, :] = (normed * g2[...] + b2[...]).astype(BF16)
        grad = go_ref[at, :].astype(F32)
        dh = norm_back(grad, normed, inverse, g2[...])
        dh_ref[at, :] = dh
        dm_ref[at, :] = dh.astype(BF16)
        gain_sum += jnp.sum(grad * normed, axis=0, keepdims=True)
        bias_sum += jnp.sum(grad, axis=0, keepdims=True)
    sums_ref[0:1, :] = gain_sum
    sums_ref[1:2, :] = bias_sum


def mid_norm(xhat, own, got, out_grad, g1, b1, g2, b2, awaits=()):
    rows, width = xhat.shape
    return run(
        mid_kernel,
        3,
        8,
        (),
        (xhat, own, out_grad, g1, b1, g2, b2),
        (((rows, width), BF16), ((rows, width), F32), ((rows, width), BF16), ((2, width), F32)),
        [pltpu.VMEM((rows, width), BF16), pltpu.SemaphoreType.DMA((rows // 128,))],
        awaits,
        apart=got,
    )


def mlp_back_chunks(x, total, wgu, wd, da, db, at, dg=None, du=None):
    hidden = wd.shape[0]
    for col in range(0, hidden, BLK):
        cols, ups = slice(col, col + BLK), slice(hidden + col, hidden + col + BLK)
        dhid = mm(x[...], wd[cols, :], NT)
        dgate = (dhid * da[at, cols].astype(F32)).astype(BF16)
        dup = (dhid * db[at, cols].astype(F32)).astype(BF16)
        if dg is not None:
            dg[:, cols] = dgate
            du[:, cols] = dup
        part = mm(dgate, wgu[:, cols], NT) + mm(dup, wgu[:, ups], NT)
        total = part if total is None else total + part
    return total


def back_own_kernel(dm0, wgu, wd, da, db, acc, dg, du):
    acc[...] = mlp_back_chunks(dm0, None, wgu, wd, da, db, slice(0, dm0.shape[0]), dg, du)


def back_own(dm0, wgu, wd, da, db):
    rows, width = dm0.shape
    saved = ((rows, wd.shape[0]), BF16)
    return run(back_own_kernel, 3, 10, (), (dm0, wgu, wd, da, db), [((rows, width), F32), saved, saved])


def back_far_kernel(dm1_ref, wgu, wd, wgu_p, wd_p, da_o, db_o, da_p, db_p, sib0, sib1, dg, du, dm1, sem):
    rows = dm1.shape[0]
    copy = pltpu.make_async_copy(dm1_ref, dm1, sem)
    copy.start()
    copy.wait()
    total = mlp_back_chunks(dm1, None, wgu, wd, da_o, db_o, slice(rows, 2 * rows), dg, du)
    total = mlp_back_chunks(dm1, total, wgu_p, wd_p, da_p, db_p, slice(0, rows))
    sib0[...] = total[0 : rows // 2].astype(BF16)
    sib1[...] = total[rows // 2 :].astype(BF16)


def back_far(dm1, wgu, wd, wgu_p, wd_p, da_o, db_o, da_p, db_p):
    rows, width = dm1.shape
    saved = ((rows, wd.shape[0]), BF16)
    return run(
        back_far_kernel,
        6,
        12,
        (),
        (wgu, wd, wgu_p, wd_p, da_o, db_o, da_p, db_p),
        [((rows // 2, width), BF16)] * 2 + [saved, saved],
        [pltpu.VMEM((rows, width), BF16), pltpu.SemaphoreType.DMA],
        apart=(dm1,),
    )


def back_last_kernel(dm0, acc, wgu, wd, da, db, own):
    own[...] = mlp_back_chunks(dm0, acc[...], wgu, wd, da, db, slice(0, dm0.shape[0]))


def back_last(dm0, acc, wgu, wd, da, db):
    return run(back_last_kernel, 3, 10, (), (dm0, acc, wgu, wd, da, db), [(acc.shape, F32)])[0]


def first_norm_kernel(
    got_ref, got_late, dh2, own, xhat, inv, g1, sums2, a0, a1, a2, a3, w0, w1, w2, w3,
    dh1, d0, d1, d2, d3, ea, dat_scr, got, sem,
):
    gain_sum, bias_sum = 0.0, 0.0
    half = got_ref.shape[0]
    copies = copies_of(got_ref, got, sem) + copies_of(got_late, got.at[pl.ds(half, half), :], sem.at[pl.ds(half // 128, half // 128)])
    for start in range(0, dh2.shape[0], 128):
        at = slice(start, start + 128)
        copies[start // 128].wait()
        dmid = dh2[at, :] + (own[at, :] + got[at, :].astype(F32))
        normed = xhat[at, :]
        gain_sum += jnp.sum(dmid * normed, axis=0, keepdims=True)
        bias_sum += jnp.sum(dmid, axis=0, keepdims=True)
        grad = norm_back(dmid, normed, inv[at, 0:1], g1[...])
        dh1[at, :] = grad
        dat_scr[at, :] = grad.astype(BF16)
    sums = jnp.concatenate([gain_sum, bias_sum, sums2[...]], axis=0)
    high = sums.astype(BF16).astype(F32)
    both = jnp.concatenate([high, sums - high], axis=0)
    rest = jnp.concatenate([both[:, 512:], jnp.zeros((8, dh2.shape[0] - 256), F32)], axis=1)
    tail = jnp.concatenate([both[:, 0:512], rest], axis=0).astype(BF16)
    dat = dat_scr[...]
    for w, d in ((w0, d0), (w1, d1), (w2, d2), (w3, d3)):
        d[0:192, :] = mm(w[...], dat, NT).astype(BF16)
        d[192:208, :] = tail
    ea[...] = mm(jnp.concatenate([a0[...], a2[...]], axis=0), dat).astype(BF16)
    pack_rows(d1, 208, mm(jnp.concatenate([a1[...], a3[...]], axis=0), dat))


def pack_rows(dst, start, value):
    n = value.shape[0]
    rest = value[:, 512:]
    dst[start : start + n, :] = value[:, 0:512].astype(dst.dtype)
    dst[start + n : start + n + n // 2, :] = jnp.concatenate([rest[0 : n // 2], rest[n // 2 :]], axis=1).astype(dst.dtype)


def unpack_rows(src, start, n):
    rest = src[start + n : start + n + n // 2, :].astype(F32)
    rest = jnp.concatenate([rest[:, 0:256], rest[:, 256:]], axis=0)
    return jnp.concatenate([src[start : start + n, :].astype(F32), rest], axis=1)


def first_norm_back(dh2, own, got, xhat, inv, g1, sums2, a, w, awaits=()):
    rows, width = dh2.shape
    heads = a[0].shape[0]
    d = ((heads + 16, rows), BF16)
    return run(
        first_norm_kernel,
        5,
        12,
        (),
        (dh2, own, xhat, inv, g1, sums2, *a, *w),
        [((rows, width), F32), d, ((4 * heads + 16, rows), BF16), d, d, ((2 * heads, width), BF16)],
        [pltpu.VMEM((rows, width), BF16), pltpu.VMEM((rows, width), BF16), pltpu.SemaphoreType.DMA((rows // 128,))],
        awaits,
        apart=got,
    )


def far_kernel(
    fast, spots_a, spots_b, dm0, dm1, dm2, dm3, ml2, ml3, wgu, wd, hid_o,
    a_first, a_second, b_first, b_second, dg, du, dmt_a, dmt_b, hids,
):
    rows = dm0.shape[0]
    hidden = wd.shape[0]
    for p, u in enumerate((dm0, dm1, dm2, dm3)):
        cols = slice(p * rows, (p + 1) * rows)
        transpose_into(dmt_a, u[...], spots_a if fast else None, cols)
        transpose_into(dmt_b, u[...], spots_b if fast else None, cols)
    for col in range(0, hidden, BLK):
        cols, ups = slice(col, col + BLK), slice(hidden + col, hidden + col + BLK)
        hids[0 : 2 * rows, :] = hid_o[:, cols]
        for block, (x, dm) in enumerate(((ml2, dm2), (ml3, dm3))):
            at = slice(block * rows, (block + 1) * rows)
            gate, up, dhid = mm(x[...], wgu[:, cols]), mm(x[...], wgu[:, ups]), mm(dm[...], wd[cols, :], NT)
            s = sigmoid(gate)
            act = gate * s
            hids[(2 + block) * rows : (3 + block) * rows, :] = (act * up).astype(BF16)
            dg[at, cols] = (dhid * (up * (s + act * (1.0 - s)))).astype(BF16)
            du[at, cols] = (dhid * act).astype(BF16)
        for turned, first, second, start in ((dmt_a, a_first, a_second, 0), (dmt_b, b_first, b_second, hidden // 2)):
            lo, hi = max(col, start), min(col + BLK, start + hidden // 2)
            if lo < hi:
                there = slice(lo - start, hi - start)
                split_rows(mm(turned[...], hids[:, lo - col : hi - col]), first.at[:, there], second.at[:, there])


def far_rows(fast, spots, dm, ml, wgu, wd, hid, awaits=()):
    rows, width = dm[0].shape
    hidden = wd.shape[0]
    half = ((width // 2, hidden // 2), BF16)
    return run(
        functools.partial(far_kernel, fast),
        8,
        18,
        spots,
        (*dm, *ml, wgu, wd, hid),
        [half] * 4 + [((2 * rows, hidden), BF16)] * 2,
        [*[pltpu.VMEM((width, 4 * rows), BF16)] * 2, pltpu.VMEM((4 * rows, BLK), BF16)],
        awaits,
    )


def weight_kernel(
    fast, spots_a, spots_b, d0, d1, d2, d3, ml0, ml1, ml2, ml3, dg0, dg1, du0, du1, dg_f, du_f, da_first, da_second, db_first,
    db_second, a_first, a_second, b_first, b_second, total, mlt_a, mlt_b, tail_scr, sem,
):
    rows = ml0.shape[0]
    hidden = dg0.shape[1]
    copies = [
        pltpu.make_async_copy(d.at[pl.ds(3 * HD, 16), :], tail_scr.at[p], sem.at[p]) for p, d in enumerate((d0, d1, d2, d3))
    ]
    for c in copies:
        c.start()
    for p, u in enumerate((ml0, ml1, ml2, ml3)):
        cols = slice(p * rows, (p + 1) * rows)
        transpose_into(mlt_a, u[...], spots_a if fast else None, cols)
        transpose_into(mlt_b, u[...], spots_b if fast else None, cols)
    for src, dst in ((da_first, a_first), (da_second, a_second), (db_first, b_first), (db_second, b_second)):
        dst[0 : src.shape[0], hidden:] = src[...]
    wide = slice(0, hidden)
    half = a_first.shape[0]
    for turned, near, late, far, first, second in (
        (mlt_a, dg0, dg1, dg_f, a_first, a_second),
        (mlt_b, du0, du1, du_f, b_first, b_second),
    ):
        grad = mm(turned[:, 0:rows], near[...]) + mm(turned[:, rows : 2 * rows], late[...])
        grad += mm(turned[:, 2 * rows :], far[...])
        split_rows(grad, first.at[:, wide], second.at[0:half, wide])
    for c in copies:
        c.wait()
    sums = [tail_scr[p].astype(F32) for p in range(4)]
    joined = (sums[0] + sums[1]) + (sums[2] + sums[3])
    whole = jnp.concatenate([joined[0:4] + joined[4:8], (joined[8:12] + joined[12:16])[:, 0:256]], axis=1)
    high = whole.astype(BF16).astype(F32)
    low = (whole - high).astype(BF16).astype(F32)
    total[...] = high + low
    rest = jnp.zeros((8, hidden), F32)
    a_second[half : half + EXTRA, wide] = jnp.concatenate([high, low, rest], axis=0).astype(BF16)
    a_second[half : half + EXTRA, hidden:] = jnp.zeros((EXTRA, a_second.shape[1] - hidden), BF16)


def weight_grads(fast, spots, d, ml, near, far, down, awaits=()):
    rows, width = ml[0].shape
    hidden = near[0].shape[1]
    chain = ((width // 2, hidden + hidden // 2), BF16)
    return run(
        functools.partial(weight_kernel, fast),
        6,
        16,
        spots,
        (*ml, *near, *far, *down),
        [chain, ((width // 2 + EXTRA, hidden + hidden // 2), BF16), chain, chain, ((4, width), F32)],
        [
            *[pltpu.VMEM((width, 4 * rows), BF16)] * 2,
            pltpu.VMEM((4, 16, rows), BF16),
            pltpu.SemaphoreType.DMA((4,)),
        ],
        awaits,
        apart=d,
    )


def join_kernel(core, got1, got2, out, sem):
    heads = 3 * HD
    pieces = ((core, 0, 4 * heads), (got1, heads, heads), (got2, heads, heads))
    copies, at = [], 0
    for n, (src, start, count) in enumerate(pieces):
        copies.append(pltpu.make_async_copy(src.at[pl.ds(start, count), :], out.at[pl.ds(at, count), :], sem.at[n]))
        copies[-1].start()
        at += count
    for c in copies:
        c.wait()


def join(core, got1, got2):
    return run(
        join_kernel,
        1,
        4,
        (),
        (),
        [((18 * HD, core.shape[1]), BF16)],
        [pltpu.SemaphoreType.DMA((3,))],
        apart=(core, got1, got2),
    )[0]


def by_heads(w):
    heads = 3 * HD
    return jnp.concatenate([w[c * heads + h * HD : c * heads + (h + 1) * HD, :] for h in range(3) for c in range(3)], axis=0)


def near_kernel(f0, f1, f2, dh1, n0, n1, n2, w0, w2, out, far, sem):
    heads = 3 * HD
    copies = []
    for n, f in enumerate((f0, f1, f2)):
        spot = pl.ds(n * heads, heads)
        copies.append(pltpu.make_async_copy(f.at[pl.ds(0, heads), :], far.at[spot, :], sem.at[n]))
        copies[-1].start()
    near = jnp.concatenate([n0[...], n1[...], n2[...]], axis=0)
    out[...] = dh1[...] + mm(near, by_heads(w0), TN)
    for c in copies:
        c.wait()
    out[...] += mm(far[...], by_heads(w2), TN)


def input_near(dh1, near, far, w0, w2):
    return run(
        near_kernel,
        3,
        12,
        (),
        (dh1, *near, w0, w2),
        [(dh1.shape, F32)],
        [pltpu.VMEM((9 * HD, dh1.shape[0]), BF16), pltpu.SemaphoreType.DMA((3,))],
        apart=far,
    )[0]


def input_kernel(core_ref, before, w1, w3, out, core, total, sem):
    arrival = pltpu.make_async_copy(core_ref, core, sem.at[0])
    arrival.start()
    w = jnp.concatenate([by_heads(w1), by_heads(w3)], axis=0)
    arrival.wait()
    copies = []
    for half in range(before.shape[0] // BLK):
        at = slice(half * BLK, (half + 1) * BLK)
        total[at, :] = before[at, :] + mm(core[:, at], w, TN)
        spot = pl.ds(half * BLK, BLK)
        copies.append(pltpu.make_async_copy(total.at[spot, :], out.at[spot, :], sem.at[1 + half]))
        copies[-1].start()
    for c in copies:
        c.wait()


def input_back(before, core, w1, w3):
    return run(
        input_kernel,
        3,
        14,
        (),
        (before, w1, w3),
        [(before.shape, F32)],
        [
            pltpu.VMEM(core.shape, BF16),
            pltpu.VMEM(before.shape, F32),
            pltpu.SemaphoreType.DMA((1 + before.shape[0] // BLK,)),
        ],
        apart=(core,),
        hbm=(0,),
    )[0]


def split_halves(v):
    return v[0 : v.shape[0] // 2], v[v.shape[0] // 2 :]


def swap(v, bit, axis="tensor"):
    n = lax.axis_size(axis)
    return lax.ppermute(v, axis, [(i, i ^ bit) for i in range(n)])


def bits_of(n):
    return n.bit_length() - 1


def spots_of(order, n):
    block = jnp.arange(n, dtype=jnp.int32) ^ lax.axis_index("dp")
    spot = jnp.zeros((n,), jnp.int32)
    for s, bit in enumerate(order):
        spot = spot + (((block >> bit) & 1) << (len(order) - 1 - s))
    return spot


def last_kernel(chains, kind, *refs):
    count = sum(chains)
    parts, outs, scrs, sem = refs[:count], refs[count:-count - 1], refs[-count - 1 : -1], refs[-1]
    copies = []
    for n, (part, scr) in enumerate(zip(parts, scrs)):
        copies.append(pltpu.make_async_copy(part.at[pl.ds(0, scr.shape[0]), :], scr, sem.at[n]))
        copies[-1].start()
    for c in copies:
        c.wait()
    sums, at = [], 0
    for length in chains:
        sums.append(sum(scr[...].astype(F32) for scr in scrs[at : at + length]))
        at += length
    if kind == "mlp":
        gu, down = outs
        width = down.shape[1]
        one, two = sums[0:2]
        if len(sums) > 2:
            one += sums[2][:, 0 : one.shape[1]]
            two += sums[2][:, one.shape[1] :]
        gu[:, 0, :] = one[:, 0:width]
        gu[:, 1, :] = two[:, 0:width]
        down[...] = jnp.concatenate([one[:, width:], two[:, width:]], axis=1)
    else:
        qkv, out = outs
        total = jnp.concatenate(sums[0:2], axis=1)
        if len(sums) > 2:
            total += sums[2]
        for c in range(3):
            qkv[c] = jnp.concatenate([total[:, (3 * h + c) * HD : (3 * h + c + 1) * HD] for h in range(3)], axis=1)
        out[...] = total[:, 9 * HD :].T


def last_sums(kind, rows, chains, outs):
    parts = [part for chain in chains for part in chain]
    return run(
        functools.partial(last_kernel, [len(chain) for chain in chains], kind),
        2,
        8,
        (),
        (),
        outs,
        [pltpu.VMEM((rows, part.shape[1]), BF16) for part in parts] + [pltpu.SemaphoreType.DMA((len(parts),))],
        apart=parts,
    )


def in_two(v):
    high = lax.reduce_precision(v, 8, 7)
    low = lax.reduce_precision(v - high, 8, 7)
    return jnp.concatenate([high, low], axis=0), high + low


class scatter_steps:
    def __init__(self, first, second, order, ride=None):
        self.parts, self.order, self.step = [first], order, 0
        self.sent, self.ride, self.base = second, ride, None
        self.extra = 0 if ride is None else EXTRA

    def advance(self):
        self.base = self.ride
        self.parts.append(swap(self.sent, 1 << self.order[self.step], "dp"))
        self.step += 1
        self.next_sent()
        return self.parts[-1]

    def carried(self, got):
        n, width = self.base.shape
        rows = got[got.shape[0] - EXTRA : got.shape[0] - EXTRA + 2 * n, 0:width].astype(F32)
        return self.base + (rows[0:n] + rows[n:])

    def next_sent(self):
        if self.extra:
            self.ride = self.carried(self.parts[-1])
        if self.step < len(self.order):
            length = self.parts[-1].shape[0] - self.extra
            sent = sum(u[length // 2 : length].astype(F32) for u in self.parts)
            if self.extra:
                rows, self.ride = in_two(self.ride)
                padding = ((0, EXTRA - rows.shape[0]), (0, sent.shape[1] - rows.shape[1]))
                sent = jnp.concatenate([sent, jnp.pad(rows, padding)], axis=0)
            self.sent = sent.astype(BF16)

    def all_parts(self):
        while self.step < len(self.order):
            self.advance()
        return self.parts


def advance_together(chains):
    bits = {chain.order[chain.step] for chain in chains}
    if len(bits) > 1 or any(chain.step < len(chain.order) - 1 for chain in chains):
        return None
    tall = max(chain.sent.shape[0] for chain in chains)
    sent = [jnp.pad(chain.sent, ((0, tall - chain.sent.shape[0]), (0, 0))) for chain in chains]
    got = swap(jnp.concatenate(sent, axis=1), 1 << bits.pop(), "dp")
    for chain in chains:
        chain.step += 1
        chain.base = chain.ride
    return got


def first_sums(chains, rows):
    return [sum(part[0:rows].astype(F32) for part in chain) for chain in chains]


def quarter_of(w):
    rows = w.shape[0] // 4
    return lax.dynamic_slice_in_dim(w, (lax.axis_index("dp") % 4) * rows, rows, axis=0)


def local(
    tokens,
    doc_lengths,
    key_mask,
    qkv_weight,
    out_weight,
    gate_up_weight,
    down_weight,
    norm1_gain,
    norm1_bias,
    norm2_gain,
    norm2_bias,
    out_grad,
):
    rows, width = tokens.shape
    flags = jnp.pad(key_mask.astype(BF16).reshape(1, rows), ((0, EXTRA - 1), (0, width - rows)))
    tok0 = jnp.concatenate([tokens, flags], axis=0)
    tok1 = swap(tok0, 1)
    tok2 = swap(tok0, 2)
    sp = jnp.concatenate([doc_lengths[0], lax.axis_index("tensor").reshape(1)]).astype(jnp.int32)
    quarter = (lax.axis_index("dp") % 4).reshape(1).astype(jnp.int32)
    freqs = 1000.0 ** (-(jnp.arange(HD // 2, dtype=F32) * 2.0 / HD))
    freqs = jnp.broadcast_to(freqs[:, None], (HD // 2, 128))
    wt = jnp.transpose(qkv_weight, (1, 2, 0)).reshape(-1, width)

    n_dp = lax.axis_size("dp")
    fast = (width // n_dp) % 16 == 0
    order = list(range(bits_of(n_dp)))
    order_b = order[1:2] + order[0:1] + order[2:]
    spots, spots_b = (spots_of(u, n_dp) for u in (order, order_b))

    def arranged(v, at):
        if fast:
            return v
        blocks = v.reshape(v.shape[0], n_dp, width // n_dp)
        return jnp.take(blocks, jnp.argsort(at), axis=1).reshape(v.shape)

    ORDER.last = ()
    wo0 = out_weight
    wo1, wt1 = swap(wo0, 1), swap(wt, 1)
    wgu = gate_up_weight.reshape(width, -1)
    part_b = quarter_of(wgu)
    part_a = jnp.concatenate([quarter_of(down_weight), wo0], axis=0)

    proj = [project(0, sp, freqs, tok0, wt), project(1, sp, freqs, tok1, wt, awaits=(part_a, part_b, wt1))]
    tok2, part_b = gate(tok2, part_b)
    tok3, pb0 = swap(tok2, 1), swap(part_b, 2)
    tok = (tok0, tok1, tok2, tok3)
    proj.append(project(2, sp, freqs, tok2, wt))
    *more, part_a = project(3, sp, freqs, tok3, wt, carry=(part_a,))
    proj.append(more)
    pa0 = swap(part_a, 2)
    qt, kt, k, vt, cs = zip(*proj)
    o2, o3, q2, q3 = attend(1, sp, qt, k, vt, (wo1,))
    o2, pb0 = gate(o2, pb0)
    pb1, pb2, g2 = swap(pb0, 1, "dp"), swap(pb0, 2, "dp"), swap(o2, 2)
    o0, o1, q0, q1 = attend(0, sp, qt, k, vt)
    half2, half1 = park((), ((pb2, 0), (pb1, 1)))
    half2, half1, o3, pa0 = gate(half2, half1, o3, pa0)
    g3, pb3 = swap(o3, 3), (swap(half2, 1, "dp"), swap(half1, 2, "dp"))
    (tok_t,) = transposed(fast, (spots,), tok, rows)
    if not fast:
        tok_t = arranged(tok_t.T, spots).T
    pa0, wo2 = park((), ((pa0, 0), (pa0, 1)))
    o1, pa0, wo2 = gate(o1, pa0, wo2, awaits=(g2, g3, *pb3))
    g1, wo3 = swap(o1, 1), swap(wo2, 1)
    pa1, pa2, pa3 = swap(pa0, 1, "dp"), swap(pa0, 2, "dp"), swap(pa0, 3, "dp")
    wo = (wo0, wo1, wo2, wo3)

    gain1, bias1, gain2, bias2 = (u.reshape(1, width) for u in (norm1_gain, norm1_bias, norm2_gain, norm2_bias))
    ml0, xhat1, inv1, *halves = out_project((o0, g1, g2, g3), wo, tokens, gain1, bias1)
    ml2 = swap(ml0, 2)
    acc, da_o, db_o, hid_o, ml1 = mlp_own(ml0, [swap(u, 1) for u in halves], wgu, down_weight)
    parts = (pb0, pb1, pb2, *pb3, pa0, pa1, pa2, pa3)
    kept = park((*kt, *k, *vt, q0, q1, q2, q3, tok_t))
    kt, k, vt, (q0, q1, q2, q3, tok_t) = kept[0:4], kept[4:8], kept[8:12], kept[12:17]
    sib0, sib1, da_1, db_1, wgu_p, wd_p = mlp_far(quarter, ml1, acc, parts)
    own, da_0, db_0 = mlp_last(ml0, acc, wgu_p, wd_p)
    gate(awaits=(ml2,))
    output, dh2, dm0, sums2 = mid_norm(
        xhat1, own, (swap(sib0, 1), swap(sib1, 1)), out_grad, gain1, bias1, gain2, bias2
    )
    dm0, ml2 = gate(dm0, ml2)
    dm1, dm2 = swap(dm0, 1), swap(dm0, 2)
    ml3 = swap(ml2, 1)
    acc, dg_0, du_0 = back_own(dm0, wgu, down_weight, da_o, db_o)
    sib0, sib1, dg_1, du_1 = back_far(dm1, wgu, down_weight, wgu_p, wd_p, da_o, db_o, da_1, db_1)
    own = back_last(dm0, acc, wgu_p, wd_p, da_0, db_0)
    dh1, d0, d1, d2, d3, ea = first_norm_back(
        dh2, own, (swap(sib0, 1), swap(sib1, 1)), xhat1, inv1, gain1, sums2, (o0, g1, g2, g3), wo, (ml3,)
    )
    d1, d2, d3, dm2 = gate(d1, d2, d3, dm2)
    dm3 = swap(dm2, 1)
    d = (d0, swap(d1, 1), swap(d2, 2), swap(d3, 3))
    ml, dm, both = (ml0, ml1, ml2, ml3), (dm0, dm1, dm2, dm3), (spots, spots_b)
    *down, dg_f, du_f = far_rows(fast, both, dm, ml[2:], wgu, down_weight, hid_o)
    (wt,) = gate(wt, awaits=d[1:])
    wt2 = swap(wt, 2)
    a_first, a_second, b_first, b_second, sums = weight_grads(
        fast, both, d, ml, (dg_0, dg_1, du_0, du_1), (dg_f, du_f), down
    )
    if not fast:
        tail = a_second[width // 2 :]
        a_first, a_second = split_halves(arranged(jnp.concatenate([a_first, a_second[0 : width // 2]]).T, spots).T)
        a_second = jnp.concatenate([a_second, tail])
        b_first, b_second = split_halves(arranged(jnp.concatenate([b_first, b_second]).T, spots_b).T)
    a_second, b_second = gate(a_second, b_second)
    chain_a = scatter_steps(a_first, a_second, order, sums)
    chain_b = scatter_steps(b_first, b_second, order_b)
    a_got, b_got = chain_a.advance(), chain_b.advance()

    arrange = jnp.zeros((8, 128), BF16)
    if not fast:
        column = jnp.arange(width)
        target = spots[column // (width // n_dp)] * (width // n_dp) + column % (width // n_dp)
        arrange = (column[:, None] == target[None, :]).astype(BF16)
    back = functools.partial(
        attend_back,
        fast=fast,
        spots=spots,
        sp=sp,
        q=(q0, q1, q2, q3),
        kt=kt,
        k=k,
        vt=vt,
        o=(o0, o1, o2, o3),
        d=d,
        cs=cs,
        tok_t=tok_t,
    )
    near0, far0, core0, grad0, e_own = back(0, given=(ea,))
    far0, chain_a.parts[-1], chain_b.parts[-1], wt2 = gate(far0, a_got, b_got, wt2)
    for chain in (chain_a, chain_b):
        chain.next_sent()
    a_got, b_got, got0 = chain_a.advance(), chain_b.advance(), swap(far0, 2)
    near1, far1, core1, first, second = back(1, given=(core0, grad0))
    far1, second, chain_a.parts[-1], chain_b.parts[-1], wt2 = gate(far1, second, a_got, b_got, wt2)
    for chain in (chain_a, chain_b):
        chain.next_sent()
    c1 = scatter_steps(first, second, order)
    c1_got, mlp3 = c1.advance(), advance_together((chain_a, chain_b))
    wt3 = swap(wt2, 1)
    got1 = swap(far1, 2)
    near2, far2, core2, first, second = back(2, given=(core1, got0, e_own, arrange))
    far2, second, c1.parts[-1] = gate(far2, second, c1_got, awaits=(got1, wt3))
    c1.next_sent()
    c2 = scatter_steps(first, second, order)
    c2_got, got2 = c2.advance(), swap(far2, 2)
    c2.parts[-1], *late = gate(c2_got, *([] if mlp3 is None else [mlp3]))
    c2.next_sent()
    c2_got, c1_got = c2.advance(), c1.advance()
    mlp, shard = [chain_a.all_parts(), chain_b.all_parts()], width // n_dp
    if mlp3 is not None:
        mlp.append([mlp3])
    core = swap(join(core2, got1, got2), 1)
    input_grad = input_near(dh1, (near0, near1, near2), (got0, got1, got2), wt, wt2)
    c2.parts[-1], c1.parts[-1] = gate(c2_got, c1_got)
    c2.next_sent()
    c1.next_sent()
    if late:
        chain_a.ride = chain_a.carried(late[0])
        mlp[-1] = late
    both = advance_together((c1, c2))
    attention = [c1.all_parts(), c2.all_parts()]
    if both is not None:
        attention.append([both])
    input_grad = input_back(input_grad, core, wt1, wt3)
    sums = chain_a.ride
    if fast:
        hidden = down_weight.shape[0]
        gu_part, down_part = last_sums("mlp", shard, mlp, [((shard, 2, hidden), F32), ((shard, hidden), F32)])
        qkv_part, out_part = last_sums(
            "attention", shard, attention, [((3, shard, 3 * HD), F32), ((3 * HD, shard), F32)]
        )
        qkv_part = jnp.transpose(qkv_part, (1, 0, 2))
    else:
        one, two = first_sums(mlp, shard)
        gu_part = jnp.stack([one[:, 0:width], two[:, 0:width]], axis=1)
        down_part = jnp.concatenate([one[:, width:], two[:, width:]], axis=1)
        total = jnp.concatenate(first_sums(attention, shard), axis=1)
        out_part = total[:, 9 * HD :].T
        qkv_part = jnp.transpose(total[:, 0 : 9 * HD].reshape(shard, 3, 3, HD), (0, 2, 1, 3)).reshape(shard, 3, 3 * HD)
    return (
        output,
        input_grad,
        qkv_part,
        out_part,
        gu_part,
        down_part.T,
        sums[0],
        sums[1],
        sums[2],
        sums[3],
    )


def solution(mesh):
    placed = (
        P(("dp", "tensor"), None),
        P("dp", None),
        P(("dp", "tensor")),
        P(None, None, "tensor"),
        P("tensor", None),
        P(None, None, "tensor"),
        P("tensor", None),
        P(),
        P(),
        P(),
        P(),
        P(("dp", "tensor"), None),
    )
    return jax.shard_map(
        local,
        mesh=mesh,
        in_specs=placed,
        out_specs=(
            P(("dp", "tensor"), None),
            P(("dp", "tensor"), None),
            P("dp", None, "tensor"),
            P("tensor", "dp"),
            P("dp", None, "tensor"),
            P("tensor", "dp"),
            P(),
            P(),
            P(),
            P(),
        ),
        check_vma=False,
    )
```

```python
import functools
import math

import jax
import jax.numpy as jnp
from jax import lax
from jax.experimental import pallas as pl
from jax.experimental.pallas import tpu as pltpu
from jax.sharding import PartitionSpec as P

HD = 64
F32 = jnp.float32
BF16 = jnp.bfloat16
BIG = -1e30
BLK = 256
WINDOWS = (640, 1664, 2048)
SCALE = 0.15
EXTRA = 16
NN = (((1,), (0,)), ((), ()))
NT = (((1,), (1,)), ((), ()))
TN = (((0,), (0,)), ((), ()))


def mm(a, b, dims=NN):
    return lax.dot_general(a, b, dims, preferred_element_type=F32)


class Order:
    def __init__(self):
        self.last = ()


ORDER = Order()


def run(kernel, us, mib, scalars, args, outs, scratch=(), awaits=(), carry=(), apart=(), hbm=()):
    in_vmem = pl.BlockSpec(memory_space=pltpu.VMEM)
    anywhere = pl.BlockSpec(memory_space=pl.ANY)
    awaits = (*awaits, *ORDER.last)
    sizes = [math.prod(shape) for n, (shape, dtype) in enumerate(outs) if n not in hbm]
    token = not sizes or min(sizes) > 1 << 15
    if token:
        inner, outs = kernel, [*outs, ((8, 128), F32)]

        def kernel(*refs):
            spot = n_in + len(outs) - 1
            refs[spot][...] = jnp.zeros((8, 128), F32)
            inner(*refs[:spot], *refs[spot + 1 :])

    n_in = len(scalars) + len(apart) + len(args)
    n_skip, n_out = len(awaits) + len(carry), len(outs)

    def body(*refs):
        rest = refs[n_in + n_skip :]
        kernel(*refs[:n_in], *rest[:n_out], *rest[n_out + len(carry) :])

    results = pl.pallas_call(
        body,
        in_specs=[pl.BlockSpec(memory_space=pltpu.SMEM)] * len(scalars)
        + [anywhere] * len(apart)
        + [in_vmem] * len(args)
        + [anywhere] * n_skip,
        out_specs=[pl.BlockSpec(memory_space=pltpu.HBM) if n in hbm else in_vmem for n in range(n_out)]
        + [anywhere] * len(carry),
        out_shape=[jax.ShapeDtypeStruct(*o) for o in outs] + [jax.ShapeDtypeStruct(c.shape, c.dtype) for c in carry],
        scratch_shapes=list(scratch),
        input_output_aliases={n_in + len(awaits) + i: n_out + i for i in range(len(carry))},
        compiler_params=pltpu.CompilerParams(vmem_limit_bytes=mib << 20),
        cost_estimate=pl.CostEstimate(flops=int(us * SCALE * 1.1e9), bytes_accessed=1 << 18, transcendentals=0),
    )(*scalars, *apart, *args, *awaits, *carry)
    ORDER.last = (min((r for n, r in enumerate(results[:n_out]) if n not in hbm), key=lambda r: r.size),)
    if token:
        results = [*results[: n_out - 1], *results[n_out:]]
    return results


def gate_kernel(out):
    out[...] = jnp.zeros(out.shape, F32)


def gate(*arrays, awaits=()):
    return run(gate_kernel, 0.1, 4, (), (), [((8, 128), F32)], awaits=awaits, carry=arrays)[1:]


def park_kernel(places, *refs):
    count = len(places)
    copies = []
    for n, (first, rows) in enumerate(places):
        src = refs[n] if rows is None else refs[n].at[pl.ds(first, rows), :]
        copies.append(pltpu.make_async_copy(src, refs[count + n], refs[-1].at[n]))
        copies[-1].start()
    for c in copies:
        c.wait()


def park(arrays, halves=()):
    places = [(0, None) for _ in arrays] + [(n * (u.shape[0] // 2), u.shape[0] // 2) for u, n in halves]
    outs = [(u.shape, u.dtype) for u in arrays] + [((u.shape[0] // 2, u.shape[1]), u.dtype) for u, n in halves]
    return run(
        functools.partial(park_kernel, places),
        3,
        4,
        (),
        (),
        outs,
        [pltpu.SemaphoreType.DMA((len(outs),))],
        apart=(*arrays, *[u for u, n in halves]),
        hbm=range(len(outs)),
    )


def split3(v):
    top = v.astype(BF16).astype(F32)
    rest = v - top
    middle = rest.astype(BF16).astype(F32)
    return top, middle, rest - middle


def split_rows(value, first, second):
    half = first.shape[0]
    first[...] = value[0:half].astype(first.dtype)
    second[...] = value[half:].astype(second.dtype)


def transpose_into(dst, value, spots, cols):
    turned = value.T
    if spots is None:
        dst[:, cols] = turned
        return
    count = spots.shape[0]
    rows = turned.shape[0] // count
    for b in range(count):
        dst[pl.ds(pl.multiple_of(spots[b] * rows, rows), rows), cols] = turned[b * rows : (b + 1) * rows]


def transpose_kernel(fast, *refs):
    count = (len(refs) - 4) // 2
    spots, tokens, outs = refs[:count], refs[count : count + 4], refs[count + 4 :]
    rows = outs[0].shape[1] // 4
    for p, t in enumerate(tokens):
        for spot, out in zip(spots, outs):
            transpose_into(out, t[0:rows, :], spot if fast else None, slice(p * rows, (p + 1) * rows))


def transposed(fast, spots, pieces, rows):
    width = pieces[0].shape[1]
    outs = [((width, 4 * rows), BF16)] * len(spots)
    return run(functools.partial(transpose_kernel, fast), 2, 8, spots, pieces, outs)


def project_kernel(piece, sp_ref, freq_ref, tok_ref, w_ref, qt_ref, kt_ref, k_ref, vt_ref, cs_ref):
    n = tok_ref.shape[0] - EXTRA
    place = (sp_ref[8] ^ piece) * n + lax.broadcasted_iota(jnp.int32, (1, n), 1)
    seg = jnp.zeros((1, n), jnp.int32)
    pos = place
    end = 0
    for d in range(8):
        length = sp_ref[d]
        end = end + length
        past = place >= end
        seg += past.astype(jnp.int32)
        pos -= jnp.where(past, length, 0)
    angles = pos.astype(F32) * freq_ref[:, 0:1]
    cosine, sine = jnp.cos(angles), jnp.sin(angles)
    cs_ref[0:32, :] = cosine
    cs_ref[32:64, :] = sine
    idx = lax.broadcasted_iota(jnp.int32, (64, n), 0)
    which = jnp.where(idx < 19, idx - 8, idx - 19)
    bit = (jnp.broadcast_to(place, (64, n)) >> jnp.clip(which, 0, 10)) & 1
    flipped = jnp.where(idx < 19, bit, 1 - bit).astype(F32)
    same = (idx == seg).astype(F32)
    coded = (idx >= 8) & (idx < 30)
    invalid = 1.0 - tok_ref[n : n + EXTRA, 0:n].astype(F32)[0:1]
    q_tail = jnp.where(idx < 8, BIG * (1.0 - same), jnp.where(coded, BIG * flipped, 0.0))
    k_tail = jnp.where(idx < 8, same, jnp.where(coded, invalid * (1.0 - flipped), 0.0))
    k_tail = jnp.where((idx >= 32) & (idx < 35), 1.0, k_tail)
    v_tail = jnp.where(idx < 3, 1.0, 0.0)
    y = mm(w_ref[...], tok_ref[0:n, :], NT)

    def rotated(at):
        a, b = y[at : at + 32], y[at + 32 : at + 64]
        return jnp.concatenate([a * cosine - b * sine, b * cosine + a * sine], axis=0)

    for h in range(3):
        qt_ref[h] = jnp.concatenate([rotated(h * HD) * 0.125, q_tail], axis=0).astype(BF16)
        key = jnp.concatenate([rotated(192 + h * HD), k_tail], axis=0)
        kt_ref[h] = key.astype(BF16)
        k_ref[h] = key.T.astype(BF16)
        vt_ref[h] = jnp.concatenate([y[384 + h * HD : 448 + h * HD], v_tail], axis=0).astype(BF16)


def project(piece, sp, freqs, tok, w, awaits=(), carry=()):
    rows = tok.shape[0] - EXTRA
    wide, tall = ((3, 128, rows), BF16), ((3, rows, 128), BF16)
    return run(
        functools.partial(project_kernel, piece),
        2.5,
        10,
        (sp,),
        (freqs, tok, w),
        (wide, wide, tall, wide, ((HD, rows), F32)),
        awaits=awaits,
        carry=carry,
    )


def window_of(sp_ref, block, total):
    a = block * BLK
    b = a + BLK - 1
    first, last, end = 0, 0, 0
    for d in range(8):
        begin, end = end, end + sp_ref[d]
        first = jnp.where(begin <= a, begin, first)
        last = jnp.where(begin <= b, end, last)
    start = (first // 128) * 128
    kind = jnp.where(last - start <= WINDOWS[0], 0, jnp.where(last - start <= WINDOWS[1], 1, 2))
    size = jnp.where(kind == 0, WINDOWS[0], jnp.where(kind == 1, WINDOWS[1], WINDOWS[2]))
    return pl.multiple_of(jnp.minimum(start, total - size), 128), kind


def place_of(sp_ref, piece, rows):
    return pl.ds(pl.multiple_of((sp_ref[8] ^ piece) * rows, rows), rows)


def attend_kernel(base, sp_ref, qa, qb, k0, k1, k2, k3, v0, v1, v2, v3, oa, ob, ba, bb, k_scr, v_scr, s_scr, q_scr, o_scr):
    rows = qa.shape[2]
    total = 4 * rows
    for p, (k, v) in enumerate(((k0, v0), (k1, v1), (k2, v2), (k3, v3))):
        at = place_of(sp_ref, p, rows)
        k_scr[:, at, :] = k[...]
        v_scr[:, :, at] = v[...]
    for n in range(4):
        q_scr[n] = (qa, qb)[n // 2][:, :, (n % 2) * BLK : (n % 2 + 1) * BLK]

    def q_block(i, carry):
        start, kind = window_of(sp_ref, (base + i) ^ (2 * sp_ref[8]), total)

        def scores(h, size):
            s = mm(k_scr[h, pl.ds(start, size), :], q_scr[i, h])
            s_scr[h, 0:size, :] = s
            return jnp.max(s, axis=0, keepdims=True)

        def weigh(h, size, top):
            p = jnp.exp(s_scr[h, 0:size, :] - top).astype(BF16)
            acc = mm(v_scr[h, :, pl.ds(start, size)], p)
            norm = acc[64:65]
            o_scr[i, h * HD : (h + 1) * HD, :] = (acc[0:64] / norm).astype(BF16)
            parts = split3(-(top + jnp.log(norm)))
            q_scr[i, h, 96:112, :] = jnp.concatenate([*parts, jnp.zeros((13, BLK), F32)], axis=0).astype(BF16)

        for mode, size in enumerate(WINDOWS):

            @pl.when(kind == mode)
            def _():
                t0 = scores(0, size)
                t1 = scores(1, size)
                weigh(0, size, t0)
                t2 = scores(2, size)
                weigh(1, size, t1)
                weigh(2, size, t2)

        return carry

    lax.fori_loop(0, 4, q_block, 0)
    for n in range(4):
        at = slice((n % 2) * BLK, (n % 2 + 1) * BLK)
        (oa, ob)[n // 2][:, at] = o_scr[n]
        (ba, bb)[n // 2][:, :, at] = q_scr[n]


def attend(half, sp, qt, k, vt, awaits=(), carry=()):
    rows = qt[0].shape[2]
    total = 4 * rows
    out, back = ((3 * HD, rows), BF16), ((3, 128, rows), BF16)
    return run(
        functools.partial(attend_kernel, half * 4),
        8,
        18,
        (sp,),
        (qt[2 * half], qt[2 * half + 1], *k, *vt),
        (out, out, back, back),
        [
            pltpu.VMEM((3, total, 128), BF16),
            pltpu.VMEM((3, 128, total), BF16),
            pltpu.VMEM((3, total, BLK), F32),
            pltpu.VMEM((4, 3, 128, BLK), BF16),
            pltpu.VMEM((4, 3 * HD, BLK), BF16),
        ],
        awaits,
        carry,
    )


def attend_back_kernel(h, fast, sp_ref, spots, *refs):
    q_refs, kt_refs, k_refs, vt_refs, o_refs, d_refs = (refs[4 * n : 4 * n + 4] for n in range(6))
    n_given = (1, 2, 4)[h]
    cs_refs, tok_t, given, outs = refs[24:28], refs[28], refs[29 : 29 + n_given], refs[29 + n_given : -12]
    q_scr, do_scr, o_scr, kt_scr, k_scr, vt_scr, dq_scr, dk_scr, dv_scr, g_scr, eb_scr, sem = refs[-12:]
    rows = kt_refs[0].shape[2]
    total = 4 * rows
    head = pl.ds(h * HD, HD)
    copies = []
    for p in range(4):
        spot, at = place_of(sp_ref, p, rows), pl.ds(p * rows, rows)
        copies += [
            (kt_refs[p].at[h], kt_scr.at[:, spot]),
            (k_refs[p].at[h], k_scr.at[spot, :]),
            (vt_refs[p].at[h], vt_scr.at[:, spot]),
            (q_refs[p].at[h], q_scr.at[:, at]),
            (d_refs[p].at[head, :], do_scr.at[pl.ds(0, HD), at]),
            (o_refs[p].at[head, :], o_scr.at[:, at]),
        ]
    if h == 0:
        copies.append((d_refs[1].at[pl.ds(208, 576), :], eb_scr))
    copies = [pltpu.make_async_copy(src, dst, sem.at[n]) for n, (src, dst) in enumerate(copies)]
    for c in copies:
        c.start()
    dk_scr[...] = jnp.zeros(dk_scr.shape, F32)
    dv_scr[...] = jnp.zeros(dv_scr.shape, F32)
    for c in copies:
        c.wait()
    do_scr[64:128, :] = jnp.zeros((64, total), BF16)
    delta = jnp.sum(do_scr[0:64, :].astype(F32) * o_scr[...].astype(F32), axis=0, keepdims=True)
    do_scr[64:80, :] = jnp.concatenate([*split3(-delta), jnp.zeros((13, total), F32)], axis=0).astype(BF16)

    def q_block(i, carry):
        start, kind = window_of(sp_ref, i ^ (2 * sp_ref[8]), total)
        here = pl.ds(pl.multiple_of(i * BLK, BLK), BLK)
        for mode, size in enumerate(WINDOWS):

            @pl.when(kind == mode)
            def _():
                qt, dot = q_scr[:, here], do_scr[:, here]
                q, do = qt.astype(F32).T.astype(BF16), dot.astype(F32).T.astype(BF16)
                win = pl.ds(start, size)
                p = jnp.exp(mm(q, kt_scr[:, win]))
                ds = (p * mm(do, vt_scr[:, win])).astype(BF16)
                dv_scr[:, win] += mm(dot, p.astype(BF16))
                dk_scr[:, win] += mm(qt, ds)
                dq_scr[here, :] = mm(ds, k_scr[win, :])

        return carry

    lax.fori_loop(0, 8, q_block, 0)

    def unrotated(g, cosine, sine):
        g = g.astype(BF16).astype(F32)
        a, b = g[0:32], g[32:64]
        return jnp.concatenate([a * cosine + b * sine, b * cosine - a * sine], axis=0).astype(BF16)

    for p in range(4):
        at = slice(p * rows, (p + 1) * rows)
        cosine, sine = cs_refs[p][0:32, :], cs_refs[p][32:64, :]
        src = place_of(sp_ref, p, rows)
        g_scr[0:64, at] = unrotated(dq_scr[at, :].T[0:64] * 0.125, cosine, sine)
        g_scr[64:128, at] = unrotated(dk_scr[0:64, src], cosine, sine)
        g_scr[128:192, at] = dv_scr[0:64, src].astype(BF16)
    grad = mm(tok_t[...], g_scr[...], NT)
    heads = 3 * HD
    near, far, core = outs[0:3]
    near[...] = g_scr[:, 0:rows]
    far[0:heads, :] = g_scr[:, 2 * rows : 3 * rows]
    far[heads : 2 * heads, :] = g_scr[:, 3 * rows :]
    if h == 0:
        (ea,) = given
        grad_out, e_own = outs[3:]
        core[...] = g_scr[:, rows : 2 * rows]
        grad_out[...] = grad.astype(BF16)
        e = ea[...].astype(F32) + unpack_rows(eb_scr, 0, 2 * heads)
        e_own[...] = e[0:heads].astype(BF16)
        pack_rows(far, 2 * heads, e[heads:])
    elif h == 1:
        core_before, before = given
        first, second = outs[3:]
        core[0:heads, :] = core_before[...]
        core[heads:, :] = g_scr[:, rows : 2 * rows]
        split_rows(jnp.concatenate([before[...].astype(F32), grad], axis=1), first, second)
    else:
        core_before, far0, e_own, arrange = given
        first, second = outs[3:]
        core[0 : 2 * heads, :] = core_before[...]
        core[2 * heads : 3 * heads, :] = g_scr[:, rows : 2 * rows]
        core[3 * heads :, :] = far0[heads : 2 * heads, :]
        e = e_own[...].astype(F32) + unpack_rows(far0, 2 * heads, heads)
        if fast:
            transpose_into(eb_scr, e, spots, slice(None))
            e = eb_scr[...]
        else:
            e = mm(arrange[...], e.astype(BF16), NT)
        split_rows(jnp.concatenate([grad, e], axis=1), first, second)


def attend_back(h, fast, spots, sp, q, kt, k, vt, o, d, cs, tok_t, given, awaits=()):
    rows = kt[0].shape[2]
    total = 4 * rows
    width = tok_t.shape[0]
    heads = 3 * HD
    far = (2 * heads + 3 * heads // 2, 2 * heads, 2 * heads)[h]
    outs = [((heads, rows), BF16), ((far, rows), BF16), (((1, 2, 4)[h] * heads, rows), BF16)]
    if h == 0:
        outs += [((width, heads), BF16), ((heads, width), BF16)]
    else:
        outs += [((width // 2, 2 * heads), BF16)] * 2
    return run(
        functools.partial(attend_back_kernel, h, fast),
        12,
        20,
        (sp, spots),
        (*cs, tok_t, *given),
        outs,
        [
            pltpu.VMEM((128, total), BF16),
            pltpu.VMEM((128, total), BF16),
            pltpu.VMEM((HD, total), BF16),
            pltpu.VMEM((128, total), BF16),
            pltpu.VMEM((total, 128), BF16),
            pltpu.VMEM((128, total), BF16),
            pltpu.VMEM((total, 128), F32),
            pltpu.VMEM((128, total), F32),
            pltpu.VMEM((128, total), F32),
            pltpu.VMEM((heads, total), BF16),
            pltpu.VMEM((3 * heads, rows), BF16) if h == 0 else pltpu.VMEM((width, heads), F32),
            pltpu.SemaphoreType.DMA((25,)),
        ],
        awaits,
        apart=(*q, *kt, *k, *vt, *o, *d),
    )


def norm_parts(h):
    centred = h - jnp.mean(h, axis=-1, keepdims=True)
    inverse = lax.rsqrt(jnp.mean(centred * centred, axis=-1, keepdims=True) + 1e-05)
    return centred * inverse, inverse


def norm_back(grad, normed, inverse, gain):
    scaled = grad * gain
    return inverse * (
        scaled
        - jnp.mean(scaled, axis=-1, keepdims=True)
        - normed * jnp.mean(scaled * normed, axis=-1, keepdims=True)
    )


def sigmoid(v):
    return 0.5 + 0.5 * jnp.tanh(0.5 * v)


def out_kernel(a0, a1, a2, a3, w0, w1, w2, w3, tok_ref, gain_ref, bias_ref, low_ref, xhat_ref, inv_ref, *halves):
    w = jnp.concatenate([w0[...], w1[...], w2[...], w3[...]], axis=0)
    for half in range(2):
        at = slice(half * BLK, (half + 1) * BLK)
        a = jnp.concatenate([a0[:, at], a1[:, at], a2[:, at], a3[:, at]], axis=0)
        normed, inverse = norm_parts(tok_ref[at, :].astype(F32) + mm(a, w, TN))
        xhat_ref[at, :] = normed
        inv_ref[at, :] = jnp.broadcast_to(inverse, (BLK, 128))
        low = (normed * gain_ref[...] + bias_ref[...]).astype(BF16)
        low_ref[at, :] = low
        halves[half][...] = low


def out_project(a, w, tok, gain, bias, awaits=()):
    rows, width = tok.shape
    return run(
        out_kernel,
        3,
        10,
        (),
        (*a, *w, tok, gain, bias),
        (((rows, width), BF16), ((rows, width), F32), ((rows, 128), F32), *[((rows // 2, width), BF16)] * 2),
        awaits=awaits,
    )


def part_places(half):
    places = [(n, 0, 2 * half, 0, 0, n, 0) for n in range(3)]
    for n, quarter in ((3, 1), (4, 2)):
        places.append((n, 0, half, 0, 0, 3, (n - 3) * half))
        places += [(n, half, half, side, 1, quarter, side * half) for side in range(2)]
    return places + [(5, 0, 2 * half, 0, 1, 0, 0), (6, 0, 2 * half, 0, 1, 3, 0)]


N_PARTS, N_PLACES = 7, 11


def gather_weights(at_ref, parts, wgu, wd, sem):
    copies = []
    half, width = wgu.shape[0] // 8, wd.shape[1]
    for n, (part, first, count, side, which, quarter, row) in enumerate(part_places(half)):
        dst = (wgu, wd)[which]
        spot = pl.multiple_of((at_ref[0] ^ quarter) * (2 * half) + row, half)
        src = parts[part].at[pl.ds(first, count), pl.ds(side * width, dst.shape[1])]
        copies.append(pltpu.make_async_copy(src, dst.at[pl.ds(spot, count), :], sem.at[n]))
    for c in copies:
        c.start()
    return copies


def pack_kernel(pb1, pb2, pa, to_y, to_z, pa_out, wo_out, sem):
    half, wide = to_y.shape[0] // 2, pa.shape[1]
    pairs = [
        (pb2.at[pl.ds(0, half), :], to_y.at[pl.ds(0, half), :]),
        (pb1.at[pl.ds(half, half), :], to_z.at[pl.ds(0, half), :]),
        (pa.at[pl.ds(0, 2 * half), :], pa_out),
        (pa.at[pl.ds(2 * half, wo_out.shape[0]), :], wo_out),
    ]
    for dst in (to_y, to_z):
        for side in range(2):
            spot = dst.at[pl.ds(half, half), pl.ds(side * wide, wide)]
            pairs.append((pa.at[pl.ds(side * half, half), :], spot))
    copies = [pltpu.make_async_copy(src, dst, sem.at[n]) for n, (src, dst) in enumerate(pairs)]
    for c in copies:
        c.start()
    for c in copies:
        c.wait()


def pack_parts(pb1, pb2, pa):
    rows, wide = pb1.shape
    outs = [(pb1.shape, BF16)] * 2 + [((rows, pa.shape[1]), BF16), ((pa.shape[0] - rows, pa.shape[1]), BF16)]
    return run(pack_kernel, 1, 4, (), (), outs, [pltpu.SemaphoreType.DMA((8,))], apart=(pb1, pb2, pa))


def mlp_rows(x, wg, wu, down, da, db, hid):
    gate, up = mm(x, wg), mm(x, wu)
    s = sigmoid(gate)
    act = gate * s
    low = (act * up).astype(BF16)
    da[...] = (up * (s + act * (1.0 - s))).astype(BF16)
    db[...] = act.astype(BF16)
    if hid is not None:
        hid[...] = low
    return mm(low, down)


def mlp_own_kernel(half0, half1, ml0, wgu, wd, acc, da, db, hid, ml1, sem):
    rows = ml0.shape[0]
    hidden = wd.shape[0]
    copies = []
    for n, half in enumerate((half0, half1)):
        copies.append(pltpu.make_async_copy(half, ml1.at[pl.ds(n * (rows // 2), rows // 2), :], sem.at[n]))
        copies[-1].start()
    for block, x in enumerate((ml0, ml1)):
        if block:
            for c in copies:
                c.wait()
        at = slice(block * rows, (block + 1) * rows)
        total = None
        for col in range(0, hidden, BLK):
            cols, ups = slice(col, col + BLK), slice(hidden + col, hidden + col + BLK)
            saved = [u.at[at, cols] for u in (da, db, hid)]
            part = mlp_rows(x[...], wgu[:, cols], wgu[:, ups], wd[cols, :], *saved)
            total = part if total is None else total + part
        acc[at, :] = total


def mlp_own(ml0, halves, wgu, wd, awaits=()):
    rows, width = ml0.shape
    hidden = wd.shape[0]
    saved = ((2 * rows, hidden), BF16)
    return run(
        mlp_own_kernel,
        0.1,
        10,
        (),
        (ml0, wgu, wd),
        [((2 * rows, width), F32)] + [saved] * 3 + [((rows, width), BF16)],
        [pltpu.SemaphoreType.DMA((2,))],
        awaits,
        apart=halves,
    )


def mlp_chunks(x, total, wgu, wd, da, db):
    hidden = wd.shape[0]
    for col in range(0, hidden, BLK):
        cols, ups = slice(col, col + BLK), slice(hidden + col, hidden + col + BLK)
        total += mlp_rows(x[...], wgu[:, cols], wgu[:, ups], wd[cols, :], da.at[:, cols], db.at[:, cols], None)
    return total


def mlp_far_kernel(at_ref, *refs):
    n_parts = N_PARTS
    ml1, acc, sib0, sib1, da, db, wgu, wd, sem = refs[n_parts:]
    rows = ml1.shape[0]
    for c in gather_weights(at_ref, refs[:n_parts], wgu, wd, sem):
        c.wait()
    total = mlp_chunks(ml1, acc[rows:, :], wgu, wd, da, db)
    sib0[...] = total[0 : rows // 2].astype(BF16)
    sib1[...] = total[rows // 2 :].astype(BF16)


def mlp_far(at, ml1, acc, parts, awaits=()):
    rows, width = ml1.shape
    hidden = parts[0].shape[1] // 2
    return run(
        mlp_far_kernel,
        4,
        10,
        (at,),
        (ml1, acc),
        [((rows // 2, width), BF16)] * 2
        + [((rows, hidden), BF16)] * 2
        + [((width, 2 * hidden), BF16), ((hidden, width), BF16)],
        [pltpu.SemaphoreType.DMA((N_PLACES,))],
        awaits,
        apart=parts,
    )


def mlp_last_kernel(ml0, acc, wgu, wd, own, da, db):
    own[...] = mlp_chunks(ml0, acc[0 : ml0.shape[0], :], wgu, wd, da, db)


def mlp_last(ml0, acc, wgu, wd):
    rows, width = ml0.shape
    saved = ((rows, wd.shape[0]), BF16)
    return run(mlp_last_kernel, 3, 10, (), (ml0, acc, wgu, wd), [((rows, width), F32), saved, saved])


def copies_of(src, dst, sem, rows=128):
    copies = []
    for n in range(src.shape[0] // rows):
        at = pl.ds(n * rows, rows)
        copies.append(pltpu.make_async_copy(src.at[at, :], dst.at[at, :], sem.at[n]))
        copies[-1].start()
    return copies


def mid_kernel(
    got, got_late, xhat_ref, own_ref, go_ref, g1, b1, g2, b2, out_ref, dh_ref, dm_ref, sums_ref, got_ref, sem
):
    gain_sum, bias_sum = 0.0, 0.0
    half = got.shape[0]
    copies = copies_of(got, got_ref, sem)
    copies += copies_of(got_late, got_ref.at[pl.ds(half, half), :], sem.at[pl.ds(half // 128, half // 128)])
    for start in range(0, xhat_ref.shape[0], 128):
        at = slice(start, start + 128)
        copies[start // 128].wait()
        mid = xhat_ref[at, :] * g1[...] + b1[...]
        normed, inverse = norm_parts(mid + (own_ref[at, :] + got_ref[at, :].astype(F32)))
        out_ref[at, :] = (normed * g2[...] + b2[...]).astype(BF16)
        grad = go_ref[at, :].astype(F32)
        dh = norm_back(grad, normed, inverse, g2[...])
        dh_ref[at, :] = dh
        dm_ref[at, :] = dh.astype(BF16)
        gain_sum += jnp.sum(grad * normed, axis=0, keepdims=True)
        bias_sum += jnp.sum(grad, axis=0, keepdims=True)
    sums_ref[0:1, :] = gain_sum
    sums_ref[1:2, :] = bias_sum


def mid_norm(xhat, own, got, out_grad, g1, b1, g2, b2, awaits=()):
    rows, width = xhat.shape
    return run(
        mid_kernel,
        3,
        8,
        (),
        (xhat, own, out_grad, g1, b1, g2, b2),
        (((rows, width), BF16), ((rows, width), F32), ((rows, width), BF16), ((2, width), F32)),
        [pltpu.VMEM((rows, width), BF16), pltpu.SemaphoreType.DMA((rows // 128,))],
        awaits,
        apart=got,
    )


def mlp_back_chunks(x, total, wgu, wd, da, db, at, dg=None, du=None):
    hidden = wd.shape[0]
    for col in range(0, hidden, BLK):
        cols, ups = slice(col, col + BLK), slice(hidden + col, hidden + col + BLK)
        dhid = mm(x[...], wd[cols, :], NT)
        dgate = (dhid * da[at, cols].astype(F32)).astype(BF16)
        dup = (dhid * db[at, cols].astype(F32)).astype(BF16)
        if dg is not None:
            dg[:, cols] = dgate
            du[:, cols] = dup
        part = mm(dgate, wgu[:, cols], NT) + mm(dup, wgu[:, ups], NT)
        total = part if total is None else total + part
    return total


def back_own_kernel(dm0, wgu, wd, da, db, acc, dg, du):
    acc[...] = mlp_back_chunks(dm0, None, wgu, wd, da, db, slice(0, dm0.shape[0]), dg, du)


def back_own(dm0, wgu, wd, da, db):
    rows, width = dm0.shape
    saved = ((rows, wd.shape[0]), BF16)
    return run(back_own_kernel, 3, 10, (), (dm0, wgu, wd, da, db), [((rows, width), F32), saved, saved])


def back_far_kernel(dm1_ref, wgu, wd, wgu_p, wd_p, da_o, db_o, da_p, db_p, sib0, sib1, dg, du, dm1, sem):
    rows = dm1.shape[0]
    copy = pltpu.make_async_copy(dm1_ref, dm1, sem)
    copy.start()
    copy.wait()
    total = mlp_back_chunks(dm1, None, wgu, wd, da_o, db_o, slice(rows, 2 * rows), dg, du)
    total = mlp_back_chunks(dm1, total, wgu_p, wd_p, da_p, db_p, slice(0, rows))
    sib0[...] = total[0 : rows // 2].astype(BF16)
    sib1[...] = total[rows // 2 :].astype(BF16)


def back_far(dm1, wgu, wd, wgu_p, wd_p, da_o, db_o, da_p, db_p):
    rows, width = dm1.shape
    saved = ((rows, wd.shape[0]), BF16)
    return run(
        back_far_kernel,
        6,
        12,
        (),
        (wgu, wd, wgu_p, wd_p, da_o, db_o, da_p, db_p),
        [((rows // 2, width), BF16)] * 2 + [saved, saved],
        [pltpu.VMEM((rows, width), BF16), pltpu.SemaphoreType.DMA],
        apart=(dm1,),
    )


def back_last_kernel(dm0, acc, wgu, wd, da, db, own):
    own[...] = mlp_back_chunks(dm0, acc[...], wgu, wd, da, db, slice(0, dm0.shape[0]))


def back_last(dm0, acc, wgu, wd, da, db):
    return run(back_last_kernel, 3, 10, (), (dm0, acc, wgu, wd, da, db), [(acc.shape, F32)])[0]


def first_norm_kernel(
    got_ref, got_late, dh2, own, xhat, inv, g1, sums2, a0, a1, a2, a3, w0, w1, w2, w3,
    dh1, d0, d1, d2, d3, ea, dat_scr, got, sem,
):
    gain_sum, bias_sum = 0.0, 0.0
    half = got_ref.shape[0]
    copies = copies_of(got_ref, got, sem) + copies_of(got_late, got.at[pl.ds(half, half), :], sem.at[pl.ds(half // 128, half // 128)])
    for start in range(0, dh2.shape[0], 128):
        at = slice(start, start + 128)
        copies[start // 128].wait()
        dmid = dh2[at, :] + (own[at, :] + got[at, :].astype(F32))
        normed = xhat[at, :]
        gain_sum += jnp.sum(dmid * normed, axis=0, keepdims=True)
        bias_sum += jnp.sum(dmid, axis=0, keepdims=True)
        grad = norm_back(dmid, normed, inv[at, 0:1], g1[...])
        dh1[at, :] = grad
        dat_scr[at, :] = grad.astype(BF16)
    sums = jnp.concatenate([gain_sum, bias_sum, sums2[...]], axis=0)
    high = sums.astype(BF16).astype(F32)
    both = jnp.concatenate([high, sums - high], axis=0)
    rest = jnp.concatenate([both[:, 512:], jnp.zeros((8, dh2.shape[0] - 256), F32)], axis=1)
    tail = jnp.concatenate([both[:, 0:512], rest], axis=0).astype(BF16)
    dat = dat_scr[...]
    for w, d in ((w0, d0), (w1, d1), (w2, d2), (w3, d3)):
        d[0:192, :] = mm(w[...], dat, NT).astype(BF16)
        d[192:208, :] = tail
    ea[...] = mm(jnp.concatenate([a0[...], a2[...]], axis=0), dat).astype(BF16)
    pack_rows(d1, 208, mm(jnp.concatenate([a1[...], a3[...]], axis=0), dat))


def pack_rows(dst, start, value):
    n = value.shape[0]
    rest = value[:, 512:]
    dst[start : start + n, :] = value[:, 0:512].astype(dst.dtype)
    dst[start + n : start + n + n // 2, :] = jnp.concatenate([rest[0 : n // 2], rest[n // 2 :]], axis=1).astype(dst.dtype)


def unpack_rows(src, start, n):
    rest = src[start + n : start + n + n // 2, :].astype(F32)
    rest = jnp.concatenate([rest[:, 0:256], rest[:, 256:]], axis=0)
    return jnp.concatenate([src[start : start + n, :].astype(F32), rest], axis=1)


def first_norm_back(dh2, own, got, xhat, inv, g1, sums2, a, w, awaits=()):
    rows, width = dh2.shape
    heads = a[0].shape[0]
    d = ((heads + 16, rows), BF16)
    return run(
        first_norm_kernel,
        5,
        12,
        (),
        (dh2, own, xhat, inv, g1, sums2, *a, *w),
        [((rows, width), F32), d, ((4 * heads + 16, rows), BF16), d, d, ((2 * heads, width), BF16)],
        [pltpu.VMEM((rows, width), BF16), pltpu.VMEM((rows, width), BF16), pltpu.SemaphoreType.DMA((rows // 128,))],
        awaits,
        apart=got,
    )


def far_kernel(
    fast, spots_a, spots_b, dm0, dm1, dm2, dm3, ml2, ml3, wgu, wd, hid_o,
    a_first, a_second, b_first, b_second, dg, du, dmt_a, dmt_b, hids,
):
    rows = dm0.shape[0]
    hidden = wd.shape[0]
    for p, u in enumerate((dm0, dm1, dm2, dm3)):
        cols = slice(p * rows, (p + 1) * rows)
        transpose_into(dmt_a, u[...], spots_a if fast else None, cols)
        transpose_into(dmt_b, u[...], spots_b if fast else None, cols)
    for col in range(0, hidden, BLK):
        cols, ups = slice(col, col + BLK), slice(hidden + col, hidden + col + BLK)
        hids[0 : 2 * rows, :] = hid_o[:, cols]
        for block, (x, dm) in enumerate(((ml2, dm2), (ml3, dm3))):
            at = slice(block * rows, (block + 1) * rows)
            gate, up, dhid = mm(x[...], wgu[:, cols]), mm(x[...], wgu[:, ups]), mm(dm[...], wd[cols, :], NT)
            s = sigmoid(gate)
            act = gate * s
            hids[(2 + block) * rows : (3 + block) * rows, :] = (act * up).astype(BF16)
            dg[at, cols] = (dhid * (up * (s + act * (1.0 - s)))).astype(BF16)
            du[at, cols] = (dhid * act).astype(BF16)
        for turned, first, second, start in ((dmt_a, a_first, a_second, 0), (dmt_b, b_first, b_second, hidden // 2)):
            lo, hi = max(col, start), min(col + BLK, start + hidden // 2)
            if lo < hi:
                there = slice(lo - start, hi - start)
                split_rows(mm(turned[...], hids[:, lo - col : hi - col]), first.at[:, there], second.at[:, there])


def far_rows(fast, spots, dm, ml, wgu, wd, hid, awaits=()):
    rows, width = dm[0].shape
    hidden = wd.shape[0]
    half = ((width // 2, hidden // 2), BF16)
    return run(
        functools.partial(far_kernel, fast),
        8,
        18,
        spots,
        (*dm, *ml, wgu, wd, hid),
        [half] * 4 + [((2 * rows, hidden), BF16)] * 2,
        [*[pltpu.VMEM((width, 4 * rows), BF16)] * 2, pltpu.VMEM((4 * rows, BLK), BF16)],
        awaits,
    )


def weight_kernel(
    fast, spots_a, spots_b, d0, d1, d2, d3, ml0, ml1, ml2, ml3, dg0, dg1, du0, du1, dg_f, du_f, da_first, da_second, db_first,
    db_second, a_first, a_second, b_first, b_second, total, mlt_a, mlt_b, tail_scr, sem,
):
    rows = ml0.shape[0]
    hidden = dg0.shape[1]
    copies = [
        pltpu.make_async_copy(d.at[pl.ds(3 * HD, 16), :], tail_scr.at[p], sem.at[p]) for p, d in enumerate((d0, d1, d2, d3))
    ]
    for c in copies:
        c.start()
    for p, u in enumerate((ml0, ml1, ml2, ml3)):
        cols = slice(p * rows, (p + 1) * rows)
        transpose_into(mlt_a, u[...], spots_a if fast else None, cols)
        transpose_into(mlt_b, u[...], spots_b if fast else None, cols)
    for src, dst in ((da_first, a_first), (da_second, a_second), (db_first, b_first), (db_second, b_second)):
        dst[0 : src.shape[0], hidden:] = src[...]
    wide = slice(0, hidden)
    half = a_first.shape[0]
    for turned, near, late, far, first, second in (
        (mlt_a, dg0, dg1, dg_f, a_first, a_second),
        (mlt_b, du0, du1, du_f, b_first, b_second),
    ):
        grad = mm(turned[:, 0:rows], near[...]) + mm(turned[:, rows : 2 * rows], late[...])
        grad += mm(turned[:, 2 * rows :], far[...])
        split_rows(grad, first.at[:, wide], second.at[0:half, wide])
    for c in copies:
        c.wait()
    sums = [tail_scr[p].astype(F32) for p in range(4)]
    joined = (sums[0] + sums[1]) + (sums[2] + sums[3])
    whole = jnp.concatenate([joined[0:4] + joined[4:8], (joined[8:12] + joined[12:16])[:, 0:256]], axis=1)
    high = whole.astype(BF16).astype(F32)
    low = (whole - high).astype(BF16).astype(F32)
    total[...] = high + low
    rest = jnp.zeros((8, hidden), F32)
    a_second[half : half + EXTRA, wide] = jnp.concatenate([high, low, rest], axis=0).astype(BF16)
    a_second[half : half + EXTRA, hidden:] = jnp.zeros((EXTRA, a_second.shape[1] - hidden), BF16)


def weight_grads(fast, spots, d, ml, near, far, down, awaits=()):
    rows, width = ml[0].shape
    hidden = near[0].shape[1]
    chain = ((width // 2, hidden + hidden // 2), BF16)
    return run(
        functools.partial(weight_kernel, fast),
        6,
        16,
        spots,
        (*ml, *near, *far, *down),
        [chain, ((width // 2 + EXTRA, hidden + hidden // 2), BF16), chain, chain, ((4, width), F32)],
        [
            *[pltpu.VMEM((width, 4 * rows), BF16)] * 2,
            pltpu.VMEM((4, 16, rows), BF16),
            pltpu.SemaphoreType.DMA((4,)),
        ],
        awaits,
        apart=d,
    )


def join_kernel(core, got1, got2, out, sem):
    heads = 3 * HD
    pieces = ((core, 0, 4 * heads), (got1, heads, heads), (got2, heads, heads))
    copies, at = [], 0
    for n, (src, start, count) in enumerate(pieces):
        copies.append(pltpu.make_async_copy(src.at[pl.ds(start, count), :], out.at[pl.ds(at, count), :], sem.at[n]))
        copies[-1].start()
        at += count
    for c in copies:
        c.wait()


def join(core, got1, got2):
    return run(
        join_kernel,
        1,
        4,
        (),
        (),
        [((18 * HD, core.shape[1]), BF16)],
        [pltpu.SemaphoreType.DMA((3,))],
        apart=(core, got1, got2),
    )[0]


def by_heads(w):
    heads = 3 * HD
    return jnp.concatenate([w[c * heads + h * HD : c * heads + (h + 1) * HD, :] for h in range(3) for c in range(3)], axis=0)


def near_kernel(f0, f1, f2, dh1, n0, n1, n2, w0, w2, out, far, sem):
    heads = 3 * HD
    copies = []
    for n, f in enumerate((f0, f1, f2)):
        spot = pl.ds(n * heads, heads)
        copies.append(pltpu.make_async_copy(f.at[pl.ds(0, heads), :], far.at[spot, :], sem.at[n]))
        copies[-1].start()
    near = jnp.concatenate([n0[...], n1[...], n2[...]], axis=0)
    out[...] = dh1[...] + mm(near, by_heads(w0), TN)
    for c in copies:
        c.wait()
    out[...] += mm(far[...], by_heads(w2), TN)


def input_near(dh1, near, far, w0, w2):
    return run(
        near_kernel,
        3,
        12,
        (),
        (dh1, *near, w0, w2),
        [(dh1.shape, F32)],
        [pltpu.VMEM((9 * HD, dh1.shape[0]), BF16), pltpu.SemaphoreType.DMA((3,))],
        apart=far,
    )[0]


def input_kernel(core_ref, before, w1, w3, out, core, total, sem):
    arrival = pltpu.make_async_copy(core_ref, core, sem.at[0])
    arrival.start()
    w = jnp.concatenate([by_heads(w1), by_heads(w3)], axis=0)
    arrival.wait()
    copies = []
    for half in range(before.shape[0] // BLK):
        at = slice(half * BLK, (half + 1) * BLK)
        total[at, :] = before[at, :] + mm(core[:, at], w, TN)
        spot = pl.ds(half * BLK, BLK)
        copies.append(pltpu.make_async_copy(total.at[spot, :], out.at[spot, :], sem.at[1 + half]))
        copies[-1].start()
    for c in copies:
        c.wait()


def input_back(before, core, w1, w3):
    return run(
        input_kernel,
        3,
        14,
        (),
        (before, w1, w3),
        [(before.shape, F32)],
        [
            pltpu.VMEM(core.shape, BF16),
            pltpu.VMEM(before.shape, F32),
            pltpu.SemaphoreType.DMA((1 + before.shape[0] // BLK,)),
        ],
        apart=(core,),
        hbm=(0,),
    )[0]


def split_halves(v):
    return v[0 : v.shape[0] // 2], v[v.shape[0] // 2 :]


def swap(v, bit, axis="tensor"):
    n = lax.axis_size(axis)
    return lax.ppermute(v, axis, [(i, i ^ bit) for i in range(n)])


def bits_of(n):
    return n.bit_length() - 1


def spots_of(order, n):
    block = jnp.arange(n, dtype=jnp.int32) ^ lax.axis_index("dp")
    spot = jnp.zeros((n,), jnp.int32)
    for s, bit in enumerate(order):
        spot = spot + (((block >> bit) & 1) << (len(order) - 1 - s))
    return spot


def last_kernel(chains, kind, *refs):
    count = sum(chains)
    parts, outs, scrs, sem = refs[:count], refs[count:-count - 1], refs[-count - 1 : -1], refs[-1]
    copies = []
    for n, (part, scr) in enumerate(zip(parts, scrs)):
        copies.append(pltpu.make_async_copy(part.at[pl.ds(0, scr.shape[0]), :], scr, sem.at[n]))
        copies[-1].start()
    for c in copies:
        c.wait()
    sums, at = [], 0
    for length in chains:
        sums.append(sum(scr[...].astype(F32) for scr in scrs[at : at + length]))
        at += length
    if kind == "mlp":
        gu, down = outs
        width = down.shape[1]
        one, two = sums[0:2]
        if len(sums) > 2:
            one += sums[2][:, 0 : one.shape[1]]
            two += sums[2][:, one.shape[1] :]
        gu[:, 0, :] = one[:, 0:width]
        gu[:, 1, :] = two[:, 0:width]
        down[...] = jnp.concatenate([one[:, width:], two[:, width:]], axis=1)
    else:
        qkv, out = outs
        total = jnp.concatenate(sums[0:2], axis=1)
        if len(sums) > 2:
            total += sums[2]
        for c in range(3):
            qkv[c] = jnp.concatenate([total[:, (3 * h + c) * HD : (3 * h + c + 1) * HD] for h in range(3)], axis=1)
        out[...] = total[:, 9 * HD :].T


def last_sums(kind, rows, chains, outs):
    parts = [part for chain in chains for part in chain]
    return run(
        functools.partial(last_kernel, [len(chain) for chain in chains], kind),
        2,
        8,
        (),
        (),
        outs,
        [pltpu.VMEM((rows, part.shape[1]), BF16) for part in parts] + [pltpu.SemaphoreType.DMA((len(parts),))],
        apart=parts,
    )


def in_two(v):
    high = lax.reduce_precision(v, 8, 7)
    low = lax.reduce_precision(v - high, 8, 7)
    return jnp.concatenate([high, low], axis=0), high + low


class scatter_steps:
    def __init__(self, first, second, order, ride=None):
        self.parts, self.order, self.step = [first], order, 0
        self.sent, self.ride, self.base = second, ride, None
        self.extra = 0 if ride is None else EXTRA

    def advance(self):
        self.base = self.ride
        self.parts.append(swap(self.sent, 1 << self.order[self.step], "dp"))
        self.step += 1
        self.next_sent()
        return self.parts[-1]

    def carried(self, got):
        n, width = self.base.shape
        rows = got[got.shape[0] - EXTRA : got.shape[0] - EXTRA + 2 * n, 0:width].astype(F32)
        return self.base + (rows[0:n] + rows[n:])

    def next_sent(self):
        if self.extra:
            self.ride = self.carried(self.parts[-1])
        if self.step < len(self.order):
            length = self.parts[-1].shape[0] - self.extra
            sent = sum(u[length // 2 : length].astype(F32) for u in self.parts)
            if self.extra:
                rows, self.ride = in_two(self.ride)
                padding = ((0, EXTRA - rows.shape[0]), (0, sent.shape[1] - rows.shape[1]))
                sent = jnp.concatenate([sent, jnp.pad(rows, padding)], axis=0)
            self.sent = sent.astype(BF16)

    def all_parts(self):
        while self.step < len(self.order):
            self.advance()
        return self.parts


def advance_together(chains):
    bits = {chain.order[chain.step] for chain in chains}
    if len(bits) > 1 or any(chain.step < len(chain.order) - 1 for chain in chains):
        return None
    tall = max(chain.sent.shape[0] for chain in chains)
    sent = [jnp.pad(chain.sent, ((0, tall - chain.sent.shape[0]), (0, 0))) for chain in chains]
    got = swap(jnp.concatenate(sent, axis=1), 1 << bits.pop(), "dp")
    for chain in chains:
        chain.step += 1
        chain.base = chain.ride
    return got


def first_sums(chains, rows):
    return [sum(part[0:rows].astype(F32) for part in chain) for chain in chains]


def quarter_of(w):
    rows = w.shape[0] // 4
    return lax.dynamic_slice_in_dim(w, (lax.axis_index("dp") % 4) * rows, rows, axis=0)


def local(
    tokens,
    doc_lengths,
    key_mask,
    qkv_weight,
    out_weight,
    gate_up_weight,
    down_weight,
    norm1_gain,
    norm1_bias,
    norm2_gain,
    norm2_bias,
    out_grad,
):
    rows, width = tokens.shape
    flags = jnp.pad(key_mask.astype(BF16).reshape(1, rows), ((0, EXTRA - 1), (0, width - rows)))
    tok0 = jnp.concatenate([tokens, flags], axis=0)
    tok1 = swap(tok0, 1)
    tok2 = swap(tok0, 2)
    sp = jnp.concatenate([doc_lengths[0], lax.axis_index("tensor").reshape(1)]).astype(jnp.int32)
    quarter = (lax.axis_index("dp") % 4).reshape(1).astype(jnp.int32)
    freqs = 1000.0 ** (-(jnp.arange(HD // 2, dtype=F32) * 2.0 / HD))
    freqs = jnp.broadcast_to(freqs[:, None], (HD // 2, 128))
    wt = jnp.transpose(qkv_weight, (1, 2, 0)).reshape(-1, width)

    n_dp = lax.axis_size("dp")
    fast = (width // n_dp) % 16 == 0
    order = list(range(bits_of(n_dp)))
    order_b = order[1:2] + order[0:1] + order[2:]
    spots, spots_b = (spots_of(u, n_dp) for u in (order, order_b))

    def arranged(v, at):
        if fast:
            return v
        blocks = v.reshape(v.shape[0], n_dp, width // n_dp)
        return jnp.take(blocks, jnp.argsort(at), axis=1).reshape(v.shape)

    ORDER.last = ()
    wo0 = out_weight
    wo1, wt1 = swap(wo0, 1), swap(wt, 1)
    wgu = gate_up_weight.reshape(width, -1)
    part_b = quarter_of(wgu)
    part_a = jnp.concatenate([quarter_of(down_weight), wo0], axis=0)

    proj = [project(0, sp, freqs, tok0, wt), project(1, sp, freqs, tok1, wt, awaits=(part_a, part_b))]
    tok2, part_b = gate(tok2, part_b)
    tok3, pb0 = swap(tok2, 1), swap(part_b, 2)
    tok = (tok0, tok1, tok2, tok3)
    proj.append(project(2, sp, freqs, tok2, wt))
    *more, part_a = project(3, sp, freqs, tok3, wt, carry=(part_a,))
    proj.append(more)
    pa0 = swap(part_a, 2)
    qt, kt, k, vt, cs = zip(*proj)
    o2, o3, q2, q3 = attend(1, sp, qt, k, vt, (wo1, wt1))
    o2, pb0 = gate(o2, pb0)
    pb1, pb2, g2 = swap(pb0, 1, "dp"), swap(pb0, 2, "dp"), swap(o2, 2)
    o0, o1, q0, q1 = attend(0, sp, qt, k, vt)
    (o3,) = gate(o3, awaits=(pa0,))
    g3 = swap(o3, 3)
    (tok_t,) = transposed(fast, (spots,), tok, rows)
    if not fast:
        tok_t = arranged(tok_t.T, spots).T
    (o1,) = gate(o1)
    g1 = swap(o1, 1)
    to_y, to_z, pa0, wo2 = pack_parts(pb1, pb2, pa0)
    (wo2,) = gate(wo2)
    wo3 = swap(wo2, 1)
    kept = park((*kt, *k, *vt, q0, q1, q2, q3, tok_t))
    kt, k, vt, (q0, q1, q2, q3, tok_t) = kept[0:4], kept[4:8], kept[8:12], kept[12:17]
    from_y, from_z, pa3 = swap(to_y, 1, "dp"), swap(to_z, 2, "dp"), swap(pa0, 3, "dp")
    wo = (wo0, wo1, wo2, wo3)

    gain1, bias1, gain2, bias2 = (u.reshape(1, width) for u in (norm1_gain, norm1_bias, norm2_gain, norm2_bias))
    ml0, xhat1, inv1, *halves = out_project((o0, g1, g2, g3), wo, tokens, gain1, bias1)
    acc, da_o, db_o, hid_o, ml1 = mlp_own(ml0, [swap(u, 1) for u in halves], wgu, down_weight)
    (ml0,) = gate(ml0, awaits=(from_y, from_z, pa3))
    ml2 = swap(ml0, 2)
    parts = (pb0, pb1, pb2, from_y, from_z, pa0, pa3)
    sib0, sib1, da_1, db_1, wgu_p, wd_p = mlp_far(quarter, ml1, acc, parts)
    own, da_0, db_0 = mlp_last(ml0, acc, wgu_p, wd_p)
    output, dh2, dm0, sums2 = mid_norm(
        xhat1, own, (swap(sib0, 1), swap(sib1, 1)), out_grad, gain1, bias1, gain2, bias2
    )
    dm0, ml2 = gate(dm0, ml2)
    dm1, dm2 = swap(dm0, 1), swap(dm0, 2)
    ml3 = swap(ml2, 1)
    acc, dg_0, du_0 = back_own(dm0, wgu, down_weight, da_o, db_o)
    sib0, sib1, dg_1, du_1 = back_far(dm1, wgu, down_weight, wgu_p, wd_p, da_o, db_o, da_1, db_1)
    own = back_last(dm0, acc, wgu_p, wd_p, da_0, db_0)
    dh1, d0, d1, d2, d3, ea = first_norm_back(
        dh2, own, (swap(sib0, 1), swap(sib1, 1)), xhat1, inv1, gain1, sums2, (o0, g1, g2, g3), wo, (ml3,)
    )
    d1, d2, d3, dm2 = gate(d1, d2, d3, dm2)
    dm3 = swap(dm2, 1)
    d = (d0, swap(d1, 1), swap(d2, 2), swap(d3, 3))
    ml, dm, both = (ml0, ml1, ml2, ml3), (dm0, dm1, dm2, dm3), (spots, spots_b)
    *down, dg_f, du_f = far_rows(fast, both, dm, ml[2:], wgu, down_weight, hid_o)
    (wt,) = gate(wt, awaits=d[1:])
    wt2 = swap(wt, 2)
    a_first, a_second, b_first, b_second, sums = weight_grads(
        fast, both, d, ml, (dg_0, dg_1, du_0, du_1), (dg_f, du_f), down
    )
    if not fast:
        tail = a_second[width // 2 :]
        a_first, a_second = split_halves(arranged(jnp.concatenate([a_first, a_second[0 : width // 2]]).T, spots).T)
        a_second = jnp.concatenate([a_second, tail])
        b_first, b_second = split_halves(arranged(jnp.concatenate([b_first, b_second]).T, spots_b).T)
    a_second, b_second = gate(a_second, b_second)
    chain_a = scatter_steps(a_first, a_second, order, sums)
    chain_b = scatter_steps(b_first, b_second, order_b)
    a_got, b_got = chain_a.advance(), chain_b.advance()

    arrange = jnp.zeros((8, 128), BF16)
    if not fast:
        column = jnp.arange(width)
        target = spots[column // (width // n_dp)] * (width // n_dp) + column % (width // n_dp)
        arrange = (column[:, None] == target[None, :]).astype(BF16)
    back = functools.partial(
        attend_back,
        fast=fast,
        spots=spots,
        sp=sp,
        q=(q0, q1, q2, q3),
        kt=kt,
        k=k,
        vt=vt,
        o=(o0, o1, o2, o3),
        d=d,
        cs=cs,
        tok_t=tok_t,
    )
    near0, far0, core0, grad0, e_own = back(0, given=(ea,))
    far0, chain_a.parts[-1], chain_b.parts[-1], wt2 = gate(far0, a_got, b_got, wt2)
    for chain in (chain_a, chain_b):
        chain.next_sent()
    a_got, b_got, got0 = chain_a.advance(), chain_b.advance(), swap(far0, 2)
    near1, far1, core1, first, second = back(1, given=(core0, grad0))
    far1, second, chain_a.parts[-1], chain_b.parts[-1], wt2 = gate(far1, second, a_got, b_got, wt2)
    for chain in (chain_a, chain_b):
        chain.next_sent()
    c1 = scatter_steps(first, second, order)
    c1_got, mlp3 = c1.advance(), advance_together((chain_a, chain_b))
    wt3 = swap(wt2, 1)
    got1 = swap(far1, 2)
    near2, far2, core2, first, second = back(2, given=(core1, got0, e_own, arrange))
    far2, second, c1.parts[-1] = gate(far2, second, c1_got, awaits=(got1, wt3))
    c1.next_sent()
    c2 = scatter_steps(first, second, order)
    c2_got, got2 = c2.advance(), swap(far2, 2)
    c2.parts[-1], *late = gate(c2_got, *([] if mlp3 is None else [mlp3]))
    c2.next_sent()
    c2_got, c1_got = c2.advance(), c1.advance()
    mlp, shard = [chain_a.all_parts(), chain_b.all_parts()], width // n_dp
    if mlp3 is not None:
        mlp.append([mlp3])
    core = swap(join(core2, got1, got2), 1)
    input_grad = input_near(dh1, (near0, near1, near2), (got0, got1, got2), wt, wt2)
    c2.parts[-1], c1.parts[-1] = gate(c2_got, c1_got)
    c2.next_sent()
    c1.next_sent()
    if late:
        chain_a.ride = chain_a.carried(late[0])
        mlp[-1] = late
    both = advance_together((c1, c2))
    attention = [c1.all_parts(), c2.all_parts()]
    if both is not None:
        attention.append([both])
    input_grad = input_back(input_grad, core, wt1, wt3)
    sums = chain_a.ride
    if fast:
        hidden = down_weight.shape[0]
        gu_part, down_part = last_sums("mlp", shard, mlp, [((shard, 2, hidden), F32), ((shard, hidden), F32)])
        qkv_part, out_part = last_sums(
            "attention", shard, attention, [((3, shard, 3 * HD), F32), ((3 * HD, shard), F32)]
        )
        qkv_part = jnp.transpose(qkv_part, (1, 0, 2))
    else:
        one, two = first_sums(mlp, shard)
        gu_part = jnp.stack([one[:, 0:width], two[:, 0:width]], axis=1)
        down_part = jnp.concatenate([one[:, width:], two[:, width:]], axis=1)
        total = jnp.concatenate(first_sums(attention, shard), axis=1)
        out_part = total[:, 9 * HD :].T
        qkv_part = jnp.transpose(total[:, 0 : 9 * HD].reshape(shard, 3, 3, HD), (0, 2, 1, 3)).reshape(shard, 3, 3 * HD)
    return (
        output,
        input_grad,
        qkv_part,
        out_part,
        gu_part,
        down_part.T,
        sums[0],
        sums[1],
        sums[2],
        sums[3],
    )


def solution(mesh):
    placed = (
        P(("dp", "tensor"), None),
        P("dp", None),
        P(("dp", "tensor")),
        P(None, None, "tensor"),
        P("tensor", None),
        P(None, None, "tensor"),
        P("tensor", None),
        P(),
        P(),
        P(),
        P(),
        P(("dp", "tensor"), None),
    )
    return jax.shard_map(
        local,
        mesh=mesh,
        in_specs=placed,
        out_specs=(
            P(("dp", "tensor"), None),
            P(("dp", "tensor"), None),
            P("dp", None, "tensor"),
            P("tensor", "dp"),
            P("dp", None, "tensor"),
            P("tensor", "dp"),
            P(),
            P(),
            P(),
            P(),
        ),
        check_vma=False,
    )
```

```python
import functools
import math

import jax
import jax.numpy as jnp
from jax import lax
from jax.experimental import pallas as pl
from jax.experimental.pallas import tpu as pltpu
from jax.sharding import PartitionSpec as P

HD = 64
F32 = jnp.float32
BF16 = jnp.bfloat16
BIG = -1e30
BLK = 256
WINDOWS = (640, 1664, 2048)
SCALE = 0.15
EXTRA = 16
NN = (((1,), (0,)), ((), ()))
NT = (((1,), (1,)), ((), ()))
TN = (((0,), (0,)), ((), ()))


def mm(a, b, dims=NN):
    return lax.dot_general(a, b, dims, preferred_element_type=F32)


class Order:
    def __init__(self):
        self.last = ()


ORDER = Order()


def run(kernel, us, mib, scalars, args, outs, scratch=(), awaits=(), carry=(), apart=(), hbm=()):
    in_vmem = pl.BlockSpec(memory_space=pltpu.VMEM)
    anywhere = pl.BlockSpec(memory_space=pl.ANY)
    awaits = (*awaits, *ORDER.last)
    sizes = [math.prod(shape) for n, (shape, dtype) in enumerate(outs) if n not in hbm]
    token = not sizes or min(sizes) > 1 << 15
    if token:
        inner, outs = kernel, [*outs, ((8, 128), F32)]

        def kernel(*refs):
            spot = n_in + len(outs) - 1
            refs[spot][...] = jnp.zeros((8, 128), F32)
            inner(*refs[:spot], *refs[spot + 1 :])

    n_in = len(scalars) + len(apart) + len(args)
    n_skip, n_out = len(awaits) + len(carry), len(outs)

    def body(*refs):
        rest = refs[n_in + n_skip :]
        kernel(*refs[:n_in], *rest[:n_out], *rest[n_out + len(carry) :])

    results = pl.pallas_call(
        body,
        in_specs=[pl.BlockSpec(memory_space=pltpu.SMEM)] * len(scalars)
        + [anywhere] * len(apart)
        + [in_vmem] * len(args)
        + [anywhere] * n_skip,
        out_specs=[pl.BlockSpec(memory_space=pltpu.HBM) if n in hbm else in_vmem for n in range(n_out)]
        + [anywhere] * len(carry),
        out_shape=[jax.ShapeDtypeStruct(*o) for o in outs] + [jax.ShapeDtypeStruct(c.shape, c.dtype) for c in carry],
        scratch_shapes=list(scratch),
        input_output_aliases={n_in + len(awaits) + i: n_out + i for i in range(len(carry))},
        compiler_params=pltpu.CompilerParams(vmem_limit_bytes=mib << 20),
        cost_estimate=pl.CostEstimate(flops=int(us * SCALE * 1.1e9), bytes_accessed=1 << 18, transcendentals=0),
    )(*scalars, *apart, *args, *awaits, *carry)
    ORDER.last = (min((r for n, r in enumerate(results[:n_out]) if n not in hbm), key=lambda r: r.size),)
    if token:
        results = [*results[: n_out - 1], *results[n_out:]]
    return results


def gate_kernel(out):
    out[...] = jnp.zeros(out.shape, F32)


def gate(*arrays, awaits=()):
    return run(gate_kernel, 0.1, 4, (), (), [((8, 128), F32)], awaits=awaits, carry=arrays)[1:]


def park_kernel(places, *refs):
    count = len(places)
    copies = []
    for n, (first, rows) in enumerate(places):
        src = refs[n] if rows is None else refs[n].at[pl.ds(first, rows), :]
        copies.append(pltpu.make_async_copy(src, refs[count + n], refs[-1].at[n]))
        copies[-1].start()
    for c in copies:
        c.wait()


def park(arrays, halves=()):
    places = [(0, None) for _ in arrays] + [(n * (u.shape[0] // 2), u.shape[0] // 2) for u, n in halves]
    outs = [(u.shape, u.dtype) for u in arrays] + [((u.shape[0] // 2, u.shape[1]), u.dtype) for u, n in halves]
    return run(
        functools.partial(park_kernel, places),
        3,
        4,
        (),
        (),
        outs,
        [pltpu.SemaphoreType.DMA((len(outs),))],
        apart=(*arrays, *[u for u, n in halves]),
        hbm=range(len(outs)),
    )


def split3(v):
    top = v.astype(BF16).astype(F32)
    rest = v - top
    middle = rest.astype(BF16).astype(F32)
    return top, middle, rest - middle


def split_rows(value, first, second):
    half = first.shape[0]
    first[...] = value[0:half].astype(first.dtype)
    second[...] = value[half:].astype(second.dtype)


def transpose_into(dst, value, spots, cols):
    turned = value.T
    if spots is None:
        dst[:, cols] = turned
        return
    count = spots.shape[0]
    rows = turned.shape[0] // count
    for b in range(count):
        dst[pl.ds(pl.multiple_of(spots[b] * rows, rows), rows), cols] = turned[b * rows : (b + 1) * rows]


def transpose_kernel(fast, *refs):
    count = (len(refs) - 4) // 2
    spots, tokens, outs = refs[:count], refs[count : count + 4], refs[count + 4 :]
    rows = outs[0].shape[1] // 4
    for p, t in enumerate(tokens):
        for spot, out in zip(spots, outs):
            transpose_into(out, t[0:rows, :], spot if fast else None, slice(p * rows, (p + 1) * rows))


def transposed(fast, spots, pieces, rows):
    width = pieces[0].shape[1]
    outs = [((width, 4 * rows), BF16)] * len(spots)
    return run(functools.partial(transpose_kernel, fast), 2, 8, spots, pieces, outs)


def project_kernel(piece, sp_ref, freq_ref, tok_ref, w_ref, qt_ref, kt_ref, k_ref, vt_ref, cs_ref):
    n = tok_ref.shape[0] - EXTRA
    place = (sp_ref[8] ^ piece) * n + lax.broadcasted_iota(jnp.int32, (1, n), 1)
    seg = jnp.zeros((1, n), jnp.int32)
    pos = place
    end = 0
    for d in range(8):
        length = sp_ref[d]
        end = end + length
        past = place >= end
        seg += past.astype(jnp.int32)
        pos -= jnp.where(past, length, 0)
    angles = pos.astype(F32) * freq_ref[:, 0:1]
    cosine, sine = jnp.cos(angles), jnp.sin(angles)
    cs_ref[0:32, :] = cosine
    cs_ref[32:64, :] = sine
    idx = lax.broadcasted_iota(jnp.int32, (64, n), 0)
    which = jnp.where(idx < 19, idx - 8, idx - 19)
    bit = (jnp.broadcast_to(place, (64, n)) >> jnp.clip(which, 0, 10)) & 1
    flipped = jnp.where(idx < 19, bit, 1 - bit).astype(F32)
    same = (idx == seg).astype(F32)
    coded = (idx >= 8) & (idx < 30)
    invalid = 1.0 - tok_ref[n : n + EXTRA, 0:n].astype(F32)[0:1]
    q_tail = jnp.where(idx < 8, BIG * (1.0 - same), jnp.where(coded, BIG * flipped, 0.0))
    k_tail = jnp.where(idx < 8, same, jnp.where(coded, invalid * (1.0 - flipped), 0.0))
    k_tail = jnp.where((idx >= 32) & (idx < 35), 1.0, k_tail)
    v_tail = jnp.where(idx < 3, 1.0, 0.0)
    y = mm(w_ref[...], tok_ref[0:n, :], NT)

    def rotated(at):
        a, b = y[at : at + 32], y[at + 32 : at + 64]
        return jnp.concatenate([a * cosine - b * sine, b * cosine + a * sine], axis=0)

    for h in range(3):
        qt_ref[h] = jnp.concatenate([rotated(h * HD) * 0.125, q_tail], axis=0).astype(BF16)
        key = jnp.concatenate([rotated(192 + h * HD), k_tail], axis=0)
        kt_ref[h] = key.astype(BF16)
        k_ref[h] = key.T.astype(BF16)
        vt_ref[h] = jnp.concatenate([y[384 + h * HD : 448 + h * HD], v_tail], axis=0).astype(BF16)


def project(piece, sp, freqs, tok, w, awaits=(), carry=()):
    rows = tok.shape[0] - EXTRA
    wide, tall = ((3, 128, rows), BF16), ((3, rows, 128), BF16)
    return run(
        functools.partial(project_kernel, piece),
        2.5,
        10,
        (sp,),
        (freqs, tok, w),
        (wide, wide, tall, wide, ((HD, rows), F32)),
        awaits=awaits,
        carry=carry,
    )


def window_of(sp_ref, block, total):
    a = block * BLK
    b = a + BLK - 1
    first, last, end = 0, 0, 0
    for d in range(8):
        begin, end = end, end + sp_ref[d]
        first = jnp.where(begin <= a, begin, first)
        last = jnp.where(begin <= b, end, last)
    start = (first // 128) * 128
    kind = jnp.where(last - start <= WINDOWS[0], 0, jnp.where(last - start <= WINDOWS[1], 1, 2))
    size = jnp.where(kind == 0, WINDOWS[0], jnp.where(kind == 1, WINDOWS[1], WINDOWS[2]))
    return pl.multiple_of(jnp.minimum(start, total - size), 128), kind


def place_of(sp_ref, piece, rows):
    return pl.ds(pl.multiple_of((sp_ref[8] ^ piece) * rows, rows), rows)


def attend_kernel(base, sp_ref, qa, qb, k0, k1, k2, k3, v0, v1, v2, v3, oa, ob, ba, bb, k_scr, v_scr, s_scr, q_scr, o_scr):
    rows = qa.shape[2]
    total = 4 * rows
    for p, (k, v) in enumerate(((k0, v0), (k1, v1), (k2, v2), (k3, v3))):
        at = place_of(sp_ref, p, rows)
        k_scr[:, at, :] = k[...]
        v_scr[:, :, at] = v[...]
    for n in range(4):
        q_scr[n] = (qa, qb)[n // 2][:, :, (n % 2) * BLK : (n % 2 + 1) * BLK]

    def q_block(i, carry):
        start, kind = window_of(sp_ref, (base + i) ^ (2 * sp_ref[8]), total)

        def scores(h, size):
            s = mm(k_scr[h, pl.ds(start, size), :], q_scr[i, h])
            s_scr[h, 0:size, :] = s
            return jnp.max(s, axis=0, keepdims=True)

        def weigh(h, size, top):
            p = jnp.exp(s_scr[h, 0:size, :] - top).astype(BF16)
            acc = mm(v_scr[h, :, pl.ds(start, size)], p)
            norm = acc[64:65]
            o_scr[i, h * HD : (h + 1) * HD, :] = (acc[0:64] / norm).astype(BF16)
            parts = split3(-(top + jnp.log(norm)))
            q_scr[i, h, 96:112, :] = jnp.concatenate([*parts, jnp.zeros((13, BLK), F32)], axis=0).astype(BF16)

        for mode, size in enumerate(WINDOWS):

            @pl.when(kind == mode)
            def _():
                t0 = scores(0, size)
                t1 = scores(1, size)
                weigh(0, size, t0)
                t2 = scores(2, size)
                weigh(1, size, t1)
                weigh(2, size, t2)

        return carry

    lax.fori_loop(0, 4, q_block, 0)
    for n in range(4):
        at = slice((n % 2) * BLK, (n % 2 + 1) * BLK)
        (oa, ob)[n // 2][:, at] = o_scr[n]
        (ba, bb)[n // 2][:, :, at] = q_scr[n]


def attend(half, sp, qt, k, vt, awaits=(), carry=()):
    rows = qt[0].shape[2]
    total = 4 * rows
    out, back = ((3 * HD, rows), BF16), ((3, 128, rows), BF16)
    return run(
        functools.partial(attend_kernel, half * 4),
        8,
        18,
        (sp,),
        (qt[2 * half], qt[2 * half + 1], *k, *vt),
        (out, out, back, back),
        [
            pltpu.VMEM((3, total, 128), BF16),
            pltpu.VMEM((3, 128, total), BF16),
            pltpu.VMEM((3, total, BLK), F32),
            pltpu.VMEM((4, 3, 128, BLK), BF16),
            pltpu.VMEM((4, 3 * HD, BLK), BF16),
        ],
        awaits,
        carry,
    )


def attend_back_kernel(h, fast, sp_ref, spots, *refs):
    q_refs, kt_refs, k_refs, vt_refs, o_refs, d_refs = (refs[4 * n : 4 * n + 4] for n in range(6))
    n_given = (1, 2, 4)[h]
    cs_refs, tok_t, given, outs = refs[24:28], refs[28], refs[29 : 29 + n_given], refs[29 + n_given : -12]
    q_scr, do_scr, o_scr, kt_scr, k_scr, vt_scr, dq_scr, dk_scr, dv_scr, g_scr, eb_scr, sem = refs[-12:]
    rows = kt_refs[0].shape[2]
    total = 4 * rows
    head = pl.ds(h * HD, HD)
    copies = []
    for p in range(4):
        spot, at = place_of(sp_ref, p, rows), pl.ds(p * rows, rows)
        copies += [
            (kt_refs[p].at[h], kt_scr.at[:, spot]),
            (k_refs[p].at[h], k_scr.at[spot, :]),
            (vt_refs[p].at[h], vt_scr.at[:, spot]),
            (q_refs[p].at[h], q_scr.at[:, at]),
            (d_refs[p].at[head, :], do_scr.at[pl.ds(0, HD), at]),
            (o_refs[p].at[head, :], o_scr.at[:, at]),
        ]
    if h == 0:
        copies.append((d_refs[1].at[pl.ds(208, 576), :], eb_scr))
    copies = [pltpu.make_async_copy(src, dst, sem.at[n]) for n, (src, dst) in enumerate(copies)]
    for c in copies:
        c.start()
    dk_scr[...] = jnp.zeros(dk_scr.shape, F32)
    dv_scr[...] = jnp.zeros(dv_scr.shape, F32)
    for c in copies:
        c.wait()
    do_scr[64:128, :] = jnp.zeros((64, total), BF16)
    delta = jnp.sum(do_scr[0:64, :].astype(F32) * o_scr[...].astype(F32), axis=0, keepdims=True)
    do_scr[64:80, :] = jnp.concatenate([*split3(-delta), jnp.zeros((13, total), F32)], axis=0).astype(BF16)

    def q_block(i, carry):
        start, kind = window_of(sp_ref, i ^ (2 * sp_ref[8]), total)
        here = pl.ds(pl.multiple_of(i * BLK, BLK), BLK)
        for mode, size in enumerate(WINDOWS):

            @pl.when(kind == mode)
            def _():
                qt, dot = q_scr[:, here], do_scr[:, here]
                q, do = qt.astype(F32).T.astype(BF16), dot.astype(F32).T.astype(BF16)
                win = pl.ds(start, size)
                p = jnp.exp(mm(q, kt_scr[:, win]))
                ds = (p * mm(do, vt_scr[:, win])).astype(BF16)
                dv_scr[:, win] += mm(dot, p.astype(BF16))
                dk_scr[:, win] += mm(qt, ds)
                dq_scr[here, :] = mm(ds, k_scr[win, :])

        return carry

    lax.fori_loop(0, 8, q_block, 0)

    def unrotated(g, cosine, sine):
        g = g.astype(BF16).astype(F32)
        a, b = g[0:32], g[32:64]
        return jnp.concatenate([a * cosine + b * sine, b * cosine - a * sine], axis=0).astype(BF16)

    for p in range(4):
        at = slice(p * rows, (p + 1) * rows)
        cosine, sine = cs_refs[p][0:32, :], cs_refs[p][32:64, :]
        src = place_of(sp_ref, p, rows)
        g_scr[0:64, at] = unrotated(dq_scr[at, :].T[0:64] * 0.125, cosine, sine)
        g_scr[64:128, at] = unrotated(dk_scr[0:64, src], cosine, sine)
        g_scr[128:192, at] = dv_scr[0:64, src].astype(BF16)
    grad = mm(tok_t[...], g_scr[...], NT)
    heads = 3 * HD
    near, far, core = outs[0:3]
    near[...] = g_scr[:, 0:rows]
    far[0:heads, :] = g_scr[:, 2 * rows : 3 * rows]
    far[heads : 2 * heads, :] = g_scr[:, 3 * rows :]
    if h == 0:
        (ea,) = given
        grad_out, e_own = outs[3:]
        core[...] = g_scr[:, rows : 2 * rows]
        grad_out[...] = grad.astype(BF16)
        e = ea[...].astype(F32) + unpack_rows(eb_scr, 0, 2 * heads)
        e_own[...] = e[0:heads].astype(BF16)
        pack_rows(far, 2 * heads, e[heads:])
    elif h == 1:
        core_before, before = given
        first, second = outs[3:]
        core[0:heads, :] = core_before[...]
        core[heads:, :] = g_scr[:, rows : 2 * rows]
        split_rows(jnp.concatenate([before[...].astype(F32), grad], axis=1), first, second)
    else:
        core_before, far0, e_own, arrange = given
        first, second = outs[3:]
        core[0 : 2 * heads, :] = core_before[...]
        core[2 * heads : 3 * heads, :] = g_scr[:, rows : 2 * rows]
        core[3 * heads :, :] = far0[heads : 2 * heads, :]
        e = e_own[...].astype(F32) + unpack_rows(far0, 2 * heads, heads)
        if fast:
            transpose_into(eb_scr, e, spots, slice(None))
            e = eb_scr[...]
        else:
            e = mm(arrange[...], e.astype(BF16), NT)
        split_rows(jnp.concatenate([grad, e], axis=1), first, second)


def attend_back(h, fast, spots, sp, q, kt, k, vt, o, d, cs, tok_t, given, awaits=()):
    rows = kt[0].shape[2]
    total = 4 * rows
    width = tok_t.shape[0]
    heads = 3 * HD
    far = (2 * heads + 3 * heads // 2, 2 * heads, 2 * heads)[h]
    outs = [((heads, rows), BF16), ((far, rows), BF16), (((1, 2, 4)[h] * heads, rows), BF16)]
    if h == 0:
        outs += [((width, heads), BF16), ((heads, width), BF16)]
    else:
        outs += [((width // 2, 2 * heads), BF16)] * 2
    return run(
        functools.partial(attend_back_kernel, h, fast),
        12,
        20,
        (sp, spots),
        (*cs, tok_t, *given),
        outs,
        [
            pltpu.VMEM((128, total), BF16),
            pltpu.VMEM((128, total), BF16),
            pltpu.VMEM((HD, total), BF16),
            pltpu.VMEM((128, total), BF16),
            pltpu.VMEM((total, 128), BF16),
            pltpu.VMEM((128, total), BF16),
            pltpu.VMEM((total, 128), F32),
            pltpu.VMEM((128, total), F32),
            pltpu.VMEM((128, total), F32),
            pltpu.VMEM((heads, total), BF16),
            pltpu.VMEM((3 * heads, rows), BF16) if h == 0 else pltpu.VMEM((width, heads), F32),
            pltpu.SemaphoreType.DMA((25,)),
        ],
        awaits,
        apart=(*q, *kt, *k, *vt, *o, *d),
    )


def norm_parts(h):
    centred = h - jnp.mean(h, axis=-1, keepdims=True)
    inverse = lax.rsqrt(jnp.mean(centred * centred, axis=-1, keepdims=True) + 1e-05)
    return centred * inverse, inverse


def norm_back(grad, normed, inverse, gain):
    scaled = grad * gain
    return inverse * (
        scaled
        - jnp.mean(scaled, axis=-1, keepdims=True)
        - normed * jnp.mean(scaled * normed, axis=-1, keepdims=True)
    )


def sigmoid(v):
    return 0.5 + 0.5 * jnp.tanh(0.5 * v)


def out_kernel(a0, a1, a2, a3, w0, w1, w2, w3, tok_ref, gain_ref, bias_ref, low_ref, xhat_ref, inv_ref, *halves):
    w = jnp.concatenate([w0[...], w1[...], w2[...], w3[...]], axis=0)
    for half in range(2):
        at = slice(half * BLK, (half + 1) * BLK)
        a = jnp.concatenate([a0[:, at], a1[:, at], a2[:, at], a3[:, at]], axis=0)
        normed, inverse = norm_parts(tok_ref[at, :].astype(F32) + mm(a, w, TN))
        xhat_ref[at, :] = normed
        inv_ref[at, :] = jnp.broadcast_to(inverse, (BLK, 128))
        low = (normed * gain_ref[...] + bias_ref[...]).astype(BF16)
        low_ref[at, :] = low
        halves[half][...] = low


def out_project(a, w, tok, gain, bias, awaits=()):
    rows, width = tok.shape
    return run(
        out_kernel,
        3,
        10,
        (),
        (*a, *w, tok, gain, bias),
        (((rows, width), BF16), ((rows, width), F32), ((rows, 128), F32), *[((rows // 2, width), BF16)] * 2),
        awaits=awaits,
    )


def part_places(half):
    places = [(n, 0, 2 * half, 0, 0, n, 0) for n in range(3)]
    for n, quarter in ((3, 1), (4, 2)):
        places.append((n, 0, half, 0, 0, 3, (n - 3) * half))
        places += [(n, half, half, side, 1, quarter, side * half) for side in range(2)]
    return places + [(5, 0, 2 * half, 0, 1, 0, 0), (6, 0, 2 * half, 0, 1, 3, 0)]


N_PARTS, N_PLACES = 7, 11


def gather_weights(at_ref, parts, wgu, wd, sem):
    copies = []
    half, width = wgu.shape[0] // 8, wd.shape[1]
    for n, (part, first, count, side, which, quarter, row) in enumerate(part_places(half)):
        dst = (wgu, wd)[which]
        spot = pl.multiple_of((at_ref[0] ^ quarter) * (2 * half) + row, half)
        src = parts[part].at[pl.ds(first, count), pl.ds(side * width, dst.shape[1])]
        copies.append(pltpu.make_async_copy(src, dst.at[pl.ds(spot, count), :], sem.at[n]))
    for c in copies:
        c.start()
    return copies


def pack_kernel(pb1, pb2, pa, to_y, to_z, pa_out, wo_out, sem):
    half, wide = to_y.shape[0] // 2, pa.shape[1]
    pairs = [
        (pb2.at[pl.ds(0, half), :], to_y.at[pl.ds(0, half), :]),
        (pb1.at[pl.ds(half, half), :], to_z.at[pl.ds(0, half), :]),
        (pa.at[pl.ds(0, 2 * half), :], pa_out),
        (pa.at[pl.ds(2 * half, wo_out.shape[0]), :], wo_out),
    ]
    for dst in (to_y, to_z):
        for side in range(2):
            spot = dst.at[pl.ds(half, half), pl.ds(side * wide, wide)]
            pairs.append((pa.at[pl.ds(side * half, half), :], spot))
    copies = [pltpu.make_async_copy(src, dst, sem.at[n]) for n, (src, dst) in enumerate(pairs)]
    for c in copies:
        c.start()
    for c in copies:
        c.wait()


def pack_parts(pb1, pb2, pa):
    rows, wide = pb1.shape
    outs = [(pb1.shape, BF16)] * 2 + [((rows, pa.shape[1]), BF16), ((pa.shape[0] - rows, pa.shape[1]), BF16)]
    return run(pack_kernel, 1, 4, (), (), outs, [pltpu.SemaphoreType.DMA((8,))], apart=(pb1, pb2, pa))


def mlp_rows(x, wg, wu, down, da, db, hid):
    gate, up = mm(x, wg), mm(x, wu)
    s = sigmoid(gate)
    act = gate * s
    low = (act * up).astype(BF16)
    da[...] = (up * (s + act * (1.0 - s))).astype(BF16)
    db[...] = act.astype(BF16)
    if hid is not None:
        hid[...] = low
    return mm(low, down)


def mlp_own_kernel(half0, half1, ml0, wgu, wd, acc, da, db, hid, ml1, sem):
    rows = ml0.shape[0]
    hidden = wd.shape[0]
    copies = []
    for n, half in enumerate((half0, half1)):
        copies.append(pltpu.make_async_copy(half, ml1.at[pl.ds(n * (rows // 2), rows // 2), :], sem.at[n]))
        copies[-1].start()
    for block, x in enumerate((ml0, ml1)):
        if block:
            for c in copies:
                c.wait()
        at = slice(block * rows, (block + 1) * rows)
        total = None
        for col in range(0, hidden, BLK):
            cols, ups = slice(col, col + BLK), slice(hidden + col, hidden + col + BLK)
            saved = [u.at[at, cols] for u in (da, db, hid)]
            part = mlp_rows(x[...], wgu[:, cols], wgu[:, ups], wd[cols, :], *saved)
            total = part if total is None else total + part
        acc[at, :] = total


def mlp_own(ml0, halves, wgu, wd, awaits=()):
    rows, width = ml0.shape
    hidden = wd.shape[0]
    saved = ((2 * rows, hidden), BF16)
    return run(
        mlp_own_kernel,
        0.1,
        10,
        (),
        (ml0, wgu, wd),
        [((2 * rows, width), F32)] + [saved] * 3 + [((rows, width), BF16)],
        [pltpu.SemaphoreType.DMA((2,))],
        awaits,
        apart=halves,
    )


def mlp_chunks(x, total, wgu, wd, da, db):
    hidden = wd.shape[0]
    for col in range(0, hidden, BLK):
        cols, ups = slice(col, col + BLK), slice(hidden + col, hidden + col + BLK)
        total += mlp_rows(x[...], wgu[:, cols], wgu[:, ups], wd[cols, :], da.at[:, cols], db.at[:, cols], None)
    return total


def mlp_far_kernel(at_ref, *refs):
    n_parts = N_PARTS
    ml1, acc, sib0, sib1, da, db, wgu, wd, sem = refs[n_parts:]
    rows = ml1.shape[0]
    for c in gather_weights(at_ref, refs[:n_parts], wgu, wd, sem):
        c.wait()
    total = mlp_chunks(ml1, acc[rows:, :], wgu, wd, da, db)
    sib0[...] = total[0 : rows // 2].astype(BF16)
    sib1[...] = total[rows // 2 :].astype(BF16)


def mlp_far(at, ml1, acc, parts, awaits=()):
    rows, width = ml1.shape
    hidden = parts[0].shape[1] // 2
    return run(
        mlp_far_kernel,
        4,
        10,
        (at,),
        (ml1, acc),
        [((rows // 2, width), BF16)] * 2
        + [((rows, hidden), BF16)] * 2
        + [((width, 2 * hidden), BF16), ((hidden, width), BF16)],
        [pltpu.SemaphoreType.DMA((N_PLACES,))],
        awaits,
        apart=parts,
    )


def mlp_last_kernel(ml0, acc, wgu, wd, own, da, db):
    own[...] = mlp_chunks(ml0, acc[0 : ml0.shape[0], :], wgu, wd, da, db)


def mlp_last(ml0, acc, wgu, wd):
    rows, width = ml0.shape
    saved = ((rows, wd.shape[0]), BF16)
    return run(mlp_last_kernel, 3, 10, (), (ml0, acc, wgu, wd), [((rows, width), F32), saved, saved])


def copies_of(src, dst, sem, rows=128):
    copies = []
    for n in range(src.shape[0] // rows):
        at = pl.ds(n * rows, rows)
        copies.append(pltpu.make_async_copy(src.at[at, :], dst.at[at, :], sem.at[n]))
        copies[-1].start()
    return copies


def mid_kernel(
    got, got_late, xhat_ref, own_ref, go_ref, g1, b1, g2, b2, out_ref, dh_ref, dm_ref, sums_ref, got_ref, sem
):
    gain_sum, bias_sum = 0.0, 0.0
    half = got.shape[0]
    copies = copies_of(got, got_ref, sem)
    copies += copies_of(got_late, got_ref.at[pl.ds(half, half), :], sem.at[pl.ds(half // 128, half // 128)])
    for start in range(0, xhat_ref.shape[0], 128):
        at = slice(start, start + 128)
        copies[start // 128].wait()
        mid = xhat_ref[at, :] * g1[...] + b1[...]
        normed, inverse = norm_parts(mid + (own_ref[at, :] + got_ref[at, :].astype(F32)))
        out_ref[at, :] = (normed * g2[...] + b2[...]).astype(BF16)
        grad = go_ref[at, :].astype(F32)
        dh = norm_back(grad, normed, inverse, g2[...])
        dh_ref[at, :] = dh
        dm_ref[at, :] = dh.astype(BF16)
        gain_sum += jnp.sum(grad * normed, axis=0, keepdims=True)
        bias_sum += jnp.sum(grad, axis=0, keepdims=True)
    sums_ref[0:1, :] = gain_sum
    sums_ref[1:2, :] = bias_sum


def mid_norm(xhat, own, got, out_grad, g1, b1, g2, b2, awaits=()):
    rows, width = xhat.shape
    return run(
        mid_kernel,
        10,
        8,
        (),
        (xhat, own, out_grad, g1, b1, g2, b2),
        (((rows, width), BF16), ((rows, width), F32), ((rows, width), BF16), ((2, width), F32)),
        [pltpu.VMEM((rows, width), BF16), pltpu.SemaphoreType.DMA((rows // 128,))],
        awaits,
        apart=got,
    )


def mlp_back_chunks(x, total, wgu, wd, da, db, at, dg=None, du=None):
    hidden = wd.shape[0]
    for col in range(0, hidden, BLK):
        cols, ups = slice(col, col + BLK), slice(hidden + col, hidden + col + BLK)
        dhid = mm(x[...], wd[cols, :], NT)
        dgate = (dhid * da[at, cols].astype(F32)).astype(BF16)
        dup = (dhid * db[at, cols].astype(F32)).astype(BF16)
        if dg is not None:
            dg[:, cols] = dgate
            du[:, cols] = dup
        part = mm(dgate, wgu[:, cols], NT) + mm(dup, wgu[:, ups], NT)
        total = part if total is None else total + part
    return total


def back_own_kernel(dm0, wgu, wd, da, db, acc, dg, du):
    acc[...] = mlp_back_chunks(dm0, None, wgu, wd, da, db, slice(0, dm0.shape[0]), dg, du)


def back_own(dm0, wgu, wd, da, db):
    rows, width = dm0.shape
    saved = ((rows, wd.shape[0]), BF16)
    return run(back_own_kernel, 3, 10, (), (dm0, wgu, wd, da, db), [((rows, width), F32), saved, saved])


def back_far_kernel(dm1_ref, wgu, wd, wgu_p, wd_p, da_o, db_o, da_p, db_p, sib0, sib1, dg, du, dm1, sem):
    rows = dm1.shape[0]
    copy = pltpu.make_async_copy(dm1_ref, dm1, sem)
    copy.start()
    copy.wait()
    total = mlp_back_chunks(dm1, None, wgu, wd, da_o, db_o, slice(rows, 2 * rows), dg, du)
    total = mlp_back_chunks(dm1, total, wgu_p, wd_p, da_p, db_p, slice(0, rows))
    sib0[...] = total[0 : rows // 2].astype(BF16)
    sib1[...] = total[rows // 2 :].astype(BF16)


def back_far(dm1, wgu, wd, wgu_p, wd_p, da_o, db_o, da_p, db_p):
    rows, width = dm1.shape
    saved = ((rows, wd.shape[0]), BF16)
    return run(
        back_far_kernel,
        6,
        12,
        (),
        (wgu, wd, wgu_p, wd_p, da_o, db_o, da_p, db_p),
        [((rows // 2, width), BF16)] * 2 + [saved, saved],
        [pltpu.VMEM((rows, width), BF16), pltpu.SemaphoreType.DMA],
        apart=(dm1,),
    )


def back_last_kernel(dm0, acc, wgu, wd, da, db, own):
    own[...] = mlp_back_chunks(dm0, acc[...], wgu, wd, da, db, slice(0, dm0.shape[0]))


def back_last(dm0, acc, wgu, wd, da, db):
    return run(back_last_kernel, 3, 10, (), (dm0, acc, wgu, wd, da, db), [(acc.shape, F32)])[0]


def first_norm_kernel(
    got_ref, got_late, dh2, own, xhat, inv, g1, sums2, a0, a1, a2, a3, w0, w1, w2, w3,
    dh1, d0, d1, d2, d3, ea, dat_scr, got, sem,
):
    gain_sum, bias_sum = 0.0, 0.0
    half = got_ref.shape[0]
    copies = copies_of(got_ref, got, sem) + copies_of(got_late, got.at[pl.ds(half, half), :], sem.at[pl.ds(half // 128, half // 128)])
    for start in range(0, dh2.shape[0], 128):
        at = slice(start, start + 128)
        copies[start // 128].wait()
        dmid = dh2[at, :] + (own[at, :] + got[at, :].astype(F32))
        normed = xhat[at, :]
        gain_sum += jnp.sum(dmid * normed, axis=0, keepdims=True)
        bias_sum += jnp.sum(dmid, axis=0, keepdims=True)
        grad = norm_back(dmid, normed, inv[at, 0:1], g1[...])
        dh1[at, :] = grad
        dat_scr[at, :] = grad.astype(BF16)
    sums = jnp.concatenate([gain_sum, bias_sum, sums2[...]], axis=0)
    high = sums.astype(BF16).astype(F32)
    both = jnp.concatenate([high, sums - high], axis=0)
    rest = jnp.concatenate([both[:, 512:], jnp.zeros((8, dh2.shape[0] - 256), F32)], axis=1)
    tail = jnp.concatenate([both[:, 0:512], rest], axis=0).astype(BF16)
    dat = dat_scr[...]
    for w, d in ((w0, d0), (w1, d1), (w2, d2), (w3, d3)):
        d[0:192, :] = mm(w[...], dat, NT).astype(BF16)
        d[192:208, :] = tail
    ea[...] = mm(jnp.concatenate([a0[...], a2[...]], axis=0), dat).astype(BF16)
    pack_rows(d1, 208, mm(jnp.concatenate([a1[...], a3[...]], axis=0), dat))


def pack_rows(dst, start, value):
    n = value.shape[0]
    rest = value[:, 512:]
    dst[start : start + n, :] = value[:, 0:512].astype(dst.dtype)
    dst[start + n : start + n + n // 2, :] = jnp.concatenate([rest[0 : n // 2], rest[n // 2 :]], axis=1).astype(dst.dtype)


def unpack_rows(src, start, n):
    rest = src[start + n : start + n + n // 2, :].astype(F32)
    rest = jnp.concatenate([rest[:, 0:256], rest[:, 256:]], axis=0)
    return jnp.concatenate([src[start : start + n, :].astype(F32), rest], axis=1)


def first_norm_back(dh2, own, got, xhat, inv, g1, sums2, a, w, awaits=()):
    rows, width = dh2.shape
    heads = a[0].shape[0]
    d = ((heads + 16, rows), BF16)
    return run(
        first_norm_kernel,
        5,
        12,
        (),
        (dh2, own, xhat, inv, g1, sums2, *a, *w),
        [((rows, width), F32), d, ((4 * heads + 16, rows), BF16), d, d, ((2 * heads, width), BF16)],
        [pltpu.VMEM((rows, width), BF16), pltpu.VMEM((rows, width), BF16), pltpu.SemaphoreType.DMA((rows // 128,))],
        awaits,
        apart=got,
    )


def far_kernel(
    fast, spots_a, spots_b, dm0, dm1, dm2, dm3, ml2, ml3, wgu, wd, hid_o,
    a_first, a_second, b_first, b_second, dg, du, dmt_a, dmt_b, hids,
):
    rows = dm0.shape[0]
    hidden = wd.shape[0]
    for p, u in enumerate((dm0, dm1, dm2, dm3)):
        cols = slice(p * rows, (p + 1) * rows)
        transpose_into(dmt_a, u[...], spots_a if fast else None, cols)
        transpose_into(dmt_b, u[...], spots_b if fast else None, cols)
    for col in range(0, hidden, BLK):
        cols, ups = slice(col, col + BLK), slice(hidden + col, hidden + col + BLK)
        hids[0 : 2 * rows, :] = hid_o[:, cols]
        for block, (x, dm) in enumerate(((ml2, dm2), (ml3, dm3))):
            at = slice(block * rows, (block + 1) * rows)
            gate, up, dhid = mm(x[...], wgu[:, cols]), mm(x[...], wgu[:, ups]), mm(dm[...], wd[cols, :], NT)
            s = sigmoid(gate)
            act = gate * s
            hids[(2 + block) * rows : (3 + block) * rows, :] = (act * up).astype(BF16)
            dg[at, cols] = (dhid * (up * (s + act * (1.0 - s)))).astype(BF16)
            du[at, cols] = (dhid * act).astype(BF16)
        for turned, first, second, start in ((dmt_a, a_first, a_second, 0), (dmt_b, b_first, b_second, hidden // 2)):
            lo, hi = max(col, start), min(col + BLK, start + hidden // 2)
            if lo < hi:
                there = slice(lo - start, hi - start)
                split_rows(mm(turned[...], hids[:, lo - col : hi - col]), first.at[:, there], second.at[:, there])


def far_rows(fast, spots, dm, ml, wgu, wd, hid, awaits=()):
    rows, width = dm[0].shape
    hidden = wd.shape[0]
    half = ((width // 2, hidden // 2), BF16)
    return run(
        functools.partial(far_kernel, fast),
        8,
        18,
        spots,
        (*dm, *ml, wgu, wd, hid),
        [half] * 4 + [((2 * rows, hidden), BF16)] * 2,
        [*[pltpu.VMEM((width, 4 * rows), BF16)] * 2, pltpu.VMEM((4 * rows, BLK), BF16)],
        awaits,
    )


def weight_kernel(
    fast, spots_a, spots_b, d0, d1, d2, d3, ml0, ml1, ml2, ml3, dg0, dg1, du0, du1, dg_f, du_f, da_first, da_second, db_first,
    db_second, a_first, a_second, b_first, b_second, total, mlt_a, mlt_b, tail_scr, sem,
):
    rows = ml0.shape[0]
    hidden = dg0.shape[1]
    copies = [
        pltpu.make_async_copy(d.at[pl.ds(3 * HD, 16), :], tail_scr.at[p], sem.at[p]) for p, d in enumerate((d0, d1, d2, d3))
    ]
    for c in copies:
        c.start()
    for p, u in enumerate((ml0, ml1, ml2, ml3)):
        cols = slice(p * rows, (p + 1) * rows)
        transpose_into(mlt_a, u[...], spots_a if fast else None, cols)
        transpose_into(mlt_b, u[...], spots_b if fast else None, cols)
    for src, dst in ((da_first, a_first), (da_second, a_second), (db_first, b_first), (db_second, b_second)):
        dst[0 : src.shape[0], hidden:] = src[...]
    wide = slice(0, hidden)
    half = a_first.shape[0]
    for turned, near, late, far, first, second in (
        (mlt_a, dg0, dg1, dg_f, a_first, a_second),
        (mlt_b, du0, du1, du_f, b_first, b_second),
    ):
        grad = mm(turned[:, 0:rows], near[...]) + mm(turned[:, rows : 2 * rows], late[...])
        grad += mm(turned[:, 2 * rows :], far[...])
        split_rows(grad, first.at[:, wide], second.at[0:half, wide])
    for c in copies:
        c.wait()
    sums = [tail_scr[p].astype(F32) for p in range(4)]
    joined = (sums[0] + sums[1]) + (sums[2] + sums[3])
    whole = jnp.concatenate([joined[0:4] + joined[4:8], (joined[8:12] + joined[12:16])[:, 0:256]], axis=1)
    high = whole.astype(BF16).astype(F32)
    low = (whole - high).astype(BF16).astype(F32)
    total[...] = high + low
    rest = jnp.zeros((8, hidden), F32)
    a_second[half : half + EXTRA, wide] = jnp.concatenate([high, low, rest], axis=0).astype(BF16)
    a_second[half : half + EXTRA, hidden:] = jnp.zeros((EXTRA, a_second.shape[1] - hidden), BF16)


def weight_grads(fast, spots, d, ml, near, far, down, awaits=()):
    rows, width = ml[0].shape
    hidden = near[0].shape[1]
    chain = ((width // 2, hidden + hidden // 2), BF16)
    return run(
        functools.partial(weight_kernel, fast),
        6,
        16,
        spots,
        (*ml, *near, *far, *down),
        [chain, ((width // 2 + EXTRA, hidden + hidden // 2), BF16), chain, chain, ((4, width), F32)],
        [
            *[pltpu.VMEM((width, 4 * rows), BF16)] * 2,
            pltpu.VMEM((4, 16, rows), BF16),
            pltpu.SemaphoreType.DMA((4,)),
        ],
        awaits,
        apart=d,
    )


def join_kernel(core, got1, got2, out, sem):
    heads = 3 * HD
    pieces = ((core, 0, 4 * heads), (got1, heads, heads), (got2, heads, heads))
    copies, at = [], 0
    for n, (src, start, count) in enumerate(pieces):
        copies.append(pltpu.make_async_copy(src.at[pl.ds(start, count), :], out.at[pl.ds(at, count), :], sem.at[n]))
        copies[-1].start()
        at += count
    for c in copies:
        c.wait()


def join(core, got1, got2):
    return run(
        join_kernel,
        1,
        4,
        (),
        (),
        [((18 * HD, core.shape[1]), BF16)],
        [pltpu.SemaphoreType.DMA((3,))],
        apart=(core, got1, got2),
    )[0]


def by_heads(w):
    heads = 3 * HD
    return jnp.concatenate([w[c * heads + h * HD : c * heads + (h + 1) * HD, :] for h in range(3) for c in range(3)], axis=0)


def near_kernel(f0, f1, f2, dh1, n0, n1, n2, w0, w2, out, far, sem):
    heads = 3 * HD
    copies = []
    for n, f in enumerate((f0, f1, f2)):
        spot = pl.ds(n * heads, heads)
        copies.append(pltpu.make_async_copy(f.at[pl.ds(0, heads), :], far.at[spot, :], sem.at[n]))
        copies[-1].start()
    near = jnp.concatenate([n0[...], n1[...], n2[...]], axis=0)
    out[...] = dh1[...] + mm(near, by_heads(w0), TN)
    for c in copies:
        c.wait()
    out[...] += mm(far[...], by_heads(w2), TN)


def input_near(dh1, near, far, w0, w2):
    return run(
        near_kernel,
        3,
        12,
        (),
        (dh1, *near, w0, w2),
        [(dh1.shape, F32)],
        [pltpu.VMEM((9 * HD, dh1.shape[0]), BF16), pltpu.SemaphoreType.DMA((3,))],
        apart=far,
    )[0]


def input_kernel(core_ref, before, w1, w3, out, core, total, sem):
    arrival = pltpu.make_async_copy(core_ref, core, sem.at[0])
    arrival.start()
    w = jnp.concatenate([by_heads(w1), by_heads(w3)], axis=0)
    arrival.wait()
    copies = []
    for half in range(before.shape[0] // BLK):
        at = slice(half * BLK, (half + 1) * BLK)
        total[at, :] = before[at, :] + mm(core[:, at], w, TN)
        spot = pl.ds(half * BLK, BLK)
        copies.append(pltpu.make_async_copy(total.at[spot, :], out.at[spot, :], sem.at[1 + half]))
        copies[-1].start()
    for c in copies:
        c.wait()


def input_back(before, core, w1, w3):
    return run(
        input_kernel,
        3,
        14,
        (),
        (before, w1, w3),
        [(before.shape, F32)],
        [
            pltpu.VMEM(core.shape, BF16),
            pltpu.VMEM(before.shape, F32),
            pltpu.SemaphoreType.DMA((1 + before.shape[0] // BLK,)),
        ],
        apart=(core,),
        hbm=(0,),
    )[0]


def split_halves(v):
    return v[0 : v.shape[0] // 2], v[v.shape[0] // 2 :]


def swap(v, bit, axis="tensor"):
    n = lax.axis_size(axis)
    return lax.ppermute(v, axis, [(i, i ^ bit) for i in range(n)])


def bits_of(n):
    return n.bit_length() - 1


def spots_of(order, n):
    block = jnp.arange(n, dtype=jnp.int32) ^ lax.axis_index("dp")
    spot = jnp.zeros((n,), jnp.int32)
    for s, bit in enumerate(order):
        spot = spot + (((block >> bit) & 1) << (len(order) - 1 - s))
    return spot


def last_kernel(chains, kind, *refs):
    count = sum(chains)
    parts, outs, scrs, sem = refs[:count], refs[count:-count - 1], refs[-count - 1 : -1], refs[-1]
    copies = []
    for n, (part, scr) in enumerate(zip(parts, scrs)):
        copies.append(pltpu.make_async_copy(part.at[pl.ds(0, scr.shape[0]), :], scr, sem.at[n]))
        copies[-1].start()
    for c in copies:
        c.wait()
    sums, at = [], 0
    for length in chains:
        sums.append(sum(scr[...].astype(F32) for scr in scrs[at : at + length]))
        at += length
    if kind == "mlp":
        gu, down = outs
        width = down.shape[1]
        one, two = sums[0:2]
        if len(sums) > 2:
            one += sums[2][:, 0 : one.shape[1]]
            two += sums[2][:, one.shape[1] :]
        gu[:, 0, :] = one[:, 0:width]
        gu[:, 1, :] = two[:, 0:width]
        down[...] = jnp.concatenate([one[:, width:], two[:, width:]], axis=1)
    else:
        qkv, out = outs
        total = jnp.concatenate(sums[0:2], axis=1)
        if len(sums) > 2:
            total += sums[2]
        for c in range(3):
            qkv[c] = jnp.concatenate([total[:, (3 * h + c) * HD : (3 * h + c + 1) * HD] for h in range(3)], axis=1)
        out[...] = total[:, 9 * HD :].T


def last_sums(kind, rows, chains, outs):
    parts = [part for chain in chains for part in chain]
    return run(
        functools.partial(last_kernel, [len(chain) for chain in chains], kind),
        2,
        8,
        (),
        (),
        outs,
        [pltpu.VMEM((rows, part.shape[1]), BF16) for part in parts] + [pltpu.SemaphoreType.DMA((len(parts),))],
        apart=parts,
    )


def in_two(v):
    high = lax.reduce_precision(v, 8, 7)
    low = lax.reduce_precision(v - high, 8, 7)
    return jnp.concatenate([high, low], axis=0), high + low


class scatter_steps:
    def __init__(self, first, second, order, ride=None):
        self.parts, self.order, self.step = [first], order, 0
        self.sent, self.ride, self.base = second, ride, None
        self.extra = 0 if ride is None else EXTRA

    def advance(self):
        self.base = self.ride
        self.parts.append(swap(self.sent, 1 << self.order[self.step], "dp"))
        self.step += 1
        self.next_sent()
        return self.parts[-1]

    def carried(self, got):
        n, width = self.base.shape
        rows = got[got.shape[0] - EXTRA : got.shape[0] - EXTRA + 2 * n, 0:width].astype(F32)
        return self.base + (rows[0:n] + rows[n:])

    def next_sent(self):
        if self.extra:
            self.ride = self.carried(self.parts[-1])
        if self.step < len(self.order):
            length = self.parts[-1].shape[0] - self.extra
            sent = sum(u[length // 2 : length].astype(F32) for u in self.parts)
            if self.extra:
                rows, self.ride = in_two(self.ride)
                padding = ((0, EXTRA - rows.shape[0]), (0, sent.shape[1] - rows.shape[1]))
                sent = jnp.concatenate([sent, jnp.pad(rows, padding)], axis=0)
            self.sent = sent.astype(BF16)

    def all_parts(self):
        while self.step < len(self.order):
            self.advance()
        return self.parts


def advance_together(chains):
    bits = {chain.order[chain.step] for chain in chains}
    if len(bits) > 1 or any(chain.step < len(chain.order) - 1 for chain in chains):
        return None
    tall = max(chain.sent.shape[0] for chain in chains)
    sent = [jnp.pad(chain.sent, ((0, tall - chain.sent.shape[0]), (0, 0))) for chain in chains]
    got = swap(jnp.concatenate(sent, axis=1), 1 << bits.pop(), "dp")
    for chain in chains:
        chain.step += 1
        chain.base = chain.ride
    return got


def first_sums(chains, rows):
    return [sum(part[0:rows].astype(F32) for part in chain) for chain in chains]


def quarter_of(w):
    rows = w.shape[0] // 4
    return lax.dynamic_slice_in_dim(w, (lax.axis_index("dp") % 4) * rows, rows, axis=0)


def local(
    tokens,
    doc_lengths,
    key_mask,
    qkv_weight,
    out_weight,
    gate_up_weight,
    down_weight,
    norm1_gain,
    norm1_bias,
    norm2_gain,
    norm2_bias,
    out_grad,
):
    rows, width = tokens.shape
    flags = jnp.pad(key_mask.astype(BF16).reshape(1, rows), ((0, EXTRA - 1), (0, width - rows)))
    tok0 = jnp.concatenate([tokens, flags], axis=0)
    tok1 = swap(tok0, 1)
    tok2 = swap(tok0, 2)
    sp = jnp.concatenate([doc_lengths[0], lax.axis_index("tensor").reshape(1)]).astype(jnp.int32)
    quarter = (lax.axis_index("dp") % 4).reshape(1).astype(jnp.int32)
    freqs = 1000.0 ** (-(jnp.arange(HD // 2, dtype=F32) * 2.0 / HD))
    freqs = jnp.broadcast_to(freqs[:, None], (HD // 2, 128))
    wt = jnp.transpose(qkv_weight, (1, 2, 0)).reshape(-1, width)

    n_dp = lax.axis_size("dp")
    fast = (width // n_dp) % 16 == 0
    order = list(range(bits_of(n_dp)))
    order_b = order[1:2] + order[0:1] + order[2:]
    spots, spots_b = (spots_of(u, n_dp) for u in (order, order_b))

    def arranged(v, at):
        if fast:
            return v
        blocks = v.reshape(v.shape[0], n_dp, width // n_dp)
        return jnp.take(blocks, jnp.argsort(at), axis=1).reshape(v.shape)

    ORDER.last = ()
    wo0 = out_weight
    wo1, wt1 = swap(wo0, 1), swap(wt, 1)
    wgu = gate_up_weight.reshape(width, -1)
    part_b = quarter_of(wgu)
    part_a = jnp.concatenate([quarter_of(down_weight), wo0], axis=0)

    proj = [project(0, sp, freqs, tok0, wt), project(1, sp, freqs, tok1, wt, awaits=(part_a, part_b))]
    tok2, part_b = gate(tok2, part_b)
    tok3, pb0 = swap(tok2, 1), swap(part_b, 2)
    tok = (tok0, tok1, tok2, tok3)
    proj.append(project(2, sp, freqs, tok2, wt))
    *more, part_a = project(3, sp, freqs, tok3, wt, carry=(part_a,))
    proj.append(more)
    pa0 = swap(part_a, 2)
    qt, kt, k, vt, cs = zip(*proj)
    o2, o3, q2, q3 = attend(1, sp, qt, k, vt, (wo1, wt1))
    o2, pb0 = gate(o2, pb0)
    pb1, pb2, g2 = swap(pb0, 1, "dp"), swap(pb0, 2, "dp"), swap(o2, 2)
    o0, o1, q0, q1 = attend(0, sp, qt, k, vt)
    (o3,) = gate(o3, awaits=(pa0,))
    g3 = swap(o3, 3)
    (tok_t,) = transposed(fast, (spots,), tok, rows)
    if not fast:
        tok_t = arranged(tok_t.T, spots).T
    (o1,) = gate(o1)
    g1 = swap(o1, 1)
    to_y, to_z, pa0, wo2 = pack_parts(pb1, pb2, pa0)
    (wo2,) = gate(wo2)
    wo3 = swap(wo2, 1)
    kept = park((*kt, *k, *vt, q0, q1, q2, q3, tok_t))
    kt, k, vt, (q0, q1, q2, q3, tok_t) = kept[0:4], kept[4:8], kept[8:12], kept[12:17]
    from_y, from_z, pa3 = swap(to_y, 1, "dp"), swap(to_z, 2, "dp"), swap(pa0, 3, "dp")
    wo = (wo0, wo1, wo2, wo3)

    gain1, bias1, gain2, bias2 = (u.reshape(1, width) for u in (norm1_gain, norm1_bias, norm2_gain, norm2_bias))
    ml0, xhat1, inv1, *halves = out_project((o0, g1, g2, g3), wo, tokens, gain1, bias1)
    acc, da_o, db_o, hid_o, ml1 = mlp_own(ml0, [swap(u, 1) for u in halves], wgu, down_weight)
    (ml0,) = gate(ml0)
    ml2 = swap(ml0, 2)
    gate(awaits=(from_y, from_z, pa3))
    parts = (pb0, pb1, pb2, from_y, from_z, pa0, pa3)
    sib0, sib1, da_1, db_1, wgu_p, wd_p = mlp_far(quarter, ml1, acc, parts)
    own, da_0, db_0 = mlp_last(ml0, acc, wgu_p, wd_p)
    output, dh2, dm0, sums2 = mid_norm(
        xhat1, own, (swap(sib0, 1), swap(sib1, 1)), out_grad, gain1, bias1, gain2, bias2
    )
    dm0, ml2 = gate(dm0, ml2)
    dm1, dm2 = swap(dm0, 1), swap(dm0, 2)
    ml3 = swap(ml2, 1)
    acc, dg_0, du_0 = back_own(dm0, wgu, down_weight, da_o, db_o)
    sib0, sib1, dg_1, du_1 = back_far(dm1, wgu, down_weight, wgu_p, wd_p, da_o, db_o, da_1, db_1)
    own = back_last(dm0, acc, wgu_p, wd_p, da_0, db_0)
    dh1, d0, d1, d2, d3, ea = first_norm_back(
        dh2, own, (swap(sib0, 1), swap(sib1, 1)), xhat1, inv1, gain1, sums2, (o0, g1, g2, g3), wo, (ml3,)
    )
    d1, d2, d3, dm2 = gate(d1, d2, d3, dm2)
    dm3 = swap(dm2, 1)
    d = (d0, swap(d1, 1), swap(d2, 2), swap(d3, 3))
    ml, dm, both = (ml0, ml1, ml2, ml3), (dm0, dm1, dm2, dm3), (spots, spots_b)
    *down, dg_f, du_f = far_rows(fast, both, dm, ml[2:], wgu, down_weight, hid_o)
    (wt,) = gate(wt, awaits=d[1:])
    wt2 = swap(wt, 2)
    a_first, a_second, b_first, b_second, sums = weight_grads(
        fast, both, d, ml, (dg_0, dg_1, du_0, du_1), (dg_f, du_f), down
    )
    if not fast:
        tail = a_second[width // 2 :]
        a_first, a_second = split_halves(arranged(jnp.concatenate([a_first, a_second[0 : width // 2]]).T, spots).T)
        a_second = jnp.concatenate([a_second, tail])
        b_first, b_second = split_halves(arranged(jnp.concatenate([b_first, b_second]).T, spots_b).T)
    a_second, b_second = gate(a_second, b_second)
    chain_a = scatter_steps(a_first, a_second, order, sums)
    chain_b = scatter_steps(b_first, b_second, order_b)
    a_got, b_got = chain_a.advance(), chain_b.advance()

    arrange = jnp.zeros((8, 128), BF16)
    if not fast:
        column = jnp.arange(width)
        target = spots[column // (width // n_dp)] * (width // n_dp) + column % (width // n_dp)
        arrange = (column[:, None] == target[None, :]).astype(BF16)
    back = functools.partial(
        attend_back,
        fast=fast,
        spots=spots,
        sp=sp,
        q=(q0, q1, q2, q3),
        kt=kt,
        k=k,
        vt=vt,
        o=(o0, o1, o2, o3),
        d=d,
        cs=cs,
        tok_t=tok_t,
    )
    near0, far0, core0, grad0, e_own = back(0, given=(ea,))
    far0, chain_a.parts[-1], chain_b.parts[-1], wt2 = gate(far0, a_got, b_got, wt2)
    for chain in (chain_a, chain_b):
        chain.next_sent()
    a_got, b_got, got0 = chain_a.advance(), chain_b.advance(), swap(far0, 2)
    near1, far1, core1, first, second = back(1, given=(core0, grad0))
    far1, second, chain_a.parts[-1], chain_b.parts[-1], wt2 = gate(far1, second, a_got, b_got, wt2)
    for chain in (chain_a, chain_b):
        chain.next_sent()
    c1 = scatter_steps(first, second, order)
    c1_got, mlp3 = c1.advance(), advance_together((chain_a, chain_b))
    wt3 = swap(wt2, 1)
    got1 = swap(far1, 2)
    near2, far2, core2, first, second = back(2, given=(core1, got0, e_own, arrange))
    far2, second, c1.parts[-1] = gate(far2, second, c1_got, awaits=(got1, wt3))
    c1.next_sent()
    c2 = scatter_steps(first, second, order)
    c2_got, got2 = c2.advance(), swap(far2, 2)
    c2.parts[-1], *late = gate(c2_got, *([] if mlp3 is None else [mlp3]))
    c2.next_sent()
    c2_got, c1_got = c2.advance(), c1.advance()
    mlp, shard = [chain_a.all_parts(), chain_b.all_parts()], width // n_dp
    if mlp3 is not None:
        mlp.append([mlp3])
    core = swap(join(core2, got1, got2), 1)
    input_grad = input_near(dh1, (near0, near1, near2), (got0, got1, got2), wt, wt2)
    c2.parts[-1], c1.parts[-1] = gate(c2_got, c1_got)
    c2.next_sent()
    c1.next_sent()
    if late:
        chain_a.ride = chain_a.carried(late[0])
        mlp[-1] = late
    both = advance_together((c1, c2))
    attention = [c1.all_parts(), c2.all_parts()]
    if both is not None:
        attention.append([both])
    input_grad = input_back(input_grad, core, wt1, wt3)
    sums = chain_a.ride
    if fast:
        hidden = down_weight.shape[0]
        gu_part, down_part = last_sums("mlp", shard, mlp, [((shard, 2, hidden), F32), ((shard, hidden), F32)])
        qkv_part, out_part = last_sums(
            "attention", shard, attention, [((3, shard, 3 * HD), F32), ((3 * HD, shard), F32)]
        )
        qkv_part = jnp.transpose(qkv_part, (1, 0, 2))
    else:
        one, two = first_sums(mlp, shard)
        gu_part = jnp.stack([one[:, 0:width], two[:, 0:width]], axis=1)
        down_part = jnp.concatenate([one[:, width:], two[:, width:]], axis=1)
        total = jnp.concatenate(first_sums(attention, shard), axis=1)
        out_part = total[:, 9 * HD :].T
        qkv_part = jnp.transpose(total[:, 0 : 9 * HD].reshape(shard, 3, 3, HD), (0, 2, 1, 3)).reshape(shard, 3, 3 * HD)
    return (
        output,
        input_grad,
        qkv_part,
        out_part,
        gu_part,
        down_part.T,
        sums[0],
        sums[1],
        sums[2],
        sums[3],
    )


def solution(mesh):
    placed = (
        P(("dp", "tensor"), None),
        P("dp", None),
        P(("dp", "tensor")),
        P(None, None, "tensor"),
        P("tensor", None),
        P(None, None, "tensor"),
        P("tensor", None),
        P(),
        P(),
        P(),
        P(),
        P(("dp", "tensor"), None),
    )
    return jax.shard_map(
        local,
        mesh=mesh,
        in_specs=placed,
        out_specs=(
            P(("dp", "tensor"), None),
            P(("dp", "tensor"), None),
            P("dp", None, "tensor"),
            P("tensor", "dp"),
            P("dp", None, "tensor"),
            P("tensor", "dp"),
            P(),
            P(),
            P(),
            P(),
        ),
        check_vma=False,
    )
```
